128 devices in a mesh: dp: 16 (over y_lo, z, core), tensor: 8 (over x, y_hi).
Axes of the slice: x: 4, y: 4 (y_hi: 2, y_lo: 2; y = y_hi * 2 + y_lo), z: 4, core: 2. Of those that a mesh axis runs over, the one named last changes fastest.
Arguments:
- tokens: bfloat16 [2, 2048, 2048], P(None, 'dp'), may hold values from -6 to 6
- cotangent: bfloat16 [2, 2048, 2048], P(None, 'dp'), may hold values from -6 to 6
- pack_perm: int32 [2, 2048], replicated, may hold values from 0 to 2047, as said below
- lengths: int32 [2, 2], replicated, may hold values from 1024 to 1024, as said below
- routes: int32 [2, 2048, 8], P(None, 'dp'), may hold values from 0 to 15, all different within a row; in each aligned block of 128 rows (0 to 127, 128 to 255, ..., all dimensions but the last counted through in order) at most 80 rows name the same one
- gates: float32 [2, 2048, 8], P(None, 'dp'), may hold values from 0.06 to 0.19
- attn_gain: bfloat16 [2048], P('dp'), may hold values from 0.5 to 1.5
- w_query: bfloat16 [2048, 2048], P('dp', 'tensor'), may hold values from -0.125 to 0.125
- w_key: bfloat16 [2048, 2048], P('dp', 'tensor'), may hold values from -0.125 to 0.125
- w_value: bfloat16 [2048, 2048], P('dp', 'tensor'), may hold values from -0.125 to 0.125
- query_gain: bfloat16 [16, 128], P('tensor', 'dp'), may hold values from 0.5 to 1.5
- key_gain: bfloat16 [16, 128], P('tensor', 'dp'), may hold values from 0.5 to 1.5
- w_out: bfloat16 [2048, 2048], P('tensor', 'dp'), may hold values from -1.5 to 1.5
- moe_gain: bfloat16 [2048], P('dp'), may hold values from 0.5 to 1.5
- w_gate: bfloat16 [16, 2048, 1024], P(None, 'dp', 'tensor'), may hold values from -0.125 to 0.125
- w_up: bfloat16 [16, 2048, 1024], P(None, 'dp', 'tensor'), may hold values from -0.125 to 0.125
- w_down: bfloat16 [16, 1024, 2048], P(None, 'tensor', 'dp'), may hold values from -0.75 to 0.75
Outputs:
- output: bfloat16 [2, 2048, 2048], P(None, 'dp')
- input_grad: bfloat16 [2, 2048, 2048], P(None, 'dp')
- attn_gain_grad: float32 [2048], P('dp')
- query_grad: float32 [2048, 2048], P('dp', 'tensor')
- key_grad: float32 [2048, 2048], P('dp', 'tensor')
- value_grad: float32 [2048, 2048], P('dp', 'tensor')
- query_gain_grad: float32 [16, 128], P('tensor', 'dp')
- key_gain_grad: float32 [16, 128], P('tensor', 'dp')
- out_grad: float32 [2048, 2048], P('tensor', 'dp')
- moe_gain_grad: float32 [2048], P('dp')
- gate_grad: float32 [16, 2048, 1024], P(None, 'dp', 'tensor')
- up_grad: float32 [16, 2048, 1024], P(None, 'dp', 'tensor')
- down_grad: float32 [16, 1024, 2048], P(None, 'tensor', 'dp')
The draws below stay inside these ranges and needn't reach their ends.
Inputs may be any that keep to these rules, and one draw needn't show every extreme that they name: `pack_perm`: each row is a permutation of the rows of its micro-batch. Every aligned block of 128 packed positions holds exactly 128 // 16 tokens from every aligned block of 128 given rows. `lengths`: each row sums to 2048. `routes`: in each aligned block of 128 rows (one index of dp in one micro-batch) an expert is named by at most 80 rows, a bound that some block reaches.
All inputs are finite; a program needn't handle non-finite values.
Results may differ from the reference program's by a relative error of at most 0.035.
Values may be sent and summed in bfloat16 or wider, within the bound.
No kernel may reach another device: no remote copies, remote signals or barrier semaphores. Data moves between devices by JAX's collectives and lax.ppermute only.
A program may use at most 256 MiB of HBM per device.

```python
import math
import jax
import jax.numpy as jnp
import numpy as np
from jax import lax

D = 2048
HEADS = 16
HEAD = 128
FF = 1024
TOPK = 8
EXPERTS = 16
MICRO = 2
MIN_LEN = 1024
TOK_DEV = 128
TOKENS_MB = 2048
CAP = 80


def shuffle_block(key):
    return jax.random.permutation(key, TOK_DEV)


def deal_once(key):
    blocks = TOKENS_MB // TOK_DEV
    per_pair = TOK_DEV // blocks
    first_key, second_key = jax.random.split(key)
    picks = jax.vmap(shuffle_block)(jax.random.split(first_key, blocks))
    source = (picks // per_pair).reshape(-1)
    hot_table = (source[:, None] == jnp.arange(blocks, dtype=jnp.int32)[None, :]).astype(jnp.int32)
    slot_rank = jnp.sum((jnp.cumsum(hot_table, axis=0) - hot_table) * hot_table, axis=1)
    places = jax.vmap(shuffle_block)(jax.random.split(second_key, blocks))
    return (source * TOK_DEV + places[source, slot_rank]).astype(jnp.int32)


def draw_pack_perm(key, part):
    key = jax.random.fold_in(key, 11)
    return jax.vmap(deal_once)(jax.random.split(key, MICRO)).astype(jnp.int32)


def draw_lengths(key, part):
    key = jax.random.fold_in(key, 23)
    leading = jax.random.randint(key, (MICRO,), MIN_LEN, TOKENS_MB - MIN_LEN + 1)
    trailing = TOKENS_MB - leading
    return jnp.stack([leading, trailing], axis=1).astype(jnp.int32)


def steps_of(stream_key, dims, cuts, smallest, high):
    level = 1.0
    for dim, parts in cuts:
        heights = jax.random.uniform(jax.random.fold_in(jax.random.fold_in(stream_key, 6), dim), (parts,), jnp.float32, smallest / len(cuts), high / len(cuts))
        level = level * jnp.repeat(jnp.exp(heights), dims[dim] // parts).reshape((-1,) + (1,) * (len(dims) - 1 - dim))
    return level


def shared_out(key, own, number, rows, number_of, top, most, lean):
    ranking = jax.random.permutation(key, number_of)
    packed, common = shares(number_of, rows * top, most, lean, True), shares(number_of, rows * top, most, lean, False)
    places = jnp.arange(number_of)

    def named(sizes, turn):
        used = int((sizes > 0).sum())
        fixed = max(1, used // 4)
        shifted = fixed + (places - fixed + turn * (used - fixed)) % max(1, number_of - fixed)
        return jnp.zeros((number_of,), jnp.int32).at[ranking[jnp.where(places < fixed, places, shifted)]].set(jnp.asarray(sizes, jnp.int32))

    sizes = jnp.where(number % 4 == 0, named(packed, number // 4), named(common, number - number // 4 - 1))
    mixed = jax.random.permutation(jax.random.fold_in(own, 3), number_of)
    donor, receiver = mixed[0:number_of // 2 * 2:2], mixed[1:number_of // 2 * 2:2]
    margin = jnp.minimum(sizes[donor] - 1, most - sizes[receiver]) // 2
    margin = jnp.where((donor == ranking[0]) | (receiver == ranking[0]) | (sizes[receiver] == 0), 0, jnp.maximum(margin, 0))
    shifted = jax.random.randint(jax.random.fold_in(own, 4), (number_of // 2,), 0, 1 << 20) % (margin + 1)
    sizes = sizes.at[donor].add(-shifted).at[receiver].add(shifted)
    items = jnp.searchsorted(jnp.cumsum(sizes), jnp.arange(rows * top), side="right").astype(jnp.int32)
    listing = items.reshape(top, rows).T
    listing = listing[jax.random.permutation(jax.random.fold_in(own, 1), rows)]
    turn = jax.random.randint(jax.random.fold_in(own, 2), (rows, 1), 0, top)
    return jnp.take_along_axis(listing, (jnp.arange(top)[None, :] + turn) % top, axis=1)


def shares(number_of, total, most, slope, full):
    weights = [(1 << 20) // math.isqrt(grade ** slope) + 1 for grade in range(1, number_of + 1)]
    largest = most if full else min(most, max(-(-total // number_of), total * weights[0] // sum(weights)))
    least = 1 if total - largest >= number_of - 1 else 0
    given, rest = [largest] + [least] * (number_of - 1), total - largest - least * (number_of - 1)
    while rest > 0:
        free = [i for i in range(1, number_of) if given[i] < largest] or [i for i in range(1, number_of) if given[i] < most]
        pool, left = sum([weights[i] for i in free]), rest
        for i in free:
            addition = min(most - given[i], max(1, left * weights[i] // pool), rest)
            given[i] = given[i] + addition
            rest = rest - addition
    return np.array(given)


def scatter_about(stream_key, dims, deviation, most, cuts=(), kind=jnp.bfloat16):
    values = jax.random.normal(stream_key, dims, jnp.float32) * deviation
    if len(cuts) > 0:
        values = steps_of(stream_key, dims, cuts, -0.22, 0.18) * values
    return jnp.clip(values, min=-most, max=most).astype(kind)


def setup_inputs(seed: int = 0) -> dict:
    arg_keys = jax.random.split(jax.random.key(seed), 18)
    tokens = scatter_about(arg_keys[0], (MICRO, TOKENS_MB, D), 1.0, 6.0, ((1, 16),))
    cotangent = scatter_about(arg_keys[1], (MICRO, TOKENS_MB, D), 1.0, 6.0, ((1, 16),))
    pack_perm = draw_pack_perm(jax.random.fold_in(arg_keys[17], 71), 0)
    lengths = draw_lengths(jax.random.fold_in(arg_keys[17], 71), 0)
    routes_keys = jax.random.split(jax.random.fold_in(arg_keys[4], 1), MICRO * TOKENS_MB // TOK_DEV)
    routes_turns = jax.random.permutation(jax.random.fold_in(arg_keys[4], 3), MICRO * TOKENS_MB // TOK_DEV)
    routes = jax.vmap(lambda own, number: shared_out(jax.random.fold_in(arg_keys[4], 2), own, number, TOK_DEV, EXPERTS, TOPK, CAP, 1))(routes_keys, routes_turns).reshape((MICRO, TOKENS_MB, TOPK))
    gates = jnp.clip(0.06 + 0.13 * jax.random.uniform(arg_keys[5], (MICRO, TOKENS_MB, TOPK), jnp.float32) ** steps_of(arg_keys[5], (MICRO, TOKENS_MB, TOPK), ((1, 16),), -0.2, 0.2), 0.06, 0.19)
    attn_gain = jnp.clip(1.0 + 0.1 * jax.random.normal(arg_keys[6], (D,), jnp.float32), 0.5, 1.5).astype(jnp.bfloat16)
    w_query = scatter_about(arg_keys[7], (D, D), D ** -0.5, 0.125, ((0, 16), (1, 8)))
    w_key = scatter_about(arg_keys[8], (D, D), D ** -0.5, 0.125, ((0, 16), (1, 8)))
    w_value = scatter_about(arg_keys[9], (D, D), D ** -0.5, 0.125, ((0, 16), (1, 8)))
    query_gain = jnp.clip(1.0 + 0.1 * jax.random.normal(arg_keys[10], (HEADS, HEAD), jnp.float32), 0.5, 1.5).astype(jnp.bfloat16)
    key_gain = jnp.clip(1.0 + 0.1 * jax.random.normal(arg_keys[11], (HEADS, HEAD), jnp.float32), 0.5, 1.5).astype(jnp.bfloat16)
    w_out = scatter_about(arg_keys[12], (D, D), (D // 128) ** -0.5, 1.5, ((0, 8), (1, 16)))
    moe_gain = jnp.clip(1.0 + 0.1 * jax.random.normal(arg_keys[13], (D,), jnp.float32), 0.5, 1.5).astype(jnp.bfloat16)
    w_gate = scatter_about(arg_keys[14], (EXPERTS, D, FF), D ** -0.5, 0.125, ((1, 16), (2, 8)))
    w_up = scatter_about(arg_keys[15], (EXPERTS, D, FF), D ** -0.5, 0.125, ((1, 16), (2, 8)))
    w_down = scatter_about(arg_keys[16], (EXPERTS, FF, D), (FF // 16) ** -0.5, 0.75, ((1, 8), (2, 16)))
    return dict(tokens=tokens, cotangent=cotangent, pack_perm=pack_perm, lengths=lengths, routes=routes, gates=gates, attn_gain=attn_gain, w_query=w_query, w_key=w_key, w_value=w_value, query_gain=query_gain, key_gain=key_gain, w_out=w_out, moe_gain=moe_gain, w_gate=w_gate, w_up=w_up, w_down=w_down)


epsilon = 1e-05
rope_base = 10000.0
highest = lax.Precision.HIGHEST

@jax.custom_vjp
def low(v):
    return lax.optimization_barrier(v.astype(jnp.bfloat16)).astype(jnp.float32)

@jax.custom_vjp
def low_back(v):
    return v

def low_keep(v):
    return (low(v), None)

def low_pass(kept, grad):
    return (grad,)

def back_keep(v):
    return (v, None)

def back_low(kept, grad):
    return (low(grad),)
low.defvjp(low_keep, low_pass)
low_back.defvjp(back_keep, back_low)

def rope_tables(position):
    half_dim = HEAD // 2
    frequency = rope_base ** (-(jnp.arange(half_dim, dtype=jnp.float32) * 2.0 / HEAD))
    angle = position[:, None] * frequency[None, :]
    cosine = jnp.concatenate([jnp.cos(angle), jnp.cos(angle)], axis=-1)
    sine = jnp.concatenate([jnp.sin(angle), jnp.sin(angle)], axis=-1)
    return (cosine[:, None, :], sine[:, None, :])

def rotate(values, cosine, sine):
    half_dim = values.shape[-1] // 2
    turned = jnp.concatenate([-values[..., half_dim:], values[..., :half_dim]], axis=-1)
    return values * cosine + turned * sine

def pack_layout(length_row, pack_total):
    seq_ends = jnp.cumsum(length_row)
    starts = seq_ends - length_row
    places = jnp.arange(pack_total, dtype=jnp.int32)
    segment = lax.optimization_barrier(jnp.sum((places[:, None] >= seq_ends[None, :-1]).astype(jnp.int32), axis=1))
    chosen = segment[:, None] == jnp.arange(length_row.shape[0], dtype=jnp.int32)[None, :]
    start_of = lax.optimization_barrier(jnp.sum(jnp.where(chosen, starts[None, :], 0), axis=1))
    return (segment, (places - start_of).astype(jnp.float32))

def norm_rows(values, gain):
    factor = lax.rsqrt(lax.optimization_barrier(jnp.mean(values * values, axis=-1, keepdims=True)) + epsilon)
    return values * factor * gain

def reference(tokens, cotangent, pack_perm, lengths, routes, gates, attn_gain, w_query, w_key, w_value, query_gain, key_gain, w_out, moe_gain, w_gate, w_up, w_down):

    def forward(float_tokens, attn_scale, query_matrix, key_matrix, value_matrix, query_scale, key_scale, out_matrix, moe_scale, gate_stack, up_stack, down_stack):
        results = []
        for micro_index in range(MICRO):
            order = pack_perm[micro_index]
            inputs = float_tokens[micro_index][order]
            segment, position = pack_layout(lengths[micro_index], TOKENS_MB)
            cosine, sine = rope_tables(position)
            places = jnp.arange(TOKENS_MB, dtype=jnp.int32)
            visible = (segment[:, None] == segment[None, :]) & (places[None, :] <= places[:, None])
            normed = low(norm_rows(inputs, attn_scale))
            query_pre = low_back(jnp.dot(normed, query_matrix, precision=highest))
            key_pre = low_back(jnp.dot(normed, key_matrix, precision=highest))
            values = low(low_back(jnp.dot(normed, value_matrix, precision=highest))).reshape(TOKENS_MB, HEADS, HEAD)
            query_norm = norm_rows(query_pre, query_scale.reshape(D))
            key_norm = norm_rows(key_pre, key_scale.reshape(D))
            queries = low(rotate(query_norm.reshape(TOKENS_MB, HEADS, HEAD), cosine, sine))
            keys = low(rotate(key_norm.reshape(TOKENS_MB, HEADS, HEAD), cosine, sine))

            def one_head(head_inputs):
                head_query, head_key, head_value = head_inputs
                scores = low_back(jnp.dot(head_query, head_key.T, precision=highest) * HEAD ** (-0.5))
                scores = jnp.where(visible, scores, -1e+30)
                peak = lax.optimization_barrier(jnp.max(scores, axis=-1, keepdims=True))
                weights = jnp.exp(scores - peak)
                probs = low(weights / lax.optimization_barrier(jnp.sum(weights, axis=-1, keepdims=True)))
                return low(low_back(jnp.dot(probs, head_value, precision=highest)))
            mixed = lax.map(jax.checkpoint(one_head), (queries.transpose(1, 0, 2), keys.transpose(1, 0, 2), values.transpose(1, 0, 2)))
            mixed = mixed.transpose(1, 0, 2).reshape(TOKENS_MB, D)
            attn_out = low_back(jnp.dot(mixed, out_matrix, precision=highest))
            hidden_one = inputs + attn_out
            moe_in = low(norm_rows(hidden_one, moe_scale))
            picks = (routes[micro_index][:, :, None] == jnp.arange(EXPERTS, dtype=jnp.int32)[None, None, :]).astype(jnp.float32)
            combine = lax.optimization_barrier(jnp.sum(picks * gates[micro_index][:, :, None].astype(jnp.float32), axis=1))

            def expert_step(running, expert_inputs):
                gate_matrix, up_matrix, down_matrix, weight = expert_inputs
                gate_h = low_back(jnp.dot(moe_in, gate_matrix, precision=highest))
                up_h = low_back(jnp.dot(moe_in, up_matrix, precision=highest))
                expert_hidden = low(gate_h * jax.nn.sigmoid(gate_h) * up_h)
                produced = low_back(jnp.dot(expert_hidden, down_matrix, precision=highest))
                return (running + weight[:, None] * produced, None)
            moe_out = lax.scan(jax.checkpoint(expert_step), jnp.zeros((TOKENS_MB, D), jnp.float32), (gate_stack, up_stack, down_stack, combine.T))[0]
            results.append((hidden_one + moe_out)[jnp.argsort(order)])
        return jnp.stack(results)
    floats = [array.astype(jnp.float32) for array in (tokens, attn_gain, w_query, w_key, w_value, query_gain, key_gain, w_out, moe_gain, w_gate, w_up, w_down)]
    result, pullback = jax.vjp(forward, *floats)
    grads = pullback(cotangent.astype(jnp.float32))
    return (result.astype(jnp.bfloat16), grads[0].astype(jnp.bfloat16), grads[1], grads[2], grads[3], grads[4], grads[5], grads[6], grads[7], grads[8], grads[9], grads[10], grads[11])
```

```python
import jax
import jax.numpy as jnp
from jax import lax
from jax.experimental import pallas as pl
from jax.experimental.pallas import tpu as pltpu
from jax.sharding import PartitionSpec as P

HEAD = 128
MIB = 1024 * 1024
bf16 = jnp.bfloat16
f32 = jnp.float32

epsilon = 1e-05
rope_base = 10000.0


def rope_tables(position):
    half_dim = HEAD // 2
    frequency = rope_base ** (-(jnp.arange(half_dim, dtype=f32) * 2.0 / HEAD))
    angle = position[:, None] * frequency[None, :]
    cosine = jnp.concatenate([jnp.cos(angle), jnp.cos(angle)], axis=-1)
    sine = jnp.concatenate([jnp.sin(angle), jnp.sin(angle)], axis=-1)
    return (cosine[:, None, :], sine[:, None, :])


def rotate(values, cosine, sine):
    half_dim = values.shape[-1] // 2
    turned = jnp.concatenate([-values[..., half_dim:], values[..., :half_dim]], axis=-1)
    return values * cosine + turned * sine


def rotate_back(gradient, cosine, sine):
    half_dim = gradient.shape[-1] // 2
    scaled = gradient * sine
    turned = jnp.concatenate([scaled[..., half_dim:], -scaled[..., :half_dim]], axis=-1)
    return gradient * cosine + turned


def norm_factor(values):
    return lax.rsqrt(jnp.mean(values * values, axis=-1, keepdims=True) + epsilon)


def norm_back(values, factor, gain, gradient):
    gained = gradient * gain
    inner_sum = jnp.sum(gained * values, axis=-1, keepdims=True)
    return factor * gained - values * (factor * factor * factor) * inner_sum / values.shape[-1]


def dot_nn(left_side, right_side):
    return jnp.dot(left_side, right_side, preferred_element_type=f32)


def dot_tn(left_side, right_side):
    return lax.dot_general(
        left_side, right_side, (((0,), (0,)), ((), ())), preferred_element_type=f32
    )


def dot_nt(left_side, right_side):
    return lax.dot_general(
        left_side, right_side, (((1,), (1,)), ((), ())), preferred_element_type=f32
    )


def exchange(value, axis):
    return lax.all_to_all(value, axis, split_axis=0, concat_axis=0, tiled=True)


def spread(value, axis):
    count = lax.axis_size(axis)
    return exchange(jnp.broadcast_to(value[None], (count,) + value.shape), axis)


BLOCK = 256

KEYS = slice(0, 128)
VALUES = slice(128, 256)
QUERIES = slice(256, 288)
Q_BLOCKS = 4


def masked_scores(query, keys, key_place, query_place, query_start):
    scores = dot_nt(query, keys) * (HEAD ** (-0.5))
    visible = (key_place <= query_place) & (key_place >= query_start)
    return jnp.where(visible, scores, -1e30)


def attention_kernel(packed, key_place, query_place, query_start, mixed, log_total):
    sources = packed.shape[0]
    keys = packed[:, KEYS, :].reshape(sources * 128, HEAD)
    values = packed[:, VALUES, :].reshape(sources * 128, HEAD)
    for part in range(sources // Q_BLOCKS):
        blocks = slice(part * Q_BLOCKS, (part + 1) * Q_BLOCKS)
        rows = slice(part * Q_BLOCKS * 32, (part + 1) * Q_BLOCKS * 32)
        query = packed[blocks, QUERIES, :].reshape(Q_BLOCKS * 32, HEAD)
        scores = masked_scores(
            query, keys, key_place[...], query_place[rows, :], query_start[rows, :]
        )
        peak = jnp.max(scores, axis=-1, keepdims=True)
        weights = jnp.exp(scores - peak)
        total = jnp.sum(weights, axis=-1, keepdims=True)
        probs = (weights / total).astype(bf16)
        mixed[blocks, :, :] = (
            dot_nn(probs, values).astype(bf16).reshape(Q_BLOCKS, 32, HEAD)
        )
        log_total[rows, :] = peak + jnp.log(total)


def attention_back_kernel(
    packed, key_place, query_place, query_start, log_total, delta_mixed, out, key_sum, value_sum
):
    sources = packed.shape[0]
    keys = packed[:, KEYS, :].reshape(sources * 128, HEAD)
    values = packed[:, VALUES, :].reshape(sources * 128, HEAD)
    scale = HEAD ** (-0.5)
    for part in range(sources // Q_BLOCKS):
        blocks = slice(part * Q_BLOCKS, (part + 1) * Q_BLOCKS)
        rows = slice(part * Q_BLOCKS * 32, (part + 1) * Q_BLOCKS * 32)
        query = packed[blocks, QUERIES, :].reshape(Q_BLOCKS * 32, HEAD)
        delta = delta_mixed[blocks, :, :].reshape(Q_BLOCKS * 32, HEAD)
        scores = masked_scores(
            query, keys, key_place[...], query_place[rows, :], query_start[rows, :]
        )
        probs = jnp.exp(scores - log_total[rows, :])
        delta_probs = dot_nt(delta, values)
        inner = jnp.sum(probs * delta_probs, axis=-1, keepdims=True)
        delta_scores = (probs * (delta_probs - inner)).astype(bf16)
        out[blocks, QUERIES, :] = (
            (dot_nn(delta_scores, keys) * scale).astype(bf16).reshape(Q_BLOCKS, 32, HEAD)
        )
        key_term = dot_tn(delta_scores, query)
        value_term = dot_tn(probs.astype(bf16), delta)
        if part == 0:
            key_sum[...] = key_term
            value_sum[...] = value_term
        else:
            key_sum[...] += key_term
            value_sum[...] += value_term
    out[:, KEYS, :] = (key_sum[...] * scale).astype(bf16).reshape(sources, 128, HEAD)
    out[:, VALUES, :] = value_sum[...].astype(bf16).reshape(sources, 128, HEAD)


def attention(packed, key_place, query_place, query_start):
    sources = packed.shape[0]
    return pl.pallas_call(
        attention_kernel,
        out_shape=(
            jax.ShapeDtypeStruct((sources, 32, HEAD), bf16),
            jax.ShapeDtypeStruct((sources * 32, 1), f32),
        ),
        compiler_params=pltpu.CompilerParams(vmem_limit_bytes=40 * MIB),
        name="attention",
    )(packed, key_place, query_place, query_start)


def attention_back(packed, key_place, query_place, query_start, log_total, delta_mixed):
    sources = packed.shape[0]
    return pl.pallas_call(
        attention_back_kernel,
        out_shape=jax.ShapeDtypeStruct(packed.shape, bf16),
        scratch_shapes=[
            pltpu.VMEM((sources * 128, HEAD), f32),
            pltpu.VMEM((sources * 128, HEAD), f32),
        ],
        compiler_params=pltpu.CompilerParams(vmem_limit_bytes=40 * MIB),
        name="attention_back",
    )(packed, key_place, query_place, query_start, log_total, delta_mixed)


def stack_attention_kernel(w_query, w_key, w_value, w_out, out):
    local = w_query.shape[1]
    out[:, :local] = w_query[...]
    out[:, local : 2 * local] = w_key[...]
    out[:, 2 * local : 3 * local] = w_value[...]
    out[:, 3 * local :] = w_out[...].T


def stack_attention(w_query, w_key, w_value, w_out):
    rows, local = w_query.shape
    return pl.pallas_call(
        stack_attention_kernel,
        out_shape=jax.ShapeDtypeStruct((rows, 4 * local), bf16),
        name="stack_attention",
    )(w_query, w_key, w_value, w_out)


def stack_experts_kernel(w_gate, w_up, w_down, out):
    for expert in range(w_gate.shape[0]):
        for index, stored in enumerate((w_gate, w_up, w_down)):
            start = (expert // 2) * 3 * BLOCK + index * BLOCK + (expert % 2) * HEAD
            value = stored[expert]
            out[:, start : start + HEAD] = value.T if stored is w_down else value


def stack_experts(w_gate, w_up, w_down):
    count, rows, hidden = w_gate.shape
    return pl.pallas_call(
        stack_experts_kernel,
        out_shape=jax.ShapeDtypeStruct((rows, 3 * count * hidden), bf16),
        compiler_params=pltpu.CompilerParams(vmem_limit_bytes=24 * MIB),
        name="stack_experts",
    )(w_gate, w_up, w_down)


def experts_kernel(
    rows, rows_t, upstream, upstream_t, gates, weights, out, delta_in, grads, out_sum, delta_sum
):
    step = pl.program_id(0)
    gate_w = weights[:, 0:BLOCK]
    up_w = weights[:, BLOCK : 2 * BLOCK]
    down_w = weights[:, 2 * BLOCK : 3 * BLOCK]
    gate_h = dot_nn(rows[...], gate_w)
    up_h = dot_nn(rows[...], up_w)
    delta_hidden = dot_nn(upstream[...], down_w)
    lane = lax.broadcasted_iota(jnp.int32, gates.shape, 1)
    shares = [
        jnp.sum(jnp.where(lane == step * (BLOCK // 128) + e, gates[...], 0.0), axis=1, keepdims=True)
        for e in range(BLOCK // 128)
    ]
    share = jnp.concatenate([jnp.broadcast_to(s, (s.shape[0], 128)) for s in shares], axis=1)
    sigmoid_gate = 1.0 / (1.0 + jnp.exp(-gate_h))
    active = gate_h * sigmoid_gate
    hidden = (active * up_h * share).astype(bf16)
    delta_hidden = delta_hidden * share
    delta_gate = (
        delta_hidden * up_h * sigmoid_gate * (1.0 + gate_h * (1.0 - sigmoid_gate))
    ).astype(bf16)
    delta_up = (delta_hidden * active).astype(bf16)
    grads[:, 0:BLOCK] = dot_nn(rows_t[...], delta_gate).astype(bf16)
    grads[:, BLOCK : 2 * BLOCK] = dot_nn(rows_t[...], delta_up).astype(bf16)
    grads[:, 2 * BLOCK : 3 * BLOCK] = dot_nn(upstream_t[...], hidden).astype(bf16)
    out_term = dot_nt(hidden, down_w)
    delta_term = dot_nt(delta_gate, gate_w) + dot_nt(delta_up, up_w)

    @pl.when(step == 0)
    def _():
        out_sum[...] = out_term
        delta_sum[...] = delta_term

    @pl.when(step > 0)
    def _():
        out_sum[...] += out_term
        delta_sum[...] += delta_term

    @pl.when(step == pl.num_programs(0) - 1)
    def _():
        out[...] = out_sum[...].astype(bf16)
        delta_in[...] = delta_sum[...].astype(bf16)


def experts(rows, rows_t, upstream, upstream_t, gates, weights):
    count, width = rows.shape
    steps = weights.shape[1] // (3 * BLOCK)

    def whole(shape):
        return pl.BlockSpec(shape, lambda c: (0, 0))

    return pl.pallas_call(
        experts_kernel,
        grid=(steps,),
        in_specs=[
            whole((count, width)),
            whole((width, count)),
            whole((count, width)),
            whole((width, count)),
            whole(gates.shape),
            pl.BlockSpec((width, 3 * BLOCK), lambda c: (0, c)),
        ],
        out_specs=[
            whole((count, width)),
            whole((count, width)),
            pl.BlockSpec((width, 3 * BLOCK), lambda c: (0, c)),
        ],
        out_shape=(
            jax.ShapeDtypeStruct((count, width), bf16),
            jax.ShapeDtypeStruct((count, width), bf16),
            jax.ShapeDtypeStruct(weights.shape, bf16),
        ),
        scratch_shapes=[pltpu.VMEM((count, width), f32), pltpu.VMEM((count, width), f32)],
        compiler_params=pltpu.CompilerParams(
            dimension_semantics=("arbitrary",), vmem_limit_bytes=56 * MIB
        ),
        name="experts",
    )(rows, rows_t, upstream, upstream_t, gates, weights)


def body(
    tokens,
    cotangent,
    pack_perm,
    lengths,
    routes,
    gates,
    attn_gain,
    w_query,
    w_key,
    w_value,
    query_gain,
    key_gain,
    w_out,
    moe_gain,
    w_gate,
    w_up,
    w_down,
):
    dp = lax.axis_size("dp")
    te = lax.axis_size("tensor")
    me = lax.axis_index("dp")
    my_te = lax.axis_index("tensor")
    micro, block, width = tokens.shape
    ranks = block // dp
    own = micro * block
    part = own // te
    local = w_query.shape[1]
    heads = local // HEAD
    head_part = HEAD // dp
    quarters = dp // (micro * heads)
    expert_count = w_gate.shape[0]

    attn_local = stack_attention(w_query, w_key, w_value, w_out)
    attn_w = lax.all_gather(attn_local, "dp", axis=0, tiled=True)
    moe_local = stack_experts(w_gate, w_up, w_down)

    blocks = pack_perm.reshape(micro, dp, block)
    root = blocks // block
    earlier = jnp.arange(block)[None, :] < jnp.arange(block)[:, None]
    rank = jnp.sum(
        ((root[:, :, :, None] == root[:, :, None, :]) & earlier).astype(jnp.int32), axis=3
    )
    from_me = (root == me)[:, :, None, :] & (
        rank[:, :, None, :] == jnp.arange(ranks, dtype=jnp.int32)[None, None, :, None]
    )
    given = jnp.sum(jnp.where(from_me, (blocks - me * block)[:, :, None, :], 0), axis=3)
    given = given + (jnp.arange(micro, dtype=jnp.int32) * block)[:, None, None]
    row_index = jnp.arange(own, dtype=jnp.int32)
    send_order = lax.dynamic_index_in_dim(given, my_te, axis=2, keepdims=False).T.reshape(part)
    home_order = given.transpose(2, 1, 0).reshape(own)
    send_hot = (send_order[:, None] == row_index[None, :]).astype(bf16)
    home_hot = (row_index[:, None] == home_order[None, :]).astype(bf16)
    slot = rank * dp + root
    slot_hot = slot[:, :, None, :] == jnp.arange(block, dtype=jnp.int32)[None, None, :, None]
    place_in = jnp.sum(
        jnp.where(slot_hot, jnp.arange(block, dtype=jnp.int32)[None, None, None, :], 0), axis=3
    )
    place_of = place_in + (jnp.arange(dp, dtype=jnp.int32) * block)[None, :, None]

    def chosen(values):
        return dot_nn(send_hot, values.reshape(own, width)).astype(bf16).reshape(dp, micro, width)

    gains = jnp.stack(
        [
            attn_gain,
            moe_gain,
            jnp.concatenate(
                [
                    query_gain.reshape(-1),
                    key_gain.reshape(-1),
                    jnp.zeros((block - 2 * heads * head_part,), bf16),
                ]
            ),
            jnp.zeros((block,), bf16),
        ]
    )
    dealt = jnp.concatenate(
        [
            jnp.concatenate([chosen(tokens), chosen(cotangent)], axis=1),
            jnp.broadcast_to(gains[None], (dp,) + gains.shape),
        ],
        axis=2,
    )
    dealt = exchange(dealt, "dp")
    part_tokens = dealt[:, :micro, :width].reshape(part, width)
    part_cotangent = dealt[:, micro:, :width].reshape(part, width)
    attn_gain_f = dealt[:, 0, width:].reshape(width).astype(f32)
    moe_gain_f = dealt[:, 1, width:].reshape(width).astype(f32)

    def head_gain(cut):
        return cut.reshape(dp, heads, head_part).transpose(1, 0, 2).reshape(local).astype(f32)

    query_scale = head_gain(dealt[:, 2, width : width + heads * head_part])
    key_scale = head_gain(
        dealt[:, 2, width + heads * head_part : width + 2 * heads * head_part]
    )
    own_tokens = spread(part_tokens, "tensor").reshape(own, width)

    moe_local = lax.optimization_barrier((moe_local, part_tokens))[0]
    moe_w = lax.all_gather(moe_local, "dp", axis=0, tiled=True)

    seq_ends = jnp.cumsum(lengths, axis=1)
    seq_starts = seq_ends - lengths

    def start_of(place, ends, starts):
        inside = (place[..., None] >= starts) & (place[..., None] < ends)
        return jnp.sum(jnp.where(inside, starts, 0), axis=-1)

    own_place = lax.dynamic_index_in_dim(place_of, me, axis=1, keepdims=False)
    own_start = start_of(own_place, seq_ends[:, None, :], seq_starts[:, None, :])
    position = (own_place - own_start).astype(f32)
    position = position.reshape(micro, ranks, dp).transpose(1, 2, 0).reshape(own)
    cosine, sine = rope_tables(position)
    pair_micro = me // (heads * quarters)
    quarter = me % quarters
    key_place = lax.dynamic_index_in_dim(place_of, pair_micro, axis=0, keepdims=False)
    query_place = lax.dynamic_slice_in_dim(
        key_place, quarter * (block // quarters), block // quarters, axis=1
    ).reshape(-1, 1)
    pair_ends = lax.dynamic_index_in_dim(seq_ends, pair_micro, axis=0)
    pair_starts = lax.dynamic_index_in_dim(seq_starts, pair_micro, axis=0)
    query_start = start_of(query_place, pair_ends[None], pair_starts[None])
    key_place = key_place.reshape(1, -1)

    hot = routes[..., None] == jnp.arange(expert_count, dtype=jnp.int32)
    dense = jnp.sum(jnp.where(hot, gates[..., None], 0.0), axis=2)
    own_slot_hot = lax.dynamic_index_in_dim(slot_hot, me, axis=1, keepdims=False)
    share = jnp.einsum(
        "msj,mje->mse", own_slot_hot.astype(f32), dense, precision=lax.Precision.HIGHEST
    )
    share = share.reshape(micro, ranks, dp, expert_count).transpose(1, 2, 0, 3)
    share = share.reshape(own, expert_count)
    share = jnp.pad(share, ((0, 0), (0, HEAD - expert_count)))

    qkv_w = attn_w[:, : 3 * local]
    out_w = attn_w[:, 3 * local : 4 * local]
    inputs = own_tokens.astype(f32)
    attn_factor = norm_factor(inputs)
    normed_b = (inputs * attn_factor * attn_gain_f).astype(bf16)
    qkv = dot_nn(normed_b, qkv_w)
    query_pre = qkv[:, :local]
    key_pre = qkv[:, local : 2 * local]
    value_b = qkv[:, 2 * local :].astype(bf16)
    squares = jnp.stack(
        [jnp.sum(query_pre * query_pre, axis=1), jnp.sum(key_pre * key_pre, axis=1)]
    )
    squares = jnp.sum(spread(squares, "tensor"), axis=0)
    factors = lax.rsqrt(squares / width + epsilon)
    query_factor = factors[0][:, None]
    key_factor = factors[1][:, None]
    query_b = rotate(
        (query_pre * query_factor * query_scale).reshape(own, heads, HEAD), cosine, sine
    ).astype(bf16)
    key_b = rotate(
        (key_pre * key_factor * key_scale).reshape(own, heads, HEAD), cosine, sine
    ).astype(bf16)

    def to_pairs(values):
        cut = values.reshape(ranks, dp, micro, heads, HEAD)
        return cut.transpose(2, 3, 0, 1, 4).reshape(micro, heads, block, HEAD)

    def to_quarters(values):
        return to_pairs(values).reshape(micro, heads, quarters, block // quarters, HEAD)

    def from_pairs(values):
        cut = values.reshape(micro, heads, ranks, dp, HEAD)
        return cut.transpose(2, 3, 0, 1, 4).reshape(own, local)

    copies = (micro, heads, quarters, block, HEAD)
    sent = jnp.concatenate(
        [
            jnp.broadcast_to(to_pairs(key_b)[:, :, None], copies),
            jnp.broadcast_to(to_pairs(value_b.reshape(own, heads, HEAD))[:, :, None], copies),
            to_quarters(query_b),
        ],
        axis=3,
    )
    packed = exchange(sent.reshape(dp, 2 * block + block // quarters, HEAD), "dp")
    pair_mixed, log_total = attention(packed, key_place, query_place, query_start)
    mixed_b = from_pairs(exchange(pair_mixed, "dp"))

    def shared_sum(value):
        got = exchange(value.astype(bf16).reshape(te, part, width), "tensor")
        return jnp.sum(got.astype(f32), axis=0)

    part_inputs = part_tokens.astype(f32)
    part_upstream = part_cotangent.astype(f32)
    hidden_one = part_inputs + shared_sum(dot_nt(mixed_b, out_w))

    moe_factor = norm_factor(hidden_one)
    moe_in = spread((hidden_one * moe_factor * moe_gain_f).astype(bf16), "tensor")
    moe_in = moe_in.reshape(own, width)
    own_cotangent = spread(part_cotangent, "tensor").reshape(own, width)
    moe_part, moe_grad_part, moe_grads = experts(
        moe_in, moe_in.T, own_cotangent, own_cotangent.T, share, moe_w
    )
    moe_grads = lax.psum_scatter(moe_grads, "dp", scatter_dimension=0, tiled=True)
    moe_grad = shared_sum(moe_grad_part)
    grad_moe_gain = jnp.sum(moe_grad * hidden_one * moe_factor, axis=0)
    delta_one = part_upstream + norm_back(hidden_one, moe_factor, moe_gain_f, moe_grad)
    delta_attn = spread(delta_one.astype(bf16), "tensor").reshape(own, width)
    grad_out = dot_tn(delta_attn, mixed_b)
    delta_mixed = dot_nn(delta_attn, out_w).astype(bf16)
    pair_delta = exchange(
        to_quarters(delta_mixed.reshape(own, heads, HEAD)).reshape(dp, block // quarters, HEAD),
        "dp",
    )
    pair_grads = attention_back(
        packed, key_place, query_place, query_start, log_total, pair_delta
    )
    got = exchange(pair_grads, "dp").reshape(micro, heads, quarters, -1, HEAD)
    delta_key = from_pairs(jnp.sum(got[:, :, :, KEYS].astype(f32), axis=2))
    delta_value = from_pairs(jnp.sum(got[:, :, :, VALUES].astype(f32), axis=2))
    delta_query = from_pairs(got[:, :, :, QUERIES].astype(f32))
    delta_qnorm = rotate_back(delta_query.reshape(own, heads, HEAD), cosine, sine)
    delta_qnorm = delta_qnorm.reshape(own, local)
    delta_knorm = rotate_back(delta_key.reshape(own, heads, HEAD), cosine, sine)
    delta_knorm = delta_knorm.reshape(own, local)
    grad_qgain = jnp.sum(delta_qnorm * query_pre * query_factor, axis=0)
    grad_kgain = jnp.sum(delta_knorm * key_pre * key_factor, axis=0)
    weighted_query = delta_qnorm * query_scale
    weighted_key = delta_knorm * key_scale
    inner = jnp.stack(
        [jnp.sum(weighted_query * query_pre, axis=1), jnp.sum(weighted_key * key_pre, axis=1)]
    )
    inner = jnp.sum(spread(inner, "tensor"), axis=0) / width
    delta_qpre = query_factor * weighted_query - query_pre * (
        query_factor * query_factor * query_factor
    ) * inner[0][:, None]
    delta_kpre = key_factor * weighted_key - key_pre * (
        key_factor * key_factor * key_factor
    ) * inner[1][:, None]
    delta_pre = jnp.concatenate(
        [delta_qpre.astype(bf16), delta_kpre.astype(bf16), delta_value.astype(bf16)], axis=1
    )
    attn_grad = dot_nt(delta_pre, qkv_w)
    grad_qkv = dot_tn(normed_b, delta_pre)

    def gain_cut(gradient):
        return gradient.reshape(heads, dp, head_part).transpose(1, 0, 2).reshape(dp, -1)

    below = jnp.concatenate([gain_cut(grad_qgain), gain_cut(grad_kgain)], axis=1)
    below = jnp.pad(below[:, None], ((0, 0), (0, 15), (0, 4 * local - below.shape[1])))
    attn_grads = jnp.concatenate(
        [
            jnp.concatenate([grad_qkv, grad_out], axis=1).astype(bf16).reshape(dp, block, -1),
            below.astype(bf16),
        ],
        axis=1,
    )
    grad_attn_gain = jnp.sum(attn_grad * inputs * attn_factor, axis=0)
    mine = (jnp.arange(te) == my_te)[:, None, None]

    def with_part(terms, rows):
        terms = terms.astype(f32).reshape(te, part, width)
        return (terms + jnp.where(mine, rows[None], 0.0)).astype(bf16)

    out_terms = with_part(moe_part, hidden_one)
    grad_terms = with_part(norm_back(inputs, attn_factor, attn_gain_f, attn_grad), delta_one)

    def gain_lanes(gradient):
        return gradient.reshape(dp, te, block // te).transpose(1, 0, 2)

    lanes = jnp.concatenate([gain_lanes(grad_attn_gain), gain_lanes(grad_moe_gain)], axis=2)
    lanes = jnp.pad(
        lanes.astype(bf16)[:, :, None],
        ((0, 0), (0, 0), (0, 2 * micro - 1), (0, block - lanes.shape[2])),
    )
    home = jnp.concatenate(
        [
            jnp.concatenate(
                [
                    out_terms.reshape(te, dp, micro, width),
                    grad_terms.reshape(te, dp, micro, width),
                ],
                axis=2,
            ),
            lanes,
        ],
        axis=3,
    )
    home = exchange(home.reshape(te * dp, 2 * micro, width + block), ("tensor", "dp"))
    attn_grads = lax.optimization_barrier((attn_grads, moe_grads, home))[0]
    attn_grads = lax.psum_scatter(attn_grads, "dp", scatter_dimension=0, tiled=True)[0]
    attn_grads = attn_grads.astype(f32)
    home = jnp.sum(home.reshape(te, dp, 2 * micro, width + block).astype(f32), axis=0)
    gain_sum = jnp.sum(home[:, :, width:], axis=0, keepdims=True)
    home = jnp.concatenate(
        [home[:, :, :width], jnp.broadcast_to(gain_sum, (dp,) + gain_sum.shape[1:])], axis=2
    ).astype(bf16)
    home = spread(home, "tensor")
    gain_sum = home[:, 0, 0, width:].astype(f32)
    out_rows = home[:, :, :micro, :width].reshape(own, width)
    grad_rows = home[:, :, micro:, :width].reshape(own, width)
    output = dot_nn(home_hot, out_rows).astype(bf16).reshape(micro, block, width)
    input_grad = dot_nn(home_hot, grad_rows).astype(bf16).reshape(micro, block, width)

    gain_part = block // te
    head_cut = heads * head_part
    expert_grads = moe_grads.reshape(block, expert_count // 2, 3, 2, HEAD)
    expert_grads = expert_grads.transpose(2, 1, 3, 0, 4)
    expert_grads = expert_grads.reshape(3, expert_count, block, HEAD).astype(f32)
    return (
        output,
        input_grad,
        gain_sum[:, :gain_part].reshape(block),
        attn_grads[:block, :local],
        attn_grads[:block, local : 2 * local],
        attn_grads[:block, 2 * local : 3 * local],
        attn_grads[block, :head_cut].reshape(heads, head_part),
        attn_grads[block, head_cut : 2 * head_cut].reshape(heads, head_part),
        attn_grads[:block, 3 * local :].T,
        gain_sum[:, gain_part : 2 * gain_part].reshape(block),
        expert_grads[0],
        expert_grads[1],
        expert_grads[2].transpose(0, 2, 1),
    )


def solution(mesh):
    placed = (
        P(None, "dp", None),
        P(None, "dp", None),
        P(),
        P(),
        P(None, "dp", None),
        P(None, "dp", None),
        P("dp"),
        P("dp", "tensor"),
        P("dp", "tensor"),
        P("dp", "tensor"),
        P("tensor", "dp"),
        P("tensor", "dp"),
        P("tensor", "dp"),
        P("dp"),
        P(None, "dp", "tensor"),
        P(None, "dp", "tensor"),
        P(None, "tensor", "dp"),
    )
    return jax.shard_map(
        body,
        mesh=mesh,
        in_specs=placed,
        out_specs=(
            P(None, "dp", None),
            P(None, "dp", None),
            P("dp"),
            P("dp", "tensor"),
            P("dp", "tensor"),
            P("dp", "tensor"),
            P("tensor", "dp"),
            P("tensor", "dp"),
            P("tensor", "dp"),
            P("dp"),
            P(None, "dp", "tensor"),
            P(None, "dp", "tensor"),
            P(None, "tensor", "dp"),
        ),
        check_vma=False,
    )
```

```python
import jax
import jax.numpy as jnp
from jax import lax
from jax.experimental import pallas as pl
from jax.experimental.pallas import tpu as pltpu
from jax.sharding import Mesh
from jax.sharding import PartitionSpec as P

HEAD = 128
MIB = 1024 * 1024
bf16 = jnp.bfloat16
f32 = jnp.float32

DP = ("pair", "line")
PAIR_TENSOR = ("pair", "tensor")

epsilon = 1e-05
rope_base = 10000.0


def rope_tables(position):
    half_dim = HEAD // 2
    frequency = rope_base ** (-(jnp.arange(half_dim, dtype=f32) * 2.0 / HEAD))
    angle = position[:, None] * frequency[None, :]
    cosine = jnp.concatenate([jnp.cos(angle), jnp.cos(angle)], axis=-1)
    sine = jnp.concatenate([jnp.sin(angle), jnp.sin(angle)], axis=-1)
    return (cosine[:, None, :], sine[:, None, :])


def rotate(values, cosine, sine):
    half_dim = values.shape[-1] // 2
    turned = jnp.concatenate([-values[..., half_dim:], values[..., :half_dim]], axis=-1)
    return values * cosine + turned * sine


def rotate_back(gradient, cosine, sine):
    half_dim = gradient.shape[-1] // 2
    scaled = gradient * sine
    turned = jnp.concatenate([scaled[..., half_dim:], -scaled[..., :half_dim]], axis=-1)
    return gradient * cosine + turned


def norm_factor(values):
    return lax.rsqrt(jnp.mean(values * values, axis=-1, keepdims=True) + epsilon)


def norm_back(values, factor, gain, gradient):
    gained = gradient * gain
    inner_sum = jnp.sum(gained * values, axis=-1, keepdims=True)
    return factor * gained - values * (factor * factor * factor) * inner_sum / values.shape[-1]


def dot_nn(left_side, right_side):
    return jnp.dot(left_side, right_side, preferred_element_type=f32)


def dot_tn(left_side, right_side):
    return lax.dot_general(
        left_side, right_side, (((0,), (0,)), ((), ())), preferred_element_type=f32
    )


def dot_nt(left_side, right_side):
    return lax.dot_general(
        left_side, right_side, (((1,), (1,)), ((), ())), preferred_element_type=f32
    )


def exchange(value, axis):
    return lax.all_to_all(value, axis, split_axis=0, concat_axis=0, tiled=True)


def swap(value):
    return lax.ppermute(value, "pair", [(0, 1), (1, 0)])


def in_order(first, mine, other):
    return jnp.stack([jnp.where(first, mine, other), jnp.where(first, other, mine)])


def turned(values):
    cut = values.reshape(values.shape[:-1] + (2, -1, HEAD))
    return jnp.swapaxes(cut, -3, -2).reshape(values.shape)


def spread(value, axis):
    count = lax.axis_size(axis)
    return exchange(jnp.broadcast_to(value[None], (count,) + value.shape), axis)


BLOCK = 256

RANKS = 8

KEYS = slice(0, 128)
VALUES = slice(128, 256)
QUERIES = slice(256, 288)
Q_BLOCKS = 4


def masked_scores(query, keys, key_place, query_place, query_start):
    scores = dot_nt(query, keys) * (HEAD ** (-0.5))
    visible = (key_place <= query_place) & (key_place >= query_start)
    return jnp.where(visible, scores, -1e30)


def attention_kernel(packed, key_place, query_place, query_start, mixed, log_total):
    sources = packed.shape[0]
    keys = packed[:, KEYS, :].reshape(sources * 128, HEAD)
    values = packed[:, VALUES, :].reshape(sources * 128, HEAD)
    for part in range(sources // Q_BLOCKS):
        blocks = slice(part * Q_BLOCKS, (part + 1) * Q_BLOCKS)
        rows = slice(part * Q_BLOCKS * 32, (part + 1) * Q_BLOCKS * 32)
        query = packed[blocks, QUERIES, :].reshape(Q_BLOCKS * 32, HEAD)
        scores = masked_scores(
            query, keys, key_place[...], query_place[rows, :], query_start[rows, :]
        )
        peak = jnp.max(scores, axis=-1, keepdims=True)
        weights = jnp.exp(scores - peak)
        total = jnp.sum(weights, axis=-1, keepdims=True)
        probs = (weights / total).astype(bf16)
        mixed[blocks, :, :] = (
            dot_nn(probs, values).astype(bf16).reshape(Q_BLOCKS, 32, HEAD)
        )
        log_total[rows, :] = peak + jnp.log(total)


def attention_back_kernel(
    packed, key_place, query_place, query_start, log_total, delta_mixed, out, key_sum, value_sum
):
    sources = packed.shape[0]
    keys = packed[:, KEYS, :].reshape(sources * 128, HEAD)
    values = packed[:, VALUES, :].reshape(sources * 128, HEAD)
    scale = HEAD ** (-0.5)
    for part in range(sources // Q_BLOCKS):
        blocks = slice(part * Q_BLOCKS, (part + 1) * Q_BLOCKS)
        rows = slice(part * Q_BLOCKS * 32, (part + 1) * Q_BLOCKS * 32)
        query = packed[blocks, QUERIES, :].reshape(Q_BLOCKS * 32, HEAD)
        delta = delta_mixed[blocks, :, :].reshape(Q_BLOCKS * 32, HEAD)
        scores = masked_scores(
            query, keys, key_place[...], query_place[rows, :], query_start[rows, :]
        )
        probs = jnp.exp(scores - log_total[rows, :])
        delta_probs = dot_nt(delta, values)
        inner = jnp.sum(probs * delta_probs, axis=-1, keepdims=True)
        delta_scores = (probs * (delta_probs - inner)).astype(bf16)
        out[blocks, QUERIES, :] = (
            (dot_nn(delta_scores, keys) * scale).astype(bf16).reshape(Q_BLOCKS, 32, HEAD)
        )
        key_term = dot_tn(delta_scores, query)
        value_term = dot_tn(probs.astype(bf16), delta)
        if part == 0:
            key_sum[...] = key_term
            value_sum[...] = value_term
        else:
            key_sum[...] += key_term
            value_sum[...] += value_term
    out[:, KEYS, :] = (key_sum[...] * scale).astype(bf16).reshape(sources, 128, HEAD)
    out[:, VALUES, :] = value_sum[...].astype(bf16).reshape(sources, 128, HEAD)


def attention(packed, key_place, query_place, query_start):
    sources = packed.shape[0]
    return pl.pallas_call(
        attention_kernel,
        out_shape=(
            jax.ShapeDtypeStruct((sources, 32, HEAD), bf16),
            jax.ShapeDtypeStruct((sources * 32, 1), f32),
        ),
        compiler_params=pltpu.CompilerParams(vmem_limit_bytes=40 * MIB),
        name="attention",
    )(packed, key_place, query_place, query_start)


def attention_back(packed, key_place, query_place, query_start, log_total, delta_mixed):
    sources = packed.shape[0]
    return pl.pallas_call(
        attention_back_kernel,
        out_shape=jax.ShapeDtypeStruct(packed.shape, bf16),
        scratch_shapes=[
            pltpu.VMEM((sources * 128, HEAD), f32),
            pltpu.VMEM((sources * 128, HEAD), f32),
        ],
        compiler_params=pltpu.CompilerParams(vmem_limit_bytes=40 * MIB),
        name="attention_back",
    )(packed, key_place, query_place, query_start, log_total, delta_mixed)


def stack_attention_kernel(w_query, w_key, w_value, w_out, out):
    local = w_query.shape[1]
    out[:, :local] = w_query[...]
    out[:, local : 2 * local] = w_key[...]
    out[:, 2 * local : 3 * local] = w_value[...]
    out[:, 3 * local :] = w_out[...].T


def stack_attention(w_query, w_key, w_value, w_out):
    rows, local = w_query.shape
    return pl.pallas_call(
        stack_attention_kernel,
        out_shape=jax.ShapeDtypeStruct((rows, 4 * local), bf16),
        name="stack_attention",
    )(w_query, w_key, w_value, w_out)


def stack_experts_kernel(pair, w_gate, w_up, w_down, kept, sent):
    half = w_gate.shape[0] // 2
    for out, which in ((kept, pair[0]), (sent, 1 - pair[0])):
        for expert in range(half):
            for index, stored in enumerate((w_gate, w_up, w_down)):
                start = (expert // 2) * 3 * BLOCK + index * BLOCK + (expert % 2) * HEAD
                value = stored[which * half + expert]
                out[:, start : start + HEAD] = value.T if stored is w_down else value


def stack_experts(pair, w_gate, w_up, w_down):
    count, rows, hidden = w_gate.shape
    shape = jax.ShapeDtypeStruct((rows, 3 * count * hidden // 2), bf16)
    return pl.pallas_call(
        stack_experts_kernel,
        in_specs=[pl.BlockSpec(memory_space=pltpu.SMEM)]
        + [pl.BlockSpec(memory_space=pltpu.VMEM)] * 3,
        out_shape=(shape, shape),
        compiler_params=pltpu.CompilerParams(vmem_limit_bytes=24 * MIB),
        name="stack_experts",
    )(pair.reshape(1), w_gate, w_up, w_down)


def experts_kernel(my_rank, rows, upstream, gates, weights, *refs):
    (
        out_kept,
        out_sent,
        delta_in,
        grads,
        held,
        hidden_all,
        delta_gate_all,
        delta_up_all,
        grads_out,
        out_all,
        in_sem,
        out_sem,
    ) = refs
    steps = held.shape[0]
    width = rows.shape[1]
    lines = grads.shape[0]
    lane_part = width // lines
    part = out_kept.shape[2]
    loads = [
        pltpu.make_async_copy(
            weights.at[:, pl.ds(c * 3 * BLOCK, 3 * BLOCK)], held.at[c], in_sem.at[c]
        )
        for c in range(steps)
    ]
    for load in loads:
        load.start()
    stores = []
    for c in range(steps):
        loads[c].wait()
        gate_h = dot_nn(rows[...], held[c, :, 0:BLOCK])
        up_h = dot_nn(rows[...], held[c, :, BLOCK : 2 * BLOCK])
        delta_hidden = dot_nn(upstream[...], held[c, :, 2 * BLOCK : 3 * BLOCK])
        share = jnp.concatenate(
            [
                jnp.broadcast_to(gates[:, e : e + 1], (gates.shape[0], HEAD))
                for e in range(c * BLOCK // HEAD, (c + 1) * BLOCK // HEAD)
            ],
            axis=1,
        )
        sigmoid_gate = 1.0 / (1.0 + jnp.exp(-gate_h))
        active = gate_h * sigmoid_gate
        hidden = (active * up_h * share).astype(bf16)
        delta_hidden = delta_hidden * share
        delta_gate = (
            delta_hidden * up_h * sigmoid_gate * (1.0 + gate_h * (1.0 - sigmoid_gate))
        ).astype(bf16)
        delta_up = (delta_hidden * active).astype(bf16)
        columns = slice(c * BLOCK, (c + 1) * BLOCK)
        hidden_all[:, columns] = hidden
        delta_gate_all[:, columns] = delta_gate
        delta_up_all[:, columns] = delta_up
        slot = c % 2
        if c >= 2:
            stores[c - 2].wait()
        pairs = ((delta_gate, rows), (delta_up, rows), (hidden, upstream))
        for index, (left_side, right_side) in enumerate(pairs):
            for n in range(lines):
                lanes = slice(n * lane_part, (n + 1) * lane_part)
                grads_out[slot, n, index * BLOCK : (index + 1) * BLOCK, :] = dot_tn(
                    left_side, right_side[:, lanes]
                ).astype(bf16)
        store = pltpu.make_async_copy(
            grads_out.at[slot], grads.at[:, pl.ds(c * 3 * BLOCK, 3 * BLOCK), :], out_sem.at[slot]
        )
        store.start()
        stores.append(store)
    deltas = jnp.concatenate([delta_gate_all[...], delta_up_all[...]], axis=1)
    for n in range(lines):
        lanes = slice(n * lane_part, (n + 1) * lane_part)
        gate_up = jnp.concatenate(
            [held[c, lanes, 0:BLOCK] for c in range(steps)]
            + [held[c, lanes, BLOCK : 2 * BLOCK] for c in range(steps)],
            axis=1,
        )
        delta_in[:, lanes] = dot_nt(deltas, gate_up).astype(bf16)
        down = jnp.concatenate(
            [held[c, lanes, 2 * BLOCK : 3 * BLOCK] for c in range(steps)], axis=1
        )
        produced = dot_nt(hidden_all[...], down).astype(bf16)
        out_all[:, :, lanes] = produced.reshape(2 * RANKS, part, lane_part)
    high = my_rank[0] // (RANKS // 2)
    for p in range(2):
        for q in range(RANKS // 2):
            out_kept[q, p] = out_all[p * RANKS + high * (RANKS // 2) + q]
            out_sent[q, p] = out_all[p * RANKS + (1 - high) * (RANKS // 2) + q]
    for store in stores[-2:]:
        store.wait()


def experts(my_rank, rows, upstream, gates, weights, lines):
    count, width = rows.shape
    part = count // RANKS // 2
    steps = weights.shape[1] // (3 * BLOCK)
    hidden = pltpu.VMEM((count, steps * BLOCK), bf16)
    in_vmem = pl.BlockSpec(memory_space=pltpu.VMEM)
    in_hbm = pl.BlockSpec(memory_space=pl.ANY)
    return pl.pallas_call(
        experts_kernel,
        in_specs=[pl.BlockSpec(memory_space=pltpu.SMEM), in_vmem, in_vmem, in_vmem, in_hbm],
        out_specs=[in_vmem, in_vmem, in_vmem, in_hbm],
        out_shape=(
            *[jax.ShapeDtypeStruct((RANKS // 2, 2, part, width), bf16)] * 2,
            jax.ShapeDtypeStruct((count, width), bf16),
            jax.ShapeDtypeStruct((lines, weights.shape[1], width // lines), bf16),
        ),
        scratch_shapes=[
            pltpu.VMEM((steps, width, 3 * BLOCK), bf16),
            hidden,
            hidden,
            hidden,
            pltpu.VMEM((2, lines, 3 * BLOCK, width // lines), bf16),
            pltpu.VMEM((2 * RANKS, part, width), bf16),
            pltpu.SemaphoreType.DMA((steps,)),
            pltpu.SemaphoreType.DMA((2,)),
        ],
        compiler_params=pltpu.CompilerParams(vmem_limit_bytes=56 * MIB),
        name="experts",
    )(my_rank.reshape(1), rows, upstream, gates, weights)


def summed(terms):
    total = terms[0].astype(f32)
    for k in range(1, terms.shape[0]):
        total = total + terms[k].astype(f32)
    return total


def lane_blocks(width, forward):
    lines = width // HEAD // 2
    moves = [(p * lines + n, n * 2 + p) for p in range(2) for n in range(lines)]
    return moves if forward else [(b, a) for a, b in moves]


def move_lanes(values, forward):
    moves = sorted((b, a) for a, b in lane_blocks(values.shape[-1], forward))
    return jnp.concatenate([values[:, a * HEAD : (a + 1) * HEAD] for _, a in moves], axis=1)


def before_experts_kernel(terms, tokens, gain, hidden_one, factor, moe_in):
    hidden = tokens[...].astype(f32) + summed(terms)
    scale = norm_factor(hidden)
    hidden_one[...] = hidden
    factor[...] = scale
    moe_in[...] = move_lanes((hidden * scale * gain[...]).astype(bf16), True)


def before_experts(terms, tokens, gain):
    rows, width = tokens.shape
    return pl.pallas_call(
        before_experts_kernel,
        out_shape=(
            jax.ShapeDtypeStruct((rows, width), f32),
            jax.ShapeDtypeStruct((rows, 1), f32),
            jax.ShapeDtypeStruct((rows, width), bf16),
        ),
        name="before_experts",
    )(terms, tokens, gain)


def after_experts_kernel(
    terms, hidden_one, factor, gain, upstream, delta_one, delta_attn, gain_grad
):
    gradient = move_lanes(summed(terms), False)
    hidden = hidden_one[...]
    gain_grad[...] = jnp.sum(gradient * hidden * factor[...], axis=0, keepdims=True)
    delta = move_lanes(upstream[...], False).astype(f32)
    delta = delta + norm_back(hidden, factor[...], gain[...], gradient)
    delta_one[...] = delta
    delta_attn[...] = delta.astype(bf16)


def after_experts(terms, hidden_one, factor, gain, upstream):
    rows, width = upstream.shape
    return pl.pallas_call(
        after_experts_kernel,
        out_shape=(
            jax.ShapeDtypeStruct((rows, width), f32),
            jax.ShapeDtypeStruct((rows, width), bf16),
            jax.ShapeDtypeStruct((1, width), f32),
        ),
        name="after_experts",
    )(terms, hidden_one, factor, gain, upstream)


def halve_kernel(bit, kept, got, mine, sent):
    half = mine.shape[0]
    for out, start in ((mine, bit[0] * half), (sent, (1 - bit[0]) * half)):
        for k in range(half):
            total = kept[start + k].astype(f32) + got[start + k].astype(f32)
            out[k] = total.astype(out.dtype)


def halve(bit, kept, got):
    shape = (kept.shape[0] // 2,) + kept.shape[1:]
    in_vmem = pl.BlockSpec(memory_space=pltpu.VMEM)
    return pl.pallas_call(
        halve_kernel,
        in_specs=[pl.BlockSpec(memory_space=pltpu.SMEM), in_vmem, in_vmem],
        out_shape=(jax.ShapeDtypeStruct(shape, f32), jax.ShapeDtypeStruct(shape, bf16)),
        compiler_params=pltpu.CompilerParams(vmem_limit_bytes=24 * MIB),
        name="halve",
    )(bit.reshape(1), kept, got)


def finish_kernel(
    terms, tokens, gain, delta_one, hidden_one, out_mine, out_other, moe_gain_grad, home
):
    width = tokens.shape[1]
    values = tokens[...].astype(f32)
    gradient = summed(terms)
    factor = norm_factor(values)
    gain_grad = jnp.sum(gradient * values * factor, axis=0, keepdims=True)
    moe_out = out_mine[...] + out_other[...].astype(f32)
    output = hidden_one[...] + move_lanes(moe_out, False)
    home[:, :width] = output.astype(bf16)
    home[:, width : 2 * width] = (
        delta_one[...] + norm_back(values, factor, gain[...], gradient)
    ).astype(bf16)
    rows = []
    for start in range(0, width, HEAD):
        rows.append(gain_grad[:, start : start + HEAD])
        rows.append(moe_gain_grad[:, start : start + HEAD])
    home[:, 2 * width :] = jnp.concatenate(rows, axis=0).astype(bf16)


def finish(terms, tokens, gain, delta_one, hidden_one, out_mine, out_other, moe_gain_grad):
    rows, width = tokens.shape
    return pl.pallas_call(
        finish_kernel,
        out_shape=jax.ShapeDtypeStruct((rows, 2 * width + HEAD), bf16),
        name="finish",
    )(terms, tokens, gain, delta_one, hidden_one, out_mine, out_other, moe_gain_grad)


def deliver_kernel(rows, hot, output, input_grad, gains):
    width = output.shape[1]
    output[...] = dot_nn(hot[...], rows[:, :width]).astype(bf16)
    input_grad[...] = dot_nn(hot[...], rows[:, width : 2 * width]).astype(bf16)
    terms = rows[:, 2 * width :].astype(f32)
    odd = lax.broadcasted_iota(jnp.int32, terms.shape, 0) % 2
    gains[...] = jnp.concatenate(
        [
            jnp.sum(jnp.where(odd == 0, terms, 0.0), axis=0, keepdims=True),
            jnp.sum(jnp.where(odd == 1, terms, 0.0), axis=0, keepdims=True),
        ],
        axis=0,
    )


def deliver(rows, hot):
    count, lanes = rows.shape
    width = (lanes - HEAD) // 2
    return pl.pallas_call(
        deliver_kernel,
        out_shape=(
            jax.ShapeDtypeStruct((count, width), bf16),
            jax.ShapeDtypeStruct((count, width), bf16),
            jax.ShapeDtypeStruct((2, HEAD), f32),
        ),
        compiler_params=pltpu.CompilerParams(vmem_limit_bytes=24 * MIB),
        name="deliver",
    )(rows, hot)


def body(
    tokens,
    cotangent,
    pack_perm,
    lengths,
    routes,
    gates,
    attn_gain,
    w_query,
    w_key,
    w_value,
    query_gain,
    key_gain,
    w_out,
    moe_gain,
    w_gate,
    w_up,
    w_down,
):
    pair = lax.axis_index("pair")
    first = pair == 0
    lines = lax.axis_size("line")
    dp = 2 * lines
    te = lax.axis_size("tensor")
    me = lax.axis_index(DP)
    my_te = lax.axis_index("tensor")
    micro, block, width = tokens.shape
    ranks = block // dp
    own = micro * block
    part = own // te
    local = w_query.shape[1]
    heads = local // HEAD
    head_part = HEAD // dp
    quarters = dp // (micro * heads)
    expert_count = w_gate.shape[0]

    attn_local = stack_attention(w_query, w_key, w_value, w_out)
    attn_w = lax.all_gather(attn_local, DP, axis=0, tiled=True)
    moe_kept, moe_sent = stack_experts(pair, w_gate, w_up, w_down)

    blocks = pack_perm.reshape(micro, dp, block)
    root = blocks // block
    earlier = jnp.arange(block)[None, :] < jnp.arange(block)[:, None]
    rank = jnp.sum(
        ((root[:, :, :, None] == root[:, :, None, :]) & earlier).astype(jnp.int32), axis=3
    )
    from_me = (root == me)[:, :, None, :] & (
        rank[:, :, None, :] == jnp.arange(ranks, dtype=jnp.int32)[None, None, :, None]
    )
    given = jnp.sum(jnp.where(from_me, (blocks - me * block)[:, :, None, :], 0), axis=3)
    given = given + (jnp.arange(micro, dtype=jnp.int32) * block)[:, None, None]
    row_index = jnp.arange(own, dtype=jnp.int32)
    send_order = lax.dynamic_index_in_dim(given, my_te, axis=2, keepdims=False).T.reshape(part)
    home_order = given.transpose(2, 1, 0).reshape(own)
    send_hot = (send_order[:, None] == row_index[None, :]).astype(bf16)
    home_hot = (row_index[:, None] == home_order[None, :]).astype(bf16)
    slot = rank * dp + root
    slot_hot = slot[:, :, None, :] == jnp.arange(block, dtype=jnp.int32)[None, None, :, None]
    place_in = jnp.sum(
        jnp.where(slot_hot, jnp.arange(block, dtype=jnp.int32)[None, None, None, :], 0), axis=3
    )
    place_of = place_in + (jnp.arange(dp, dtype=jnp.int32) * block)[None, :, None]

    def chosen(values):
        return dot_nn(send_hot, values.reshape(own, width)).astype(bf16)

    head_cut = heads * head_part
    head_gains = jnp.concatenate(
        [
            query_gain.reshape(1, head_cut),
            key_gain.reshape(1, head_cut),
            jnp.zeros((1, block - 2 * head_cut), bf16),
        ],
        axis=1,
    )
    gains = jnp.concatenate(
        [
            jnp.concatenate([attn_gain[None], head_gains], axis=1),
            jnp.concatenate([moe_gain[None], head_gains], axis=1),
        ],
        axis=0,
    )
    gains = jnp.broadcast_to(gains[None], (dp, micro, 2 * block)).reshape(part, 2 * block)
    sent_cotangent = turned(chosen(cotangent))
    for_partner = jnp.flip(sent_cotangent.reshape(2, part // 2, width), axis=0).reshape(part, width)
    dealt = jnp.concatenate([chosen(tokens), sent_cotangent, for_partner, gains], axis=1)
    dealt = exchange(dealt, DP)
    part_tokens = dealt[:, :width]
    part_cotangent = dealt[:, width : 2 * width]
    gains = dealt[:, 3 * width :].reshape(dp, micro, 2 * block)
    attn_gain_f = gains[:, 0, :block].reshape(1, width).astype(f32)
    moe_gain_f = gains[:, 1, :block].reshape(1, width).astype(f32)

    def head_gain(cut):
        return cut.reshape(dp, heads, head_part).transpose(1, 0, 2).reshape(local).astype(f32)

    query_scale = head_gain(gains[:, 0, block : block + head_cut])
    key_scale = head_gain(gains[:, 0, block + head_cut : block + 2 * head_cut])
    own_tokens = spread(part_tokens, "tensor").reshape(own, width)

    pair_cotangent = in_order(first, part_cotangent, dealt[:, 2 * width : 3 * width])
    pair_cotangent = pair_cotangent.reshape(2 * part, width)
    pair_cotangent = lax.all_gather(pair_cotangent, "tensor", axis=0, tiled=True)
    pair_cotangent = pair_cotangent.reshape(te, 2, part, width).transpose(1, 0, 2, 3)
    pair_cotangent = pair_cotangent.reshape(2 * own, width)

    seq_ends = jnp.cumsum(lengths, axis=1)
    seq_starts = seq_ends - lengths

    def start_of(place, ends, starts):
        inside = (place[..., None] >= starts) & (place[..., None] < ends)
        return jnp.sum(jnp.where(inside, starts, 0), axis=-1)

    own_place = lax.dynamic_index_in_dim(place_of, me, axis=1, keepdims=False)
    own_start = start_of(own_place, seq_ends[:, None, :], seq_starts[:, None, :])
    position = (own_place - own_start).astype(f32)
    position = position.reshape(micro, ranks, dp).transpose(1, 2, 0).reshape(own)
    cosine, sine = rope_tables(position)
    pair_micro = me // (heads * quarters)
    quarter = me % quarters
    key_place = lax.dynamic_index_in_dim(place_of, pair_micro, axis=0, keepdims=False)
    query_place = lax.dynamic_slice_in_dim(
        key_place, quarter * (block // quarters), block // quarters, axis=1
    ).reshape(-1, 1)
    pair_ends = lax.dynamic_index_in_dim(seq_ends, pair_micro, axis=0)
    pair_starts = lax.dynamic_index_in_dim(seq_starts, pair_micro, axis=0)
    query_start = start_of(query_place, pair_ends[None], pair_starts[None])
    key_place = key_place.reshape(1, -1)

    hot = routes[..., None] == jnp.arange(expert_count, dtype=jnp.int32)
    dense = jnp.sum(jnp.where(hot, gates[..., None], 0.0), axis=2)
    own_slot_hot = lax.dynamic_index_in_dim(slot_hot, me, axis=1, keepdims=False)
    share = jnp.einsum(
        "msj,mje->mse", own_slot_hot.astype(f32), dense, precision=lax.Precision.HIGHEST
    )
    share = share.reshape(micro, ranks, dp, expert_count).transpose(1, 2, 0, 3)
    share = share.reshape(own, expert_count)
    share = in_order(first, share, swap(share)).reshape(2 * own, expert_count)
    share = lax.dynamic_slice_in_dim(share, pair * (expert_count // 2), expert_count // 2, axis=1)

    qkv_w = attn_w[:, : 3 * local]
    out_w = attn_w[:, 3 * local : 4 * local]
    inputs = own_tokens.astype(f32)
    attn_factor = norm_factor(inputs)
    normed_b = (inputs * attn_factor * attn_gain_f).astype(bf16)
    qkv = dot_nn(normed_b, qkv_w)
    moe_sent = lax.optimization_barrier((moe_sent, qkv))[0]
    moe_local = in_order(first, moe_kept, swap(moe_sent)).reshape(2 * block, -1)
    query_pre = qkv[:, :local]
    key_pre = qkv[:, local : 2 * local]
    value_b = qkv[:, 2 * local :].astype(bf16)
    squares = jnp.stack(
        [jnp.sum(query_pre * query_pre, axis=1), jnp.sum(key_pre * key_pre, axis=1)]
    )
    squares = jnp.sum(spread(squares, "tensor"), axis=0)
    factors = lax.rsqrt(squares / width + epsilon)
    query_factor = factors[0][:, None]
    key_factor = factors[1][:, None]
    query_b = rotate(
        (query_pre * query_factor * query_scale).reshape(own, heads, HEAD), cosine, sine
    ).astype(bf16)
    key_b = rotate(
        (key_pre * key_factor * key_scale).reshape(own, heads, HEAD), cosine, sine
    ).astype(bf16)

    def to_pairs(values):
        cut = values.reshape(ranks, dp, micro, heads, HEAD)
        return cut.transpose(2, 3, 0, 1, 4).reshape(micro, heads, block, HEAD)

    def to_quarters(values):
        return to_pairs(values).reshape(micro, heads, quarters, block // quarters, HEAD)

    def from_pairs(values):
        cut = values.reshape(micro, heads, ranks, dp, HEAD)
        return cut.transpose(2, 3, 0, 1, 4).reshape(own, local)

    copies = (micro, heads, quarters, block, HEAD)
    sent = jnp.concatenate(
        [
            jnp.broadcast_to(to_pairs(key_b)[:, :, None], copies),
            jnp.broadcast_to(to_pairs(value_b.reshape(own, heads, HEAD))[:, :, None], copies),
            to_quarters(query_b),
        ],
        axis=3,
    )
    packed = exchange(sent.reshape(dp, 2 * block + block // quarters, HEAD), DP)
    moe_local, share, _ = lax.optimization_barrier((moe_local, share, packed))
    moe_w = lax.all_gather(moe_local, "line", axis=0, tiled=True)
    pair_mixed, log_total = attention(packed, key_place, query_place, query_start)
    mixed_b = from_pairs(exchange(pair_mixed, DP))

    def terms_of(value):
        return exchange(value.astype(bf16).reshape(te, part, width), "tensor")

    hidden_one, moe_factor, moe_in = before_experts(
        terms_of(dot_nt(mixed_b, out_w)), part_tokens, moe_gain_f
    )

    moe_in = spread(moe_in, PAIR_TENSOR).reshape(2 * own, width)
    out_kept, out_sent, moe_grad_part, moe_grads = experts(
        my_te, moe_in, pair_cotangent, share, moe_w, lines
    )
    moe_grads = lax.psum_scatter(moe_grads, "line", scatter_dimension=0, tiled=False)
    moe_grad_terms = exchange(moe_grad_part.reshape(2 * te, part, width), PAIR_TENSOR)
    delta_one, delta_attn, grad_moe_gain = after_experts(
        moe_grad_terms, hidden_one, moe_factor, moe_gain_f, part_cotangent
    )
    delta_attn = spread(delta_attn, "tensor").reshape(own, width)
    def across(value, partner):
        return lax.ppermute(value, "tensor", [(k, partner(k)) for k in range(te)])

    out_sent = lax.optimization_barrier((out_sent, delta_attn))[0]
    out_got = across(out_sent, lambda k: 2 * (3 - k // 2) + k % 2)
    out_kept, out_sent = halve(my_te // 2 % 2, out_kept, out_got)

    grad_out = dot_tn(delta_attn, mixed_b)
    delta_mixed = dot_nn(delta_attn, out_w).astype(bf16)
    pair_delta = exchange(
        to_quarters(delta_mixed.reshape(own, heads, HEAD)).reshape(dp, block // quarters, HEAD),
        DP,
    )
    pair_delta, moe_grads = lax.optimization_barrier((pair_delta, moe_grads))
    pair_grads = attention_back(
        packed, key_place, query_place, query_start, log_total, pair_delta
    )
    got, out_sent = lax.optimization_barrier((exchange(pair_grads, DP), out_sent))
    out_got = across(out_sent, lambda k: k ^ 2)
    out_kept, out_sent = halve(my_te % 2, out_kept, out_got)
    got = got.reshape(micro, heads, quarters, -1, HEAD)
    delta_key = from_pairs(jnp.sum(got[:, :, :, KEYS].astype(f32), axis=2))
    delta_value = from_pairs(jnp.sum(got[:, :, :, VALUES].astype(f32), axis=2))
    delta_query = from_pairs(got[:, :, :, QUERIES].astype(f32))
    delta_qnorm = rotate_back(delta_query.reshape(own, heads, HEAD), cosine, sine)
    delta_qnorm = delta_qnorm.reshape(own, local)
    delta_knorm = rotate_back(delta_key.reshape(own, heads, HEAD), cosine, sine)
    delta_knorm = delta_knorm.reshape(own, local)
    grad_qgain = jnp.sum(delta_qnorm * query_pre * query_factor, axis=0)
    grad_kgain = jnp.sum(delta_knorm * key_pre * key_factor, axis=0)
    weighted_query = delta_qnorm * query_scale
    weighted_key = delta_knorm * key_scale
    inner = jnp.stack(
        [jnp.sum(weighted_query * query_pre, axis=1), jnp.sum(weighted_key * key_pre, axis=1)]
    )
    inner = jnp.sum(spread(inner, "tensor"), axis=0) / width
    delta_qpre = query_factor * weighted_query - query_pre * (
        query_factor * query_factor * query_factor
    ) * inner[0][:, None]
    delta_kpre = key_factor * weighted_key - key_pre * (
        key_factor * key_factor * key_factor
    ) * inner[1][:, None]
    delta_pre = jnp.concatenate(
        [delta_qpre.astype(bf16), delta_kpre.astype(bf16), delta_value.astype(bf16)], axis=1
    )
    delta_pre, out_sent = lax.optimization_barrier((delta_pre, out_sent))
    out_got = across(out_sent, lambda k: k ^ 1)
    out_mine, out_other = halve(pair, out_kept[0], out_got[0])
    out_mine, out_other = out_mine[0], swap(out_other[0])
    attn_grad = dot_nt(delta_pre, qkv_w).astype(bf16)
    attn_grad_terms = terms_of(attn_grad)
    grad_qkv = dot_tn(normed_b, lax.optimization_barrier((delta_pre, attn_grad))[0])

    def gain_cut(gradient):
        return gradient.reshape(heads, dp, head_part).transpose(1, 0, 2).reshape(dp, -1)

    below = jnp.concatenate([gain_cut(grad_qgain), gain_cut(grad_kgain)], axis=1)
    below = jnp.pad(below[:, None], ((0, 0), (0, 15), (0, 4 * local - below.shape[1])))
    attn_grads = jnp.concatenate(
        [
            jnp.concatenate([grad_qkv, grad_out], axis=1).astype(bf16).reshape(dp, block, -1),
            below.astype(bf16),
        ],
        axis=1,
    )
    chunk = attn_grads.shape[1]
    attn_grads = attn_grads.reshape(2, lines, chunk, -1).swapaxes(0, 1)
    attn_grads = attn_grads.reshape(lines, 2 * chunk, -1)
    attn_grads = lax.psum_scatter(attn_grads, "line", scatter_dimension=0, tiled=False)
    low_rows, high_rows = attn_grads[:chunk], attn_grads[chunk:]
    attn_grads = jnp.where(first, low_rows, high_rows).astype(f32) + swap(
        jnp.where(first, high_rows, low_rows)
    ).astype(f32)

    home = finish(
        attn_grad_terms,
        part_tokens,
        attn_gain_f,
        delta_one,
        hidden_one,
        out_mine,
        out_other,
        grad_moe_gain,
    )
    home = spread(exchange(home, DP), "tensor").reshape(own, -1)
    output, input_grad, gain_sum = deliver(home, home_hot)
    output = output.reshape(micro, block, width)
    input_grad = input_grad.reshape(micro, block, width)

    low_lanes, high_lanes = moe_grads[:, :block], moe_grads[:, block:]
    expert_grads = in_order(
        first,
        jnp.where(first, low_lanes, high_lanes),
        swap(jnp.where(first, high_lanes, low_lanes)),
    )
    expert_grads = expert_grads.reshape(2, expert_count // 4, 3, 2, HEAD, block)
    expert_grads = expert_grads.astype(f32)

    def expert_grad(index):
        return expert_grads[:, :, index].reshape(expert_count, HEAD, block)

    return (
        output,
        input_grad,
        gain_sum[0],
        attn_grads[:block, :local],
        attn_grads[:block, local : 2 * local],
        attn_grads[:block, 2 * local : 3 * local],
        attn_grads[block, :head_cut].reshape(heads, head_part),
        attn_grads[block, head_cut : 2 * head_cut].reshape(heads, head_part),
        attn_grads[:block, 3 * local :].T,
        gain_sum[1],
        expert_grad(0).transpose(0, 2, 1),
        expert_grad(1).transpose(0, 2, 1),
        expert_grad(2),
    )


def solution(mesh):
    lines = mesh.shape["dp"] // 2
    devices = mesh.devices.reshape(2, lines, mesh.shape["tensor"])
    placed = (
        P(None, DP, None),
        P(None, DP, None),
        P(),
        P(),
        P(None, DP, None),
        P(None, DP, None),
        P(DP),
        P(DP, "tensor"),
        P(DP, "tensor"),
        P(DP, "tensor"),
        P("tensor", DP),
        P("tensor", DP),
        P("tensor", DP),
        P(DP),
        P(None, DP, "tensor"),
        P(None, DP, "tensor"),
        P(None, "tensor", DP),
    )
    return jax.shard_map(
        body,
        mesh=Mesh(devices, DP + ("tensor",)),
        in_specs=placed,
        out_specs=(
            P(None, DP, None),
            P(None, DP, None),
            P(DP),
            P(DP, "tensor"),
            P(DP, "tensor"),
            P(DP, "tensor"),
            P("tensor", DP),
            P("tensor", DP),
            P("tensor", DP),
            P(DP),
            P(None, DP, "tensor"),
            P(None, DP, "tensor"),
            P(None, "tensor", DP),
        ),
        check_vma=False,
    )
```

```python
import jax
import jax.numpy as jnp
from jax import lax
from jax.experimental import pallas as pl
from jax.experimental.pallas import tpu as pltpu
from jax.sharding import Mesh
from jax.sharding import PartitionSpec as P

HEAD = 128
MIB = 1024 * 1024
bf16 = jnp.bfloat16
f32 = jnp.float32

DP = ("pair", "line")
PAIR_TENSOR = ("pair", "tensor")

RANKS = 8

epsilon = 1e-05
rope_base = 10000.0


def rope_tables(position):
    half_dim = HEAD // 2
    frequency = rope_base ** (-(jnp.arange(half_dim, dtype=f32) * 2.0 / HEAD))
    angle = position[:, None] * frequency[None, :]
    cosine = jnp.concatenate([jnp.cos(angle), jnp.cos(angle)], axis=-1)
    sine = jnp.concatenate([jnp.sin(angle), jnp.sin(angle)], axis=-1)
    return (cosine[:, None, :], sine[:, None, :])


def rotate(values, cosine, sine):
    half_dim = values.shape[-1] // 2
    turned = jnp.concatenate([-values[..., half_dim:], values[..., :half_dim]], axis=-1)
    return values * cosine + turned * sine


def rotate_back(gradient, cosine, sine):
    half_dim = gradient.shape[-1] // 2
    scaled = gradient * sine
    turned = jnp.concatenate([scaled[..., half_dim:], -scaled[..., :half_dim]], axis=-1)
    return gradient * cosine + turned


def norm_factor(values):
    return lax.rsqrt(jnp.mean(values * values, axis=-1, keepdims=True) + epsilon)


def norm_back(values, factor, gain, gradient):
    gained = gradient * gain
    inner_sum = jnp.sum(gained * values, axis=-1, keepdims=True)
    return factor * gained - values * (factor * factor * factor) * inner_sum / values.shape[-1]


def dot_nn(left_side, right_side):
    return jnp.dot(left_side, right_side, preferred_element_type=f32)


def dot_tn(left_side, right_side):
    return lax.dot_general(
        left_side, right_side, (((0,), (0,)), ((), ())), preferred_element_type=f32
    )


def dot_nt(left_side, right_side):
    return lax.dot_general(
        left_side, right_side, (((1,), (1,)), ((), ())), preferred_element_type=f32
    )


def exchange(value, axis):
    return lax.all_to_all(value, axis, split_axis=0, concat_axis=0, tiled=True)


def swap(value):
    return lax.ppermute(value, "pair", [(0, 1), (1, 0)])


def in_order(first, mine, other):
    return jnp.stack([jnp.where(first, mine, other), jnp.where(first, other, mine)])


def turned(values):
    cut = values.reshape(values.shape[:-1] + (2, -1, HEAD))
    return jnp.swapaxes(cut, -3, -2).reshape(values.shape)


def spread(value, axis):
    count = lax.axis_size(axis)
    copies = jnp.broadcast_to(value[None], (count,) + value.shape)
    return exchange(copies, axis)


BLOCK = 512

KEYS = slice(0, 128)
VALUES = slice(128, 256)
QUERIES = slice(256, 288)
Q_BLOCKS = 4


def masked_scores(query, keys, key_place, query_place, query_start):
    scores = dot_nt(query, keys) * (HEAD ** (-0.5))
    visible = (key_place <= query_place) & (key_place >= query_start)
    return jnp.where(visible, scores, -1e30)


def attention_kernel(packed, key_place, query_place, query_start, mixed, log_total):
    sources = packed.shape[0]
    keys = packed[:, KEYS, :].reshape(sources * 128, HEAD)
    values = packed[:, VALUES, :].reshape(sources * 128, HEAD)
    for part in range(sources // Q_BLOCKS):
        blocks = slice(part * Q_BLOCKS, (part + 1) * Q_BLOCKS)
        rows = slice(part * Q_BLOCKS * 32, (part + 1) * Q_BLOCKS * 32)
        query = packed[blocks, QUERIES, :].reshape(Q_BLOCKS * 32, HEAD)
        scores = masked_scores(
            query, keys, key_place[...], query_place[rows, :], query_start[rows, :]
        )
        peak = jnp.max(scores, axis=-1, keepdims=True)
        weights = jnp.exp(scores - peak)
        total = jnp.sum(weights, axis=-1, keepdims=True)
        probs = (weights / total).astype(bf16)
        mixed[blocks, :, :] = (
            dot_nn(probs, values).astype(bf16).reshape(Q_BLOCKS, 32, HEAD)
        )
        log_total[rows, :] = peak + jnp.log(total)


def attention_back_kernel(
    packed, key_place, query_place, query_start, log_total, delta_mixed, out, key_sum, value_sum
):
    sources = packed.shape[0]
    keys = packed[:, KEYS, :].reshape(sources * 128, HEAD)
    values = packed[:, VALUES, :].reshape(sources * 128, HEAD)
    scale = HEAD ** (-0.5)
    for part in range(sources // Q_BLOCKS):
        blocks = slice(part * Q_BLOCKS, (part + 1) * Q_BLOCKS)
        rows = slice(part * Q_BLOCKS * 32, (part + 1) * Q_BLOCKS * 32)
        query = packed[blocks, QUERIES, :].reshape(Q_BLOCKS * 32, HEAD)
        delta = delta_mixed[blocks, :, :].reshape(Q_BLOCKS * 32, HEAD)
        scores = masked_scores(
            query, keys, key_place[...], query_place[rows, :], query_start[rows, :]
        )
        probs = jnp.exp(scores - log_total[rows, :])
        delta_probs = dot_nt(delta, values)
        inner = jnp.sum(probs * delta_probs, axis=-1, keepdims=True)
        delta_scores = (probs * (delta_probs - inner)).astype(bf16)
        out[blocks, QUERIES, :] = (
            (dot_nn(delta_scores, keys) * scale).astype(bf16).reshape(Q_BLOCKS, 32, HEAD)
        )
        key_term = dot_tn(delta_scores, query)
        value_term = dot_tn(probs.astype(bf16), delta)
        if part == 0:
            key_sum[...] = key_term
            value_sum[...] = value_term
        else:
            key_sum[...] += key_term
            value_sum[...] += value_term
    out[:, KEYS, :] = (key_sum[...] * scale).astype(bf16).reshape(sources, 128, HEAD)
    out[:, VALUES, :] = value_sum[...].astype(bf16).reshape(sources, 128, HEAD)


def attention(packed, key_place, query_place, query_start):
    sources = packed.shape[0]
    return pl.pallas_call(
        attention_kernel,
        out_shape=(
            jax.ShapeDtypeStruct((sources, 32, HEAD), bf16),
            jax.ShapeDtypeStruct((sources * 32, 1), f32),
        ),
        compiler_params=pltpu.CompilerParams(vmem_limit_bytes=40 * MIB),
        name="attention",
    )(packed, key_place, query_place, query_start)


def attention_back(packed, key_place, query_place, query_start, log_total, delta_mixed):
    sources = packed.shape[0]
    return pl.pallas_call(
        attention_back_kernel,
        out_shape=jax.ShapeDtypeStruct(packed.shape, bf16),
        scratch_shapes=[
            pltpu.VMEM((sources * 128, HEAD), f32),
            pltpu.VMEM((sources * 128, HEAD), f32),
        ],
        compiler_params=pltpu.CompilerParams(vmem_limit_bytes=40 * MIB),
        name="attention_back",
    )(packed, key_place, query_place, query_start, log_total, delta_mixed)


def attention_grads_kernel(normed, delta_pre, delta_attn, mixed, out):
    lines = out.shape[0]
    pre_width = delta_pre.shape[1]
    for line in range(lines):
        lanes = slice(2 * line * HEAD, 2 * (line + 1) * HEAD)
        out[line, :, :pre_width] = dot_tn(normed[:, lanes], delta_pre[...]).astype(bf16)
        out[line, :, pre_width:] = dot_tn(delta_attn[:, lanes], mixed[...]).astype(bf16)


def attention_grads(normed, delta_pre, delta_attn, mixed):
    lines = normed.shape[1] // HEAD // 2
    return pl.pallas_call(
        attention_grads_kernel,
        out_shape=jax.ShapeDtypeStruct(
            (lines, 2 * HEAD, delta_pre.shape[1] + mixed.shape[1]), bf16
        ),
        compiler_params=pltpu.CompilerParams(vmem_limit_bytes=24 * MIB),
        name="attention_grads",
    )(normed, delta_pre, delta_attn, mixed)


def stack_attention_kernel(w_query, w_key, w_value, w_out, out):
    local = w_query.shape[1]
    out[:, :local] = w_query[...]
    out[:, local : 2 * local] = w_key[...]
    out[:, 2 * local : 3 * local] = w_value[...]
    out[:, 3 * local :] = w_out[...].T


def stack_attention(w_query, w_key, w_value, w_out):
    rows, local = w_query.shape
    return pl.pallas_call(
        stack_attention_kernel,
        out_shape=jax.ShapeDtypeStruct((rows, 4 * local), bf16),
        name="stack_attention",
    )(w_query, w_key, w_value, w_out)


def stack_experts_kernel(pair, w_gate, w_up, w_down, kept, sent):
    half = w_gate.shape[0] // 2
    each = BLOCK // HEAD
    for out, which in ((kept, pair[0]), (sent, 1 - pair[0])):
        for expert in range(half):
            for index, stored in enumerate((w_gate, w_up, w_down)):
                start = expert // each * 3 * BLOCK + index * BLOCK + expert % each * HEAD
                value = stored[which * half + expert]
                out[:, start : start + HEAD] = value.T if stored is w_down else value


def stack_experts(pair, w_gate, w_up, w_down):
    count, rows, hidden = w_gate.shape
    shape = jax.ShapeDtypeStruct((rows, 3 * count * hidden // 2), bf16)
    return pl.pallas_call(
        stack_experts_kernel,
        in_specs=[pl.BlockSpec(memory_space=pltpu.SMEM)]
        + [pl.BlockSpec(memory_space=pltpu.VMEM)] * 3,
        out_shape=(shape, shape),
        compiler_params=pltpu.CompilerParams(vmem_limit_bytes=24 * MIB),
        name="stack_experts",
    )(pair.reshape(1), w_gate, w_up, w_down)


def experts_kernel(my_rank, arrived, upstream, gates, weights, *refs):
    (
        out_kept,
        out_sent,
        delta_in,
        grads,
        held,
        hidden_all,
        deltas_all,
        grads_out,
        out_all,
        rows,
        in_sem,
        out_sem,
    ) = refs
    steps = held.shape[0]
    width = upstream.shape[1]
    lines = grads.shape[0]
    lane_part = width // lines
    part = out_kept.shape[2]
    loads = [
        pltpu.make_async_copy(
            weights.at[:, pl.ds(c * 3 * BLOCK, 3 * BLOCK)], held.at[c], in_sem.at[c]
        )
        for c in range(steps)
    ]
    for load in loads:
        load.start()
    for k in range(arrived.shape[0]):
        rows[k * part : (k + 1) * part, :] = from_blocks(arrived.at[k])
    stores = []
    for c in range(steps):
        loads[c].wait()
        gate_up = dot_nn(rows[...], held[c, :, 0 : 2 * BLOCK])
        gate_h, up_h = gate_up[:, :BLOCK], gate_up[:, BLOCK:]
        delta_hidden = dot_nn(upstream[...], held[c, :, 2 * BLOCK : 3 * BLOCK])
        share = jnp.concatenate(
            [
                jnp.broadcast_to(gates[:, e : e + 1], (gates.shape[0], HEAD))
                for e in range(c * BLOCK // HEAD, (c + 1) * BLOCK // HEAD)
            ],
            axis=1,
        )
        sigmoid_gate = 1.0 / (1.0 + jnp.exp(-gate_h))
        active = gate_h * sigmoid_gate
        hidden = (active * up_h * share).astype(bf16)
        delta_hidden = delta_hidden * share
        delta_gate = (
            delta_hidden * up_h * sigmoid_gate * (1.0 + gate_h * (1.0 - sigmoid_gate))
        ).astype(bf16)
        delta_up = (delta_hidden * active).astype(bf16)
        start = 2 * c * BLOCK
        hidden_all[:, c * BLOCK : (c + 1) * BLOCK] = hidden
        deltas_all[:, start : start + BLOCK] = delta_gate
        deltas_all[:, start + BLOCK : start + 2 * BLOCK] = delta_up
        deltas = deltas_all[:, start : start + 2 * BLOCK]
        slot = c % 2
        if c >= 2:
            stores[c - 2].wait()
        for n in range(lines):
            lanes = slice(n * lane_part, (n + 1) * lane_part)
            grads_out[slot, n, 0 : 2 * BLOCK, :] = dot_tn(deltas, rows[:, lanes]).astype(bf16)
            grads_out[slot, n, 2 * BLOCK :, :] = dot_tn(hidden, upstream[:, lanes]).astype(bf16)
        store = pltpu.make_async_copy(
            grads_out.at[slot], grads.at[:, pl.ds(c * 3 * BLOCK, 3 * BLOCK), :], out_sem.at[slot]
        )
        store.start()
        stores.append(store)
    for n in range(lines):
        lanes = slice(n * lane_part, (n + 1) * lane_part)
        gate_up = jnp.concatenate(
            [held[c, lanes, 0 : 2 * BLOCK] for c in range(steps)], axis=1
        )
        produced = dot_nt(deltas_all[...], gate_up).astype(bf16)
        for k in range(2 * RANKS):
            for b in range(lane_part // HEAD):
                delta_in[k, n * (lane_part // HEAD) + b] = produced[
                    k * part : (k + 1) * part, b * HEAD : (b + 1) * HEAD
                ]
        down = jnp.concatenate(
            [held[c, lanes, 2 * BLOCK : 3 * BLOCK] for c in range(steps)], axis=1
        )
        produced = dot_nt(hidden_all[...], down).astype(bf16)
        out_all[:, :, lanes] = produced.reshape(2 * RANKS, part, lane_part)
    high = my_rank[0] // (RANKS // 2)
    for p in range(2):
        for q in range(RANKS // 2):
            out_kept[q, p] = out_all[p * RANKS + high * (RANKS // 2) + q]
            out_sent[q, p] = out_all[p * RANKS + (1 - high) * (RANKS // 2) + q]
    for store in stores[-2:]:
        store.wait()


def experts(my_rank, arrived, upstream, gates, weights, lines):
    count, width = upstream.shape
    part = count // RANKS // 2
    steps = weights.shape[1] // (3 * BLOCK)
    in_vmem = pl.BlockSpec(memory_space=pltpu.VMEM)
    in_hbm = pl.BlockSpec(memory_space=pl.ANY)
    return pl.pallas_call(
        experts_kernel,
        in_specs=[pl.BlockSpec(memory_space=pltpu.SMEM), in_vmem, in_vmem, in_vmem, in_hbm],
        out_specs=[in_vmem, in_vmem, in_vmem, in_hbm],
        out_shape=(
            *[jax.ShapeDtypeStruct((RANKS // 2, 2, part, width), bf16)] * 2,
            jax.ShapeDtypeStruct(arrived.shape, bf16),
            jax.ShapeDtypeStruct((lines, weights.shape[1], width // lines), bf16),
        ),
        scratch_shapes=[
            pltpu.VMEM((steps, width, 3 * BLOCK), bf16),
            pltpu.VMEM((count, steps * BLOCK), bf16),
            pltpu.VMEM((count, 2 * steps * BLOCK), bf16),
            pltpu.VMEM((2, lines, 3 * BLOCK, width // lines), bf16),
            pltpu.VMEM((2 * RANKS, part, width), bf16),
            pltpu.VMEM((count, width), bf16),
            pltpu.SemaphoreType.DMA((steps,)),
            pltpu.SemaphoreType.DMA((2,)),
        ],
        compiler_params=pltpu.CompilerParams(vmem_limit_bytes=56 * MIB),
        name="experts",
    )(my_rank.reshape(1), arrived, upstream, gates, weights)


def expert_gradients_kernel(pair, kept, got, gate_grad, up_grad, down_grad):
    half = gate_grad.shape[0] // 2
    each = BLOCK // HEAD
    for stored, which in ((kept, pair[0]), (got, 1 - pair[0])):
        for expert in range(half):
            for index, out in enumerate((gate_grad, up_grad, down_grad)):
                start = expert // each * 3 * BLOCK + index * BLOCK + expert % each * HEAD
                value = stored[start : start + HEAD].astype(f32)
                out[which * half + expert] = value if out is down_grad else value.T


def expert_gradients(pair, kept, got):
    count = 2 * kept.shape[0] // 3 // HEAD
    in_vmem = pl.BlockSpec(memory_space=pltpu.VMEM)
    shape = jax.ShapeDtypeStruct((count, kept.shape[1], HEAD), f32)
    return pl.pallas_call(
        expert_gradients_kernel,
        in_specs=[pl.BlockSpec(memory_space=pltpu.SMEM), in_vmem, in_vmem],
        out_shape=(shape, shape, shape),
        compiler_params=pltpu.CompilerParams(vmem_limit_bytes=24 * MIB),
        name="expert_gradients",
    )(pair.reshape(1), kept, got)


def summed(terms):
    total = terms[0].astype(f32)
    for k in range(1, terms.shape[0]):
        total = total + terms[k].astype(f32)
    return total


def put_blocks(out, rows):
    for block in range(out.shape[0]):
        out[block] = rows[:, block * HEAD : (block + 1) * HEAD]


def from_blocks(blocks):
    return jnp.concatenate([blocks[k] for k in range(blocks.shape[0])], axis=1)


def lane_blocks(width, forward):
    lines = width // HEAD // 2
    moves = [(p * lines + n, n * 2 + p) for p in range(2) for n in range(lines)]
    return moves if forward else [(b, a) for a, b in moves]


def move_lanes(values, forward):
    moves = sorted((b, a) for a, b in lane_blocks(values.shape[-1], forward))
    return jnp.concatenate([values[:, a * HEAD : (a + 1) * HEAD] for _, a in moves], axis=1)


def deal_kernel(where, places, tokens, cotangent, gains, out):
    count, width = tokens.shape
    rows, block = places.shape
    given = places[...] - where[0] * block
    mine = (given >= 0) & (given < block)
    before = lax.broadcasted_iota(jnp.int32, (block, block), 0) < lax.broadcasted_iota(
        jnp.int32, (block, block), 1
    )
    rank = dot_nn(
        jnp.where(mine, 1.0, 0.0).astype(bf16), jnp.where(before, 1.0, 0.0).astype(bf16)
    ).astype(jnp.int32)
    hit = mine & (rank == where[1])
    order = jnp.sum(jnp.where(hit, given, 0), axis=1, keepdims=True)
    micro = lax.broadcasted_iota(jnp.int32, (rows, 1), 0) % (count // block)
    hot = order + micro * block == lax.broadcasted_iota(jnp.int32, (rows, count), 1)
    hot = jnp.where(hot, 1.0, 0.0).astype(bf16)
    out[:, :width] = move_lanes(dot_nn(hot, tokens[...]).astype(bf16), True)
    gradient = move_lanes(dot_nn(hot, cotangent[...]).astype(bf16), True)
    out[:, width : 2 * width] = gradient
    out[: rows // 2, 2 * width : 3 * width] = gradient[rows // 2 :]
    out[rows // 2 :, 2 * width : 3 * width] = gradient[: rows // 2]
    odd = lax.broadcasted_iota(jnp.int32, (rows, gains.shape[1]), 0) % 2 == 1
    values = gains[...].astype(f32)
    out[:, 3 * width :] = jnp.where(odd, values[1:2], values[0:1]).astype(bf16)


def deal(where, places, tokens, cotangent, gains):
    width = tokens.shape[1]
    in_vmem = pl.BlockSpec(memory_space=pltpu.VMEM)
    return pl.pallas_call(
        deal_kernel,
        in_specs=[pl.BlockSpec(memory_space=pltpu.SMEM)] + [in_vmem] * 4,
        out_shape=jax.ShapeDtypeStruct((places.shape[0], 3 * width + gains.shape[1]), bf16),
        compiler_params=pltpu.CompilerParams(vmem_limit_bytes=24 * MIB),
        name="deal",
    )(where, places, tokens, cotangent, gains)


def before_experts_kernel(terms, tokens, gain, hidden_one, factor, moe_in):
    hidden = tokens[...].astype(f32) + summed(terms)
    scale = norm_factor(hidden)
    hidden_one[...] = hidden
    factor[...] = scale
    rows = (hidden * scale * gain[...]).astype(bf16)
    for k in range(moe_in.shape[0]):
        put_blocks(moe_in.at[k], rows)


def before_experts(terms, tokens, gain):
    rows, width = tokens.shape
    return pl.pallas_call(
        before_experts_kernel,
        out_shape=(
            jax.ShapeDtypeStruct((rows, width), f32),
            jax.ShapeDtypeStruct((rows, 1), f32),
            jax.ShapeDtypeStruct((2 * RANKS, width // HEAD, rows, HEAD), bf16),
        ),
        name="before_experts",
    )(terms, tokens, gain)


def after_experts_kernel(
    terms, hidden_one, factor, gain, upstream, delta_one, delta_attn, gain_grad
):
    gradient = from_blocks(summed(terms))
    hidden = hidden_one[...]
    gain_grad[...] = jnp.sum(gradient * hidden * factor[...], axis=0, keepdims=True)
    delta = upstream[...].astype(f32) + norm_back(hidden, factor[...], gain[...], gradient)
    delta_one[...] = delta
    for k in range(delta_attn.shape[0]):
        delta_attn[k] = delta.astype(bf16)


def after_experts(terms, hidden_one, factor, gain, upstream):
    rows, width = upstream.shape
    return pl.pallas_call(
        after_experts_kernel,
        out_shape=(
            jax.ShapeDtypeStruct((rows, width), f32),
            jax.ShapeDtypeStruct((RANKS, rows, width), bf16),
            jax.ShapeDtypeStruct((1, width), f32),
        ),
        name="after_experts",
    )(terms, hidden_one, factor, gain, upstream)


def halve_kernel(bit, kept, got, mine, sent):
    half = mine.shape[0]
    for out, start in ((mine, bit[0] * half), (sent, (1 - bit[0]) * half)):
        for k in range(half):
            total = kept[start + k].astype(f32) + got[start + k].astype(f32)
            out[k] = total.astype(out.dtype)


def halve(bit, kept, got):
    shape = (kept.shape[0] // 2,) + kept.shape[1:]
    in_vmem = pl.BlockSpec(memory_space=pltpu.VMEM)
    return pl.pallas_call(
        halve_kernel,
        in_specs=[pl.BlockSpec(memory_space=pltpu.SMEM), in_vmem, in_vmem],
        out_shape=(jax.ShapeDtypeStruct(shape, f32), jax.ShapeDtypeStruct(shape, bf16)),
        compiler_params=pltpu.CompilerParams(vmem_limit_bytes=24 * MIB),
        name="halve",
    )(bit.reshape(1), kept, got)


def quarter_terms_kernel(bits, kept, got, mine, other, across_mine, across_other):
    for out, y, p in (
        (mine, bits[0], bits[1]),
        (other, bits[0], 1 - bits[1]),
        (across_mine, 1 - bits[0], bits[1]),
        (across_other, 1 - bits[0], 1 - bits[1]),
    ):
        out[...] = (kept[y, p].astype(f32) + got[y, p].astype(f32)).astype(out.dtype)


def quarter_terms(y, pair, kept, got):
    rows, width = kept.shape[2:]
    in_vmem = pl.BlockSpec(memory_space=pltpu.VMEM)
    return pl.pallas_call(
        quarter_terms_kernel,
        in_specs=[pl.BlockSpec(memory_space=pltpu.SMEM), in_vmem, in_vmem],
        out_shape=(
            jax.ShapeDtypeStruct((rows, width), f32),
            *[jax.ShapeDtypeStruct((rows, width), bf16)] * 3,
        ),
        name="quarter_terms",
    )(jnp.stack([y, pair]), kept, got)


def finish_kernel(
    terms,
    tokens,
    gain,
    delta_one,
    hidden_one,
    out_mine,
    out_second,
    out_third,
    out_fourth,
    moe_gain_grad,
    head_gain_grads,
    home,
):
    width = tokens.shape[1]
    values = tokens[...].astype(f32)
    gradient = summed(terms)
    factor = norm_factor(values)
    gain_grad = jnp.sum(gradient * values * factor, axis=0, keepdims=True)
    moe_out = out_mine[...]
    for term in (out_second, out_third, out_fourth):
        moe_out = moe_out + term[...].astype(f32)
    output = move_lanes((hidden_one[...] + moe_out).astype(bf16), False)
    input_grad = delta_one[...] + norm_back(values, factor, gain[...], gradient)
    input_grad = move_lanes(input_grad.astype(bf16), False)
    rows = []
    for moved, _ in sorted(lane_blocks(width, False), key=lambda move: move[1]):
        lanes = slice(moved * HEAD, (moved + 1) * HEAD)
        rows.append(gain_grad[:, lanes])
        rows.append(moe_gain_grad[:, lanes])
    gains = jnp.concatenate(rows, axis=0).astype(bf16)
    sent = jnp.concatenate(
        [output, input_grad, gains, head_gain_grads[...].astype(bf16)], axis=1
    )
    micro = home.shape[2]
    for source in range(home.shape[1]):
        piece = sent[source * micro : (source + 1) * micro]
        for k in range(home.shape[0]):
            home[k, source] = piece


def finish(micro, terms, tokens, *others):
    rows, width = tokens.shape
    shape = (RANKS, rows // micro, micro, 2 * width + 2 * HEAD)
    return pl.pallas_call(
        finish_kernel,
        out_shape=jax.ShapeDtypeStruct(shape, bf16),
        name="finish",
    )(terms, tokens, *others)


def deliver_kernel(rank, rows, hot, output, input_grad, gains, head_gains):
    count, width = output.shape
    output[...] = dot_nn(hot[...], rows[:, :width]).astype(bf16)
    input_grad[...] = dot_nn(hot[...], rows[:, width : 2 * width]).astype(bf16)
    terms = rows[:, 2 * width : 2 * width + HEAD].astype(f32)
    odd = lax.broadcasted_iota(jnp.int32, terms.shape, 0) % 2
    gains[...] = jnp.concatenate(
        [
            jnp.sum(jnp.where(odd == 0, terms, 0.0), axis=0, keepdims=True),
            jnp.sum(jnp.where(odd == 1, terms, 0.0), axis=0, keepdims=True),
        ],
        axis=0,
    )
    terms = rows[:, 2 * width + HEAD :].astype(f32)
    sender = lax.broadcasted_iota(jnp.int32, terms.shape, 0) // (count // RANKS)
    head_gains[...] = jnp.sum(jnp.where(sender == rank[0], terms, 0.0), axis=0, keepdims=True)


def deliver(rank, rows, hot):
    count, lanes = rows.shape
    in_vmem = pl.BlockSpec(memory_space=pltpu.VMEM)
    shape = jax.ShapeDtypeStruct((count, lanes // 2 - HEAD), bf16)
    return pl.pallas_call(
        deliver_kernel,
        in_specs=[pl.BlockSpec(memory_space=pltpu.SMEM), in_vmem, in_vmem],
        out_shape=(
            shape,
            shape,
            jax.ShapeDtypeStruct((2, HEAD), f32),
            jax.ShapeDtypeStruct((1, HEAD), f32),
        ),
        compiler_params=pltpu.CompilerParams(vmem_limit_bytes=24 * MIB),
        name="deliver",
    )(rank.reshape(1), rows, hot)


def body(
    tokens,
    cotangent,
    pack_perm,
    lengths,
    routes,
    gates,
    attn_gain,
    w_query,
    w_key,
    w_value,
    query_gain,
    key_gain,
    w_out,
    moe_gain,
    w_gate,
    w_up,
    w_down,
):
    pair = lax.axis_index("pair")
    first = pair == 0
    lines = lax.axis_size("line")
    dp = 2 * lines
    te = lax.axis_size("tensor")
    me = lax.axis_index(DP)
    my_te = lax.axis_index("tensor")
    micro, block, width = tokens.shape
    ranks = block // dp
    own = micro * block
    part = own // te
    local = w_query.shape[1]
    heads = local // HEAD
    head_part = HEAD // dp
    quarters = dp // (micro * heads)
    expert_count = w_gate.shape[0]

    attn_local = stack_attention(w_query, w_key, w_value, w_out)
    moe_kept, moe_sent = stack_experts(pair, w_gate, w_up, w_down)

    blocks = pack_perm.reshape(micro, dp, block)
    root = blocks // block
    earlier = jnp.arange(block)[None, :] < jnp.arange(block)[:, None]
    rank = jnp.sum(
        ((root[:, :, :, None] == root[:, :, None, :]) & earlier).astype(jnp.int32), axis=3
    )
    from_me = (root == me)[:, :, None, :] & (
        rank[:, :, None, :] == jnp.arange(ranks, dtype=jnp.int32)[None, None, :, None]
    )
    given = jnp.sum(jnp.where(from_me, (blocks - me * block)[:, :, None, :], 0), axis=3)
    given = given + (jnp.arange(micro, dtype=jnp.int32) * block)[:, None, None]
    row_index = jnp.arange(own, dtype=jnp.int32)
    home_order = given.transpose(2, 1, 0).reshape(own)
    home_hot = (row_index[:, None] == home_order[None, :]).astype(bf16)
    slot = rank * dp + root
    slot_hot = slot[:, :, None, :] == jnp.arange(block, dtype=jnp.int32)[None, None, :, None]
    place_in = jnp.sum(
        jnp.where(slot_hot, jnp.arange(block, dtype=jnp.int32)[None, None, None, :], 0), axis=3
    )
    place_of = place_in + (jnp.arange(dp, dtype=jnp.int32) * block)[None, :, None]

    head_cut = heads * head_part
    head_gains = jnp.concatenate(
        [
            query_gain.reshape(1, head_cut),
            key_gain.reshape(1, head_cut),
            jnp.zeros((1, block - 2 * head_cut), bf16),
        ],
        axis=1,
    )
    gains = jnp.concatenate(
        [
            jnp.concatenate([attn_gain[None], head_gains], axis=1),
            jnp.concatenate([moe_gain[None], head_gains], axis=1),
        ],
        axis=0,
    )
    dealt = deal(
        jnp.stack([me, my_te]),
        blocks.transpose(1, 0, 2).reshape(part, block),
        tokens.reshape(own, width),
        cotangent.reshape(own, width),
        gains,
    )
    attn_local = in_order(first, attn_local, swap(attn_local)).reshape(2 * block, -1)
    attn_local = lax.optimization_barrier((attn_local, dealt))[0]
    attn_w = lax.all_gather(attn_local, "line", axis=0, tiled=True)
    dealt = exchange(dealt, DP)
    part_tokens = dealt[:, :width]
    part_cotangent = dealt[:, width : 2 * width]
    gains = dealt[:, 3 * width :].reshape(dp, micro, 2 * block)
    attn_gain_f = turned(gains[:, 0, :block].reshape(1, width)).astype(f32)
    moe_gain_f = turned(gains[:, 1, :block].reshape(1, width)).astype(f32)

    def head_gain(cut):
        return cut.reshape(dp, heads, head_part).transpose(1, 0, 2).reshape(local).astype(f32)

    query_scale = head_gain(gains[:, 0, block : block + head_cut])
    key_scale = head_gain(gains[:, 0, block + head_cut : block + 2 * head_cut])
    own_tokens = spread(part_tokens, "tensor").reshape(own, width)

    pair_cotangent = in_order(first, part_cotangent, dealt[:, 2 * width : 3 * width])
    pair_cotangent = pair_cotangent.reshape(2 * part, width)
    pair_cotangent = lax.all_gather(pair_cotangent, "tensor", axis=0, tiled=True)
    pair_cotangent = pair_cotangent.reshape(te, 2, part, width).transpose(1, 0, 2, 3)
    pair_cotangent = pair_cotangent.reshape(2 * own, width)

    seq_ends = jnp.cumsum(lengths, axis=1)
    seq_starts = seq_ends - lengths

    def start_of(place, ends, starts):
        inside = (place[..., None] >= starts) & (place[..., None] < ends)
        return jnp.sum(jnp.where(inside, starts, 0), axis=-1)

    own_place = lax.dynamic_index_in_dim(place_of, me, axis=1, keepdims=False)
    own_start = start_of(own_place, seq_ends[:, None, :], seq_starts[:, None, :])
    position = (own_place - own_start).astype(f32)
    position = position.reshape(micro, ranks, dp).transpose(1, 2, 0).reshape(own)
    cosine, sine = rope_tables(position)
    pair_micro = me // (heads * quarters)
    quarter = me % quarters
    key_place = lax.dynamic_index_in_dim(place_of, pair_micro, axis=0, keepdims=False)
    query_place = lax.dynamic_slice_in_dim(
        key_place, quarter * (block // quarters), block // quarters, axis=1
    ).reshape(-1, 1)
    pair_ends = lax.dynamic_index_in_dim(seq_ends, pair_micro, axis=0)
    pair_starts = lax.dynamic_index_in_dim(seq_starts, pair_micro, axis=0)
    query_start = start_of(query_place, pair_ends[None], pair_starts[None])
    key_place = key_place.reshape(1, -1)

    hot = routes[..., None] == jnp.arange(expert_count, dtype=jnp.int32)
    dense = jnp.sum(jnp.where(hot, gates[..., None], 0.0), axis=2)
    own_slot_hot = lax.dynamic_index_in_dim(slot_hot, me, axis=1, keepdims=False)
    share = jnp.einsum(
        "msj,mje->mse", own_slot_hot.astype(f32), dense, precision=lax.Precision.HIGHEST
    )
    share = share.reshape(micro, ranks, dp, expert_count).transpose(1, 2, 0, 3)
    share = share.reshape(own, expert_count)
    qkv_w = attn_w[:, : 3 * local]
    out_w = attn_w[:, 3 * local : 4 * local]
    inputs = own_tokens.astype(f32)
    attn_factor = norm_factor(inputs)
    normed_b = (inputs * attn_factor * attn_gain_f).astype(bf16)
    qkv = dot_nn(normed_b, qkv_w)
    moe_sent, share, _ = lax.optimization_barrier((moe_sent, share, qkv))
    moe_got, share_got = swap(moe_sent), swap(share)
    query_pre = qkv[:, :local]
    key_pre = qkv[:, local : 2 * local]
    value_b = qkv[:, 2 * local :].astype(bf16)
    squares = jnp.stack(
        [jnp.sum(query_pre * query_pre, axis=1), jnp.sum(key_pre * key_pre, axis=1)]
    )
    squares = jnp.sum(spread(squares, "tensor"), axis=0)
    factors = lax.rsqrt(squares / width + epsilon)
    query_factor = factors[0][:, None]
    key_factor = factors[1][:, None]
    query_b = rotate(
        (query_pre * query_factor * query_scale).reshape(own, heads, HEAD), cosine, sine
    ).astype(bf16)
    key_b = rotate(
        (key_pre * key_factor * key_scale).reshape(own, heads, HEAD), cosine, sine
    ).astype(bf16)

    def to_pairs(values):
        cut = values.reshape(ranks, dp, micro, heads, HEAD)
        return cut.transpose(2, 3, 0, 1, 4).reshape(micro, heads, block, HEAD)

    def to_quarters(values):
        return to_pairs(values).reshape(micro, heads, quarters, block // quarters, HEAD)

    def from_pairs(values):
        cut = values.reshape(micro, heads, ranks, dp, HEAD)
        return cut.transpose(2, 3, 0, 1, 4).reshape(own, local)

    copies = (micro, heads, quarters, block, HEAD)
    sent = jnp.concatenate(
        [
            jnp.broadcast_to(to_pairs(key_b)[:, :, None], copies),
            jnp.broadcast_to(to_pairs(value_b.reshape(own, heads, HEAD))[:, :, None], copies),
            to_quarters(query_b),
        ],
        axis=3,
    )
    moe_local = in_order(first, moe_kept, moe_got).reshape(2 * block, -1)
    share = in_order(first, share, share_got).reshape(2 * own, expert_count)
    share = lax.dynamic_slice_in_dim(share, pair * (expert_count // 2), expert_count // 2, axis=1)
    packed = exchange(sent.reshape(dp, 2 * block + block // quarters, HEAD), DP)
    moe_local = lax.optimization_barrier((moe_local, packed))[0]
    moe_w = lax.all_gather(moe_local, "line", axis=0, tiled=True)
    pair_mixed, log_total = attention(packed, key_place, query_place, query_start)
    mixed_b = from_pairs(exchange(pair_mixed, DP))

    def terms_of(value):
        return exchange(value.astype(bf16).reshape(te, part, width), "tensor")

    hidden_one, moe_factor, moe_in = before_experts(
        terms_of(dot_nt(mixed_b, out_w)), part_tokens, moe_gain_f
    )

    moe_in = exchange(moe_in, PAIR_TENSOR)
    out_kept, out_sent, moe_grad_part, moe_grads = experts(
        my_te, moe_in, pair_cotangent, share, moe_w, lines
    )
    moe_grads = lax.psum_scatter(moe_grads, "line", scatter_dimension=0, tiled=False)
    moe_grad_terms = exchange(moe_grad_part, PAIR_TENSOR)
    delta_one, delta_attn, grad_moe_gain = after_experts(
        moe_grad_terms, hidden_one, moe_factor, moe_gain_f, part_cotangent
    )
    delta_attn = exchange(delta_attn, "tensor").reshape(own, width)
    def across(value, partner):
        return lax.ppermute(value, "tensor", [(k, partner(k)) for k in range(te)])

    out_sent = lax.optimization_barrier((out_sent, delta_attn))[0]
    out_got = across(out_sent, lambda k: 2 * (3 - k // 2) + k % 2)

    delta_mixed = dot_nn(delta_attn, out_w).astype(bf16)
    pair_delta = exchange(
        to_quarters(delta_mixed.reshape(own, heads, HEAD)).reshape(dp, block // quarters, HEAD),
        DP,
    )
    pair_delta, moe_grads = lax.optimization_barrier((pair_delta, moe_grads))
    pair_grads = attention_back(
        packed, key_place, query_place, query_start, log_total, pair_delta
    )
    pair_grads, out_got = lax.optimization_barrier((pair_grads, out_got))
    out_kept, out_sent = halve(my_te // 2 % 2, out_kept, out_got)
    out_got = across(out_sent, lambda k: k ^ 2)
    got, out_got, moe_grads = lax.optimization_barrier(
        (exchange(pair_grads, DP), out_got, moe_grads)
    )
    out_terms = quarter_terms(my_te % 2, pair, out_kept, out_got)
    out_terms = (
        out_terms[0],
        swap(out_terms[1]),
        across(out_terms[2], lambda k: k ^ 1),
        lax.ppermute(
            out_terms[3], PAIR_TENSOR, [(k, (k + te) % (2 * te) ^ 1) for k in range(2 * te)]
        ),
    )
    got = got.reshape(micro, heads, quarters, -1, HEAD)
    delta_key = from_pairs(jnp.sum(got[:, :, :, KEYS].astype(f32), axis=2))
    delta_value = from_pairs(jnp.sum(got[:, :, :, VALUES].astype(f32), axis=2))
    delta_query = from_pairs(got[:, :, :, QUERIES].astype(f32))
    delta_qnorm = rotate_back(delta_query.reshape(own, heads, HEAD), cosine, sine)
    delta_qnorm = delta_qnorm.reshape(own, local)
    delta_knorm = rotate_back(delta_key.reshape(own, heads, HEAD), cosine, sine)
    delta_knorm = delta_knorm.reshape(own, local)
    grad_qgain = jnp.sum(delta_qnorm * query_pre * query_factor, axis=0)
    grad_kgain = jnp.sum(delta_knorm * key_pre * key_factor, axis=0)
    weighted_query = delta_qnorm * query_scale
    weighted_key = delta_knorm * key_scale
    inner = jnp.stack(
        [jnp.sum(weighted_query * query_pre, axis=1), jnp.sum(weighted_key * key_pre, axis=1)]
    )
    inner, moe_grads = lax.optimization_barrier((spread(inner, "tensor"), moe_grads))
    inner = jnp.sum(inner, axis=0) / width
    low_lanes, high_lanes = moe_grads[:, :block], moe_grads[:, block:]
    grads_kept = jnp.where(first, low_lanes, high_lanes)
    grads_got = swap(jnp.where(first, high_lanes, low_lanes))
    delta_qpre = query_factor * weighted_query - query_pre * (
        query_factor * query_factor * query_factor
    ) * inner[0][:, None]
    delta_kpre = key_factor * weighted_key - key_pre * (
        key_factor * key_factor * key_factor
    ) * inner[1][:, None]
    delta_pre = jnp.concatenate(
        [delta_qpre.astype(bf16), delta_kpre.astype(bf16), delta_value.astype(bf16)], axis=1
    )
    attn_grad = dot_nt(delta_pre, qkv_w).astype(bf16)
    attn_grad, out_terms = lax.optimization_barrier((attn_grad, out_terms))
    attn_grad_terms = terms_of(attn_grad)
    attn_grads = attention_grads(
        normed_b, lax.optimization_barrier((delta_pre, attn_grad))[0], delta_attn, mixed_b
    )
    attn_grads = lax.psum_scatter(attn_grads, "line", scatter_dimension=0, tiled=False)
    low_rows, high_rows = attn_grads[:block], attn_grads[block:]
    attn_grads = jnp.where(first, low_rows, high_rows).astype(f32) + swap(
        jnp.where(first, high_rows, low_rows)
    ).astype(f32)

    def gain_cut(gradient):
        return gradient.reshape(heads, dp, head_part).transpose(1, 0, 2).reshape(dp, -1)

    head_gain_grads = jnp.concatenate([gain_cut(grad_qgain), gain_cut(grad_kgain)], axis=1)
    head_gain_grads = jnp.pad(
        head_gain_grads[:, None], ((0, 0), (0, micro - 1), (0, HEAD - 2 * head_cut))
    ).reshape(part, HEAD)
    home = finish(
        micro,
        attn_grad_terms,
        part_tokens,
        attn_gain_f,
        delta_one,
        hidden_one,
        *out_terms,
        grad_moe_gain,
        head_gain_grads,
    )
    home, grads_got = lax.optimization_barrier((home, grads_got))
    home, attn_grads = lax.optimization_barrier(
        (exchange(home.reshape(te * dp, micro, -1), ("tensor",) + DP), attn_grads)
    )
    output, input_grad, gain_sum, head_gain_grads = deliver(
        my_te, home.reshape(own, -1), home_hot
    )
    output = output.reshape(micro, block, width)
    input_grad = input_grad.reshape(micro, block, width)

    gate_grad, up_grad, down_grad = expert_gradients(pair, grads_kept, grads_got)
    return (
        output,
        input_grad,
        gain_sum[0],
        attn_grads[:, :local],
        attn_grads[:, local : 2 * local],
        attn_grads[:, 2 * local : 3 * local],
        head_gain_grads[0, :head_cut].reshape(heads, head_part),
        head_gain_grads[0, head_cut : 2 * head_cut].reshape(heads, head_part),
        attn_grads[:, 3 * local :].T,
        gain_sum[1],
        gate_grad,
        up_grad,
        down_grad,
    )


def solution(mesh):
    lines = mesh.shape["dp"] // 2
    devices = mesh.devices.reshape(2, lines, mesh.shape["tensor"])
    placed = (
        P(None, DP, None),
        P(None, DP, None),
        P(),
        P(),
        P(None, DP, None),
        P(None, DP, None),
        P(DP),
        P(DP, "tensor"),
        P(DP, "tensor"),
        P(DP, "tensor"),
        P("tensor", DP),
        P("tensor", DP),
        P("tensor", DP),
        P(DP),
        P(None, DP, "tensor"),
        P(None, DP, "tensor"),
        P(None, "tensor", DP),
    )
    return jax.shard_map(
        body,
        mesh=Mesh(devices, DP + ("tensor",)),
        in_specs=placed,
        out_specs=(
            P(None, DP, None),
            P(None, DP, None),
            P(DP),
            P(DP, "tensor"),
            P(DP, "tensor"),
            P(DP, "tensor"),
            P("tensor", DP),
            P("tensor", DP),
            P("tensor", DP),
            P(DP),
            P(None, DP, "tensor"),
            P(None, DP, "tensor"),
            P(None, "tensor", DP),
        ),
        check_vma=False,
    )
```

```python
import jax
import jax.numpy as jnp
from jax import lax
from jax.experimental import pallas as pl
from jax.experimental.pallas import tpu as pltpu
from jax.sharding import Mesh
from jax.sharding import PartitionSpec as P

HEAD = 128
MIB = 1024 * 1024
bf16 = jnp.bfloat16
f32 = jnp.float32

DP = ("pair", "line")
PAIR_TENSOR = ("pair", "tensor")

RANKS = 8

epsilon = 1e-05
rope_base = 10000.0


def rope_tables(position):
    half_dim = HEAD // 2
    frequency = rope_base ** (-(jnp.arange(half_dim, dtype=f32) * 2.0 / HEAD))
    angle = position[:, None] * frequency[None, :]
    cosine = jnp.concatenate([jnp.cos(angle), jnp.cos(angle)], axis=-1)
    sine = jnp.concatenate([jnp.sin(angle), jnp.sin(angle)], axis=-1)
    return (cosine, sine)


def norm_factor(values):
    return lax.rsqrt(jnp.mean(values * values, axis=-1, keepdims=True) + epsilon)


def norm_back(values, factor, gain, gradient):
    gained = gradient * gain
    inner_sum = jnp.sum(gained * values, axis=-1, keepdims=True)
    return factor * gained - values * (factor * factor * factor) * inner_sum / values.shape[-1]


def dot_nn(left_side, right_side):
    return jnp.dot(left_side, right_side, preferred_element_type=f32)


def dot_tn(left_side, right_side):
    return lax.dot_general(
        left_side, right_side, (((0,), (0,)), ((), ())), preferred_element_type=f32
    )


def dot_nt(left_side, right_side):
    return lax.dot_general(
        left_side, right_side, (((1,), (1,)), ((), ())), preferred_element_type=f32
    )


def exchange(value, axis):
    return lax.all_to_all(value, axis, split_axis=0, concat_axis=0, tiled=True)


def swap(value):
    return lax.ppermute(value, "pair", [(0, 1), (1, 0)])


def in_order(first, mine, other, axis=0):
    return jnp.stack([jnp.where(first, mine, other), jnp.where(first, other, mine)], axis=axis)


def turned(values):
    cut = values.reshape(values.shape[:-1] + (2, -1, HEAD))
    return jnp.swapaxes(cut, -3, -2).reshape(values.shape)


def spread(value, axis):
    count = lax.axis_size(axis)
    copies = jnp.broadcast_to(value[None], (count,) + value.shape)
    return exchange(copies, axis)


BLOCK = 512

IN_VMEM = pl.BlockSpec(memory_space=pltpu.VMEM)
IN_HBM = pl.BlockSpec(memory_space=pltpu.HBM)

KEYS = slice(0, 128)
VALUES = slice(128, 256)
QUERIES = slice(256, 288)
Q_BLOCKS = 4

MICRO = 2
HEADS = 2
QUARTERS = 4


def seen(sources, part):
    return slice(0, min(sources, (part + 1) * Q_BLOCKS) * 128)


def masked_scores(query, keys, key_place, query_place, query_start):
    scores = dot_nt(query, keys) * (HEAD ** (-0.5))
    visible = (key_place <= query_place) & (key_place >= query_start)
    return jnp.where(visible, scores, -1e30)


def attention_kernel(packed, key_place, query_place, query_start, mixed, log_total):
    sources = packed.shape[0]
    keys = packed[:, KEYS, :].reshape(sources * 128, HEAD)
    values = packed[:, VALUES, :].reshape(sources * 128, HEAD)
    for part in range(sources // Q_BLOCKS):
        blocks = slice(part * Q_BLOCKS, (part + 1) * Q_BLOCKS)
        rows = slice(part * Q_BLOCKS * 32, (part + 1) * Q_BLOCKS * 32)
        query = packed[blocks, QUERIES, :].reshape(Q_BLOCKS * 32, HEAD)
        past = seen(sources, part)
        scores = masked_scores(
            query, keys[past], key_place[:, past], query_place[rows, :], query_start[rows, :]
        )
        peak = jnp.max(scores, axis=-1, keepdims=True)
        weights = jnp.exp(scores - peak)
        total = jnp.sum(weights, axis=-1, keepdims=True)
        probs = (weights / total).astype(bf16)
        mixed[blocks, :, :] = (
            dot_nn(probs, values[past]).astype(bf16).reshape(Q_BLOCKS, 32, HEAD)
        )
        log_total[rows, :] = peak + jnp.log(total)


def attention_back_kernel(
    packed, key_place, query_place, query_start, log_total, delta_mixed, out, key_sum, value_sum
):
    sources = packed.shape[0]
    keys = packed[:, KEYS, :].reshape(sources * 128, HEAD)
    values = packed[:, VALUES, :].reshape(sources * 128, HEAD)
    scale = HEAD ** (-0.5)
    for part in reversed(range(sources // Q_BLOCKS)):
        blocks = slice(part * Q_BLOCKS, (part + 1) * Q_BLOCKS)
        rows = slice(part * Q_BLOCKS * 32, (part + 1) * Q_BLOCKS * 32)
        query = packed[blocks, QUERIES, :].reshape(Q_BLOCKS * 32, HEAD)
        delta = delta_mixed[blocks, :, :].reshape(Q_BLOCKS * 32, HEAD)
        past = seen(sources, part)
        scores = masked_scores(
            query, keys[past], key_place[:, past], query_place[rows, :], query_start[rows, :]
        )
        probs = jnp.exp(scores - log_total[rows, :])
        delta_probs = dot_nt(delta, values[past])
        inner = jnp.sum(probs * delta_probs, axis=-1, keepdims=True)
        delta_scores = (probs * (delta_probs - inner)).astype(bf16)
        out[blocks, QUERIES, :] = (
            (dot_nn(delta_scores, keys[past]) * scale).astype(bf16).reshape(Q_BLOCKS, 32, HEAD)
        )
        key_term = dot_tn(delta_scores, query)
        value_term = dot_tn(probs.astype(bf16), delta)
        if part == sources // Q_BLOCKS - 1:
            key_sum[...] = key_term
            value_sum[...] = value_term
        else:
            key_sum[past, :] += key_term
            value_sum[past, :] += value_term
    out[:, KEYS, :] = (key_sum[...] * scale).astype(bf16).reshape(sources, 128, HEAD)
    out[:, VALUES, :] = value_sum[...].astype(bf16).reshape(sources, 128, HEAD)


def attention(packed, key_place, query_place, query_start):
    sources = packed.shape[0]
    return pl.pallas_call(
        attention_kernel,
        out_shape=(
            jax.ShapeDtypeStruct((sources, 32, HEAD), bf16),
            jax.ShapeDtypeStruct((sources * 32, 1), f32),
        ),
        compiler_params=pltpu.CompilerParams(vmem_limit_bytes=40 * MIB),
        name="attention",
    )(packed, key_place, query_place, query_start)


def attention_back(packed, key_place, query_place, query_start, log_total, delta_mixed):
    sources = packed.shape[0]
    return pl.pallas_call(
        attention_back_kernel,
        out_shape=jax.ShapeDtypeStruct(packed.shape, bf16),
        scratch_shapes=[
            pltpu.VMEM((sources * 128, HEAD), f32),
            pltpu.VMEM((sources * 128, HEAD), f32),
        ],
        compiler_params=pltpu.CompilerParams(vmem_limit_bytes=40 * MIB),
        name="attention_back",
    )(packed, key_place, query_place, query_start, log_total, delta_mixed)


def order_hot(count, micro, forward):
    part = count // micro
    row = lax.broadcasted_iota(jnp.int32, (count, count), 0)
    column = lax.broadcasted_iota(jnp.int32, (count, count), 1)
    if not forward:
        row, column = column, row
    return jnp.where(column == micro * (row % part) + row // part, 1.0, 0.0).astype(bf16)


def reordered(values, micro, forward):
    return dot_nn(order_hot(values.shape[0], micro, forward), values).astype(bf16)


def half_signs(shape):
    return lax.broadcasted_iota(jnp.int32, shape, 1) < HEAD // 2


def row_sums(values):
    return jnp.sum(values.T, axis=0, keepdims=True)


def as_columns(row):
    return jnp.broadcast_to(row, (HEAD, row.shape[1])).T


def head_lanes(head):
    return slice(head * HEAD, (head + 1) * HEAD)


def pair_index(micro_index, head, quarter):
    return (micro_index * HEADS + head) * QUARTERS + quarter


def project_kernel(tokens, gain, stored, normed, pre, value, squares, weights, semaphore):
    copy = load(stored.at[:, 0:3], weights, semaphore)
    values = tokens[...].astype(f32)
    rows = (values * norm_factor(values) * gain[...]).astype(bf16)
    rows = reordered(rows, MICRO, True)
    normed[...] = rows
    local = value.shape[1]
    copy.wait()
    width = rows.shape[1]
    sums = []
    for k in range(2):
        values = dot_nn(rows, weights[:, k].reshape(width, local))
        pre[:, k * local : (k + 1) * local] = values
        sums.append(row_sums(values * values))
    value[...] = dot_nn(rows, weights[:, 2].reshape(width, local)).astype(bf16)
    squares[...] = jnp.concatenate(sums, axis=0)


def project(tokens, gain, weights):
    count, width = tokens.shape
    lines, _, rows, local = weights.shape
    return pl.pallas_call(
        project_kernel,
        in_specs=[IN_VMEM, IN_VMEM, IN_HBM],
        scratch_shapes=[pltpu.VMEM((lines, 3, rows, local), bf16), pltpu.SemaphoreType.DMA],
        out_specs=[IN_VMEM] * 4,
        out_shape=(
            jax.ShapeDtypeStruct((count, width), bf16),
            jax.ShapeDtypeStruct((count, 2 * local), f32),
            jax.ShapeDtypeStruct((count, local), bf16),
            jax.ShapeDtypeStruct((2, count), f32),
        ),
        compiler_params=pltpu.CompilerParams(vmem_limit_bytes=60 * MIB),
        name="project",
    )(tokens, gain, weights)


def pack_kernel(squares, pre, value, cosine, sine, scales, packed, factors):
    count, local = value.shape
    block = count // MICRO
    total = summed(squares)
    factor = lax.rsqrt(total / (local * squares.shape[0]) + epsilon)
    low = half_signs((count, HEAD))
    signed_sine = jnp.where(low, -sine[...], sine[...])
    columns = [as_columns(factor[k : k + 1]) for k in range(2)]
    factors[...] = jnp.concatenate(columns, axis=1)
    for head in range(HEADS):
        turned_heads = []
        for k in range(2):
            lanes = slice(k * local + head * HEAD, k * local + (head + 1) * HEAD)
            values = pre[:, lanes] * columns[k] * scales[:, lanes]
            rotated = values * cosine[...] + pltpu.roll(values, HEAD // 2, 1) * signed_sine
            turned_heads.append(rotated.astype(bf16))
        query, key = turned_heads
        for m in range(MICRO):
            rows = slice(m * block, (m + 1) * block)
            for quarter in range(QUARTERS):
                index = pair_index(m, head, quarter)
                start = m * block + quarter * block // QUARTERS
                packed[index, KEYS, :] = key[rows]
                packed[index, VALUES, :] = value[rows, head_lanes(head)]
                packed[index, QUERIES, :] = query[start : start + block // QUARTERS]


def pack(squares, pre, value, cosine, sine, scales):
    count, local = value.shape
    rows = (2 * QUARTERS + 1) * (count // MICRO // QUARTERS)
    return pl.pallas_call(
        pack_kernel,
        in_specs=[IN_VMEM] * 6,
        out_specs=[IN_VMEM] * 2,
        out_shape=(
            jax.ShapeDtypeStruct((MICRO * HEADS * QUARTERS, rows, HEAD), bf16),
            jax.ShapeDtypeStruct((count, 2 * HEAD), f32),
        ),
        name="pack",
    )(squares, pre, value, cosine, sine, scales)


def from_quarters(arrived, head):
    return jnp.concatenate(
        [
            arrived[pair_index(m, head, quarter)]
            for m in range(MICRO)
            for quarter in range(QUARTERS)
        ],
        axis=0,
    )


def project_out_kernel(arrived, stored, mixed, out, weights, semaphore):
    copy = load(stored.at[:, 3], weights, semaphore)
    rows = jnp.concatenate([from_quarters(arrived, head) for head in range(HEADS)], axis=1)
    rows = reordered(rows, MICRO, False)
    mixed[...] = rows
    copy.wait()
    out[...] = dot_nt(rows, weights[...].reshape(out.shape[1], rows.shape[1])).astype(bf16)


def project_out(arrived, weights):
    lines, _, rows, local = weights.shape
    count = arrived.shape[0] * arrived.shape[1] // HEADS
    return pl.pallas_call(
        project_out_kernel,
        in_specs=[IN_VMEM, IN_HBM],
        scratch_shapes=[pltpu.VMEM((lines, rows, local), bf16), pltpu.SemaphoreType.DMA],
        out_specs=[IN_VMEM] * 2,
        out_shape=(
            jax.ShapeDtypeStruct((count, local), bf16),
            jax.ShapeDtypeStruct((count, lines * rows), bf16),
        ),
        compiler_params=pltpu.CompilerParams(vmem_limit_bytes=60 * MIB),
        name="project_out",
    )(arrived, weights)


def project_out_back_kernel(delta, stored, out, weights, semaphore):
    load(stored.at[:, 3], weights, semaphore).wait()
    rows = dot_nn(delta[...], weights[...].reshape(delta.shape[1], -1)).astype(bf16)
    rows = reordered(rows, MICRO, True)
    step = out.shape[1]
    block = rows.shape[0] // MICRO
    for m in range(MICRO):
        for head in range(HEADS):
            for quarter in range(QUARTERS):
                start = m * block + quarter * step
                out[pair_index(m, head, quarter)] = rows[start : start + step, head_lanes(head)]


def project_out_back(delta, weights):
    count = delta.shape[0]
    lines, _, rows, local = weights.shape
    devices = MICRO * HEADS * QUARTERS
    return pl.pallas_call(
        project_out_back_kernel,
        in_specs=[IN_VMEM, IN_HBM],
        scratch_shapes=[
            pltpu.VMEM((lines, rows, local), bf16),
            pltpu.SemaphoreType.DMA,
        ],
        out_specs=IN_VMEM,
        out_shape=jax.ShapeDtypeStruct((devices, count * HEADS // devices, HEAD), bf16),
        compiler_params=pltpu.CompilerParams(vmem_limit_bytes=60 * MIB),
        name="project_out_back",
    )(delta, weights)


def unpack_kernel(
    arrived, pre, factors, cosine, sine, scales, weighted, delta_value, inner, gain_grads
):
    count, local = delta_value.shape
    low = half_signs((count, HEAD))
    signs = jnp.where(low, 1.0, -1.0)
    products = [None, None]
    for head in range(HEADS):
        sums = []
        for rows in (KEYS, VALUES):
            parts = []
            for m in range(MICRO):
                total = arrived[pair_index(m, head, 0), rows, :].astype(f32)
                for quarter in range(1, QUARTERS):
                    total = total + arrived[pair_index(m, head, quarter), rows, :].astype(f32)
                parts.append(total)
            sums.append(jnp.concatenate(parts, axis=0))
        delta_key, value = sums
        delta_value[:, head_lanes(head)] = value.astype(bf16)
        delta_query = jnp.concatenate(
            [
                arrived[pair_index(m, head, quarter), QUERIES, :]
                for m in range(MICRO)
                for quarter in range(QUARTERS)
            ],
            axis=0,
        ).astype(f32)
        for k, gradient in ((0, delta_query), (1, delta_key)):
            lanes = slice(k * local + head * HEAD, k * local + (head + 1) * HEAD)
            scaled = pltpu.roll(gradient * sine[...], HEAD // 2, 1) * signs
            normed_gradient = gradient * cosine[...] + scaled
            values = pre[:, lanes]
            gain_grads[:, lanes] = jnp.sum(
                normed_gradient * values * factors[:, head_lanes(k)], axis=0, keepdims=True
            )
            gained = normed_gradient * scales[:, lanes]
            weighted[:, lanes] = gained
            product = gained * values
            products[k] = product if head == 0 else products[k] + product
    inner[...] = jnp.concatenate([row_sums(product) for product in products], axis=0)


def unpack(arrived, pre, factors, cosine, sine, scales):
    count, lanes = pre.shape
    return pl.pallas_call(
        unpack_kernel,
        in_specs=[IN_VMEM] * 6,
        out_specs=[IN_VMEM] * 4,
        out_shape=(
            jax.ShapeDtypeStruct((count, lanes), f32),
            jax.ShapeDtypeStruct((count, lanes // 2), bf16),
            jax.ShapeDtypeStruct((2, count), f32),
            jax.ShapeDtypeStruct((1, lanes), f32),
        ),
        name="unpack",
    )(arrived, pre, factors, cosine, sine, scales)


def project_back_kernel(
    inner, weighted, pre, factors, value, stored, delta_pre, out, weights, semaphore
):
    local = value.shape[1]
    copy = load(stored.at[:, 0:3], weights, semaphore)
    total = summed(inner) / (local * inner.shape[0])
    for k in range(2):
        factor = factors[:, head_lanes(k)]
        column = factor * factor * factor * as_columns(total[k : k + 1])
        for head in range(HEADS):
            lanes = slice(k * local + head * HEAD, k * local + (head + 1) * HEAD)
            delta_pre[:, lanes] = (factor * weighted[:, lanes] - pre[:, lanes] * column).astype(
                bf16
            )
    delta_pre[:, 2 * local :] = value[...]
    rows = reordered(delta_pre[...], MICRO, False)
    copy.wait()
    lines, _, step, _ = weights.shape
    for line in range(lines):
        chunk = jnp.concatenate([weights[line, k] for k in range(3)], axis=1)
        out[:, line * step : (line + 1) * step] = dot_nt(rows, chunk).astype(bf16)


def project_back(inner, weighted, pre, factors, value, weights):
    count = value.shape[0]
    lines, _, rows, local = weights.shape
    return pl.pallas_call(
        project_back_kernel,
        in_specs=[IN_VMEM] * 5 + [IN_HBM],
        scratch_shapes=[
            pltpu.VMEM((lines, 3, rows, local), bf16),
            pltpu.SemaphoreType.DMA,
        ],
        out_specs=[IN_VMEM] * 2,
        out_shape=(
            jax.ShapeDtypeStruct((count, 3 * local), bf16),
            jax.ShapeDtypeStruct((count, lines * rows), bf16),
        ),
        compiler_params=pltpu.CompilerParams(vmem_limit_bytes=60 * MIB),
        name="project_back",
    )(inner, weighted, pre, factors, value, weights)


def load(source, target, semaphore):
    copy = pltpu.make_async_copy(source, target, semaphore)
    copy.start()
    return copy


def attention_grads_kernel(normed, delta_pre, delta_attn, mixed, out):
    lines = out.shape[0]
    pre_width = delta_pre.shape[1]
    for line in range(lines):
        lanes = slice(2 * line * HEAD, 2 * (line + 1) * HEAD)
        out[line, :, :pre_width] = dot_tn(normed[:, lanes], delta_pre[...]).astype(bf16)
        out[line, :, pre_width:] = dot_tn(delta_attn[:, lanes], mixed[...]).astype(bf16)


def attention_grads(normed, delta_pre, delta_attn, mixed):
    lines = normed.shape[1] // HEAD // 2
    return pl.pallas_call(
        attention_grads_kernel,
        out_shape=jax.ShapeDtypeStruct(
            (lines, 2 * HEAD, delta_pre.shape[1] + mixed.shape[1]), bf16
        ),
        compiler_params=pltpu.CompilerParams(vmem_limit_bytes=24 * MIB),
        name="attention_grads",
    )(normed, delta_pre, delta_attn, mixed)


def stack_attention_kernel(w_query, w_key, w_value, w_out, out):
    out[0] = w_query[...]
    out[1] = w_key[...]
    out[2] = w_value[...]
    out[3] = w_out[...].T


def stack_attention(w_query, w_key, w_value, w_out):
    return pl.pallas_call(
        stack_attention_kernel,
        out_shape=jax.ShapeDtypeStruct((4,) + w_query.shape, bf16),
        name="stack_attention",
    )(w_query, w_key, w_value, w_out)


def stack_experts_kernel(pair, w_gate, w_up, w_down, kept, sent):
    half = w_gate.shape[0] // 2
    each = BLOCK // HEAD
    for out, which in ((kept, pair[0]), (sent, 1 - pair[0])):
        for expert in range(half):
            for index, stored in enumerate((w_gate, w_up, w_down)):
                start = expert // each * 3 * BLOCK + index * BLOCK + expert % each * HEAD
                value = stored[which * half + expert]
                out[:, start : start + HEAD] = value.T if stored is w_down else value


def stack_experts(pair, w_gate, w_up, w_down):
    count, rows, hidden = w_gate.shape
    shape = jax.ShapeDtypeStruct((rows, 3 * count * hidden // 2), bf16)
    return pl.pallas_call(
        stack_experts_kernel,
        in_specs=[pl.BlockSpec(memory_space=pltpu.SMEM)]
        + [pl.BlockSpec(memory_space=pltpu.VMEM)] * 3,
        out_shape=(shape, shape),
        compiler_params=pltpu.CompilerParams(vmem_limit_bytes=24 * MIB),
        name="stack_experts",
    )(pair.reshape(1), w_gate, w_up, w_down)


def experts_kernel(my_rank, arrived, upstream, gates, weights, *refs):
    (
        out_kept,
        out_sent,
        delta_in,
        grads,
        held,
        hidden_all,
        deltas_all,
        grads_out,
        out_all,
        rows,
        in_sem,
        out_sem,
    ) = refs
    steps = held.shape[0]
    width = upstream.shape[1]
    lines = grads.shape[0]
    lane_part = width // lines
    part = out_kept.shape[2]
    loads = [
        pltpu.make_async_copy(
            weights.at[:, pl.ds(c * 3 * BLOCK, 3 * BLOCK)], held.at[c], in_sem.at[c]
        )
        for c in range(steps)
    ]
    for load in loads:
        load.start()
    for k in range(arrived.shape[0]):
        rows[k * part : (k + 1) * part, :] = from_blocks(arrived.at[k])
    stores = []
    for c in range(steps):
        loads[c].wait()
        gate_up = dot_nn(rows[...], held[c, :, 0 : 2 * BLOCK])
        gate_h, up_h = gate_up[:, :BLOCK], gate_up[:, BLOCK:]
        delta_hidden = dot_nn(upstream[...], held[c, :, 2 * BLOCK : 3 * BLOCK])
        share = jnp.concatenate(
            [
                jnp.broadcast_to(gates[:, e : e + 1], (gates.shape[0], HEAD))
                for e in range(c * BLOCK // HEAD, (c + 1) * BLOCK // HEAD)
            ],
            axis=1,
        )
        sigmoid_gate = 1.0 / (1.0 + jnp.exp(-gate_h))
        active = gate_h * sigmoid_gate
        hidden = (active * up_h * share).astype(bf16)
        delta_hidden = delta_hidden * share
        delta_gate = (
            delta_hidden * up_h * sigmoid_gate * (1.0 + gate_h * (1.0 - sigmoid_gate))
        ).astype(bf16)
        delta_up = (delta_hidden * active).astype(bf16)
        start = 2 * c * BLOCK
        hidden_all[:, c * BLOCK : (c + 1) * BLOCK] = hidden
        deltas_all[:, start : start + BLOCK] = delta_gate
        deltas_all[:, start + BLOCK : start + 2 * BLOCK] = delta_up
        deltas = deltas_all[:, start : start + 2 * BLOCK]
        slot = c % 2
        if c >= 2:
            stores[c - 2].wait()
        for n in range(lines):
            lanes = slice(n * lane_part, (n + 1) * lane_part)
            grads_out[slot, n, 0 : 2 * BLOCK, :] = dot_tn(deltas, rows[:, lanes]).astype(bf16)
            grads_out[slot, n, 2 * BLOCK :, :] = dot_tn(hidden, upstream[:, lanes]).astype(bf16)
        store = pltpu.make_async_copy(
            grads_out.at[slot], grads.at[:, pl.ds(c * 3 * BLOCK, 3 * BLOCK), :], out_sem.at[slot]
        )
        store.start()
        stores.append(store)
    for n in range(lines):
        lanes = slice(n * lane_part, (n + 1) * lane_part)
        gate_up = jnp.concatenate(
            [held[c, lanes, 0 : 2 * BLOCK] for c in range(steps)], axis=1
        )
        produced = dot_nt(deltas_all[...], gate_up).astype(bf16)
        for k in range(2 * RANKS):
            for b in range(lane_part // HEAD):
                delta_in[k, n * (lane_part // HEAD) + b] = produced[
                    k * part : (k + 1) * part, b * HEAD : (b + 1) * HEAD
                ]
        down = jnp.concatenate(
            [held[c, lanes, 2 * BLOCK : 3 * BLOCK] for c in range(steps)], axis=1
        )
        produced = dot_nt(hidden_all[...], down).astype(bf16)
        out_all[:, :, lanes] = produced.reshape(2 * RANKS, part, lane_part)
    high = my_rank[0] // (RANKS // 2)
    for p in range(2):
        for q in range(RANKS // 2):
            out_kept[q, p] = out_all[p * RANKS + high * (RANKS // 2) + q]
            out_sent[q, p] = out_all[p * RANKS + (1 - high) * (RANKS // 2) + q]
    for store in stores[-2:]:
        store.wait()


def experts(my_rank, arrived, upstream, gates, weights, lines):
    count, width = upstream.shape
    part = count // RANKS // 2
    steps = weights.shape[1] // (3 * BLOCK)
    in_vmem = pl.BlockSpec(memory_space=pltpu.VMEM)
    in_hbm = pl.BlockSpec(memory_space=pl.ANY)
    return pl.pallas_call(
        experts_kernel,
        in_specs=[pl.BlockSpec(memory_space=pltpu.SMEM), in_vmem, in_vmem, in_vmem, in_hbm],
        out_specs=[in_vmem, in_vmem, in_vmem, in_hbm],
        out_shape=(
            *[jax.ShapeDtypeStruct((RANKS // 2, 2, part, width), bf16)] * 2,
            jax.ShapeDtypeStruct(arrived.shape, bf16),
            jax.ShapeDtypeStruct((lines, weights.shape[1], width // lines), bf16),
        ),
        scratch_shapes=[
            pltpu.VMEM((steps, width, 3 * BLOCK), bf16),
            pltpu.VMEM((count, steps * BLOCK), bf16),
            pltpu.VMEM((count, 2 * steps * BLOCK), bf16),
            pltpu.VMEM((2, lines, 3 * BLOCK, width // lines), bf16),
            pltpu.VMEM((2 * RANKS, part, width), bf16),
            pltpu.VMEM((count, width), bf16),
            pltpu.SemaphoreType.DMA((steps,)),
            pltpu.SemaphoreType.DMA((2,)),
        ],
        compiler_params=pltpu.CompilerParams(vmem_limit_bytes=56 * MIB),
        name="experts",
    )(my_rank.reshape(1), arrived, upstream, gates, weights)


def expert_gradients_kernel(pair, kept, got, gate_grad, up_grad, down_grad):
    half = gate_grad.shape[0] // 2
    each = BLOCK // HEAD
    for stored, which in ((kept, pair[0]), (got, 1 - pair[0])):
        for expert in range(half):
            for index, out in enumerate((gate_grad, up_grad, down_grad)):
                start = expert // each * 3 * BLOCK + index * BLOCK + expert % each * HEAD
                value = stored[start : start + HEAD].astype(f32)
                out[which * half + expert] = value if out is down_grad else value.T


def expert_gradients(pair, kept, got):
    count = 2 * kept.shape[0] // 3 // HEAD
    in_vmem = pl.BlockSpec(memory_space=pltpu.VMEM)
    shape = jax.ShapeDtypeStruct((count, kept.shape[1], HEAD), f32)
    return pl.pallas_call(
        expert_gradients_kernel,
        in_specs=[pl.BlockSpec(memory_space=pltpu.SMEM), in_vmem, in_vmem],
        out_shape=(shape, shape, shape),
        compiler_params=pltpu.CompilerParams(vmem_limit_bytes=24 * MIB),
        name="expert_gradients",
    )(pair.reshape(1), kept, got)


def summed(terms):
    total = terms[0].astype(f32)
    for k in range(1, terms.shape[0]):
        total = total + terms[k].astype(f32)
    return total


def put_blocks(out, rows):
    for block in range(out.shape[0]):
        out[block] = rows[:, block * HEAD : (block + 1) * HEAD]


def from_blocks(blocks):
    return jnp.concatenate([blocks[k] for k in range(blocks.shape[0])], axis=1)


def lane_blocks(width, forward):
    lines = width // HEAD // 2
    moves = [(p * lines + n, n * 2 + p) for p in range(2) for n in range(lines)]
    return moves if forward else [(b, a) for a, b in moves]


def move_lanes(values, forward):
    moves = sorted((b, a) for a, b in lane_blocks(values.shape[-1], forward))
    return jnp.concatenate([values[:, a * HEAD : (a + 1) * HEAD] for _, a in moves], axis=1)


def deal_kernel(
    where, places, stored_tokens, stored_cotangent, gains, out, tokens, cotangent, semaphores
):
    copies = [
        load(stored_tokens, tokens, semaphores.at[0]),
        load(stored_cotangent, cotangent, semaphores.at[1]),
    ]
    count, width = tokens.shape
    rows, block = places.shape
    given = places[...] - where[0] * block
    mine = (given >= 0) & (given < block)
    before = lax.broadcasted_iota(jnp.int32, (block, block), 0) < lax.broadcasted_iota(
        jnp.int32, (block, block), 1
    )
    rank = dot_nn(
        jnp.where(mine, 1.0, 0.0).astype(bf16), jnp.where(before, 1.0, 0.0).astype(bf16)
    ).astype(jnp.int32)
    hit = mine & (rank == where[1])
    order = jnp.sum(jnp.where(hit, given, 0), axis=1, keepdims=True)
    micro = lax.broadcasted_iota(jnp.int32, (rows, 1), 0) % (count // block)
    hot = order + micro * block == lax.broadcasted_iota(jnp.int32, (rows, count), 1)
    hot = jnp.where(hot, 1.0, 0.0).astype(bf16)
    copies[0].wait()
    token_rows = move_lanes(dot_nn(hot, tokens[...]).astype(bf16), True)
    copies[1].wait()
    gradient = move_lanes(dot_nn(hot, cotangent[...]).astype(bf16), True)
    odd = lax.broadcasted_iota(jnp.int32, (rows, gains.shape[1]), 0) % 2 == 1
    values = gains[...].astype(f32)
    beside = jnp.where(odd, values[1:2], values[0:1]).astype(bf16)
    partner = jnp.concatenate([gradient[rows // 2 :], gradient[: rows // 2]], axis=0)
    sent = jnp.concatenate([token_rows, gradient, partner, beside], axis=1)
    for chunk in range(out.shape[0]):
        out[chunk] = sent[chunk * out.shape[1] : (chunk + 1) * out.shape[1]]


def deal(where, places, tokens, cotangent, gains):
    width = tokens.shape[1]
    return pl.pallas_call(
        deal_kernel,
        in_specs=[pl.BlockSpec(memory_space=pltpu.SMEM), IN_VMEM, IN_HBM, IN_HBM, IN_VMEM],
        scratch_shapes=[
            pltpu.VMEM(tokens.shape, bf16),
            pltpu.VMEM(cotangent.shape, bf16),
            pltpu.SemaphoreType.DMA((2,)),
        ],
        out_shape=jax.ShapeDtypeStruct(
            (places.shape[0] // MICRO, MICRO, 3 * width + gains.shape[1]), bf16
        ),
        compiler_params=pltpu.CompilerParams(vmem_limit_bytes=60 * MIB),
        name="deal",
    )(where, places, tokens, cotangent, gains)


def before_experts_kernel(terms, tokens, gain, hidden_one, factor, moe_in):
    hidden = tokens[...].astype(f32) + summed(terms)
    scale = norm_factor(hidden)
    hidden_one[...] = hidden
    factor[...] = scale
    rows = (hidden * scale * gain[...]).astype(bf16)
    for k in range(moe_in.shape[0]):
        put_blocks(moe_in.at[k], rows)


def before_experts(terms, tokens, gain):
    rows, width = tokens.shape
    return pl.pallas_call(
        before_experts_kernel,
        in_specs=[IN_VMEM] * 3,
        out_specs=[IN_VMEM] * 3,
        out_shape=(
            jax.ShapeDtypeStruct((rows, width), f32),
            jax.ShapeDtypeStruct((rows, 1), f32),
            jax.ShapeDtypeStruct((2 * RANKS, width // HEAD, rows, HEAD), bf16),
        ),
        name="before_experts",
    )(terms, tokens, gain)


def after_experts_kernel(
    terms, hidden_one, factor, gain, upstream, delta_one, delta_attn, gain_grad
):
    gradient = from_blocks(summed(terms))
    hidden = hidden_one[...]
    gain_grad[...] = jnp.sum(gradient * hidden * factor[...], axis=0, keepdims=True)
    delta = upstream[...].astype(f32) + norm_back(hidden, factor[...], gain[...], gradient)
    delta_one[...] = delta
    for k in range(delta_attn.shape[0]):
        delta_attn[k] = delta.astype(bf16)


def after_experts(terms, hidden_one, factor, gain, upstream):
    rows, width = upstream.shape
    return pl.pallas_call(
        after_experts_kernel,
        in_specs=[IN_VMEM] * 5,
        out_specs=[IN_VMEM] * 3,
        out_shape=(
            jax.ShapeDtypeStruct((rows, width), f32),
            jax.ShapeDtypeStruct((RANKS, rows, width), bf16),
            jax.ShapeDtypeStruct((1, width), f32),
        ),
        name="after_experts",
    )(terms, hidden_one, factor, gain, upstream)


def halve_kernel(bit, kept, got, mine, sent):
    half = mine.shape[0]
    for out, start in ((mine, bit[0] * half), (sent, (1 - bit[0]) * half)):
        for k in range(half):
            total = kept[start + k].astype(f32) + got[start + k].astype(f32)
            out[k] = total.astype(out.dtype)


def halve(bit, kept, got):
    shape = (kept.shape[0] // 2,) + kept.shape[1:]
    in_vmem = pl.BlockSpec(memory_space=pltpu.VMEM)
    return pl.pallas_call(
        halve_kernel,
        in_specs=[pl.BlockSpec(memory_space=pltpu.SMEM), in_vmem, in_vmem],
        out_specs=[IN_VMEM] * 2,
        out_shape=(jax.ShapeDtypeStruct(shape, f32), jax.ShapeDtypeStruct(shape, bf16)),
        compiler_params=pltpu.CompilerParams(vmem_limit_bytes=24 * MIB),
        name="halve",
    )(bit.reshape(1), kept, got)


def quarter_terms_kernel(bits, kept, got, mine, other, across_mine, across_other):
    for out, y, p in (
        (mine, bits[0], bits[1]),
        (other, bits[0], 1 - bits[1]),
        (across_mine, 1 - bits[0], bits[1]),
        (across_other, 1 - bits[0], 1 - bits[1]),
    ):
        out[...] = (kept[y, p].astype(f32) + got[y, p].astype(f32)).astype(out.dtype)


def quarter_terms(y, pair, kept, got):
    rows, width = kept.shape[2:]
    in_vmem = pl.BlockSpec(memory_space=pltpu.VMEM)
    return pl.pallas_call(
        quarter_terms_kernel,
        in_specs=[pl.BlockSpec(memory_space=pltpu.SMEM), in_vmem, in_vmem],
        out_specs=[IN_VMEM] * 4,
        out_shape=(
            jax.ShapeDtypeStruct((rows, width), f32),
            *[jax.ShapeDtypeStruct((rows, width), bf16)] * 3,
        ),
        name="quarter_terms",
    )(jnp.stack([y, pair]), kept, got)


def finish_kernel(
    terms,
    tokens,
    gain,
    delta_one,
    hidden_one,
    out_mine,
    out_second,
    out_third,
    out_fourth,
    moe_gain_grad,
    head_gain_grads,
    home,
):
    width = tokens.shape[1]
    values = tokens[...].astype(f32)
    gradient = summed(terms)
    factor = norm_factor(values)
    gain_grad = jnp.sum(gradient * values * factor, axis=0, keepdims=True)
    moe_out = out_mine[...]
    for term in (out_second, out_third, out_fourth):
        moe_out = moe_out + term[...].astype(f32)
    output = move_lanes((hidden_one[...] + moe_out).astype(bf16), False)
    input_grad = delta_one[...] + norm_back(values, factor, gain[...], gradient)
    input_grad = move_lanes(input_grad.astype(bf16), False)
    rows = []
    for moved, _ in sorted(lane_blocks(width, False), key=lambda move: move[1]):
        lanes = slice(moved * HEAD, (moved + 1) * HEAD)
        rows.append(gain_grad[:, lanes])
        rows.append(moe_gain_grad[:, lanes])
    gains = jnp.concatenate(rows, axis=0).astype(bf16)
    sent = jnp.concatenate(
        [output, input_grad, gains, head_gain_grads[...].astype(bf16)], axis=1
    )
    micro = home.shape[2]
    for source in range(home.shape[1]):
        piece = sent[source * micro : (source + 1) * micro]
        for k in range(home.shape[0]):
            home[k, source] = piece


def finish(micro, terms, tokens, *others):
    rows, width = tokens.shape
    shape = (RANKS, rows // micro, micro, 2 * width + 2 * HEAD)
    return pl.pallas_call(
        finish_kernel,
        in_specs=[IN_VMEM] * 11,
        out_specs=IN_VMEM,
        out_shape=jax.ShapeDtypeStruct(shape, bf16),
        name="finish",
    )(terms, tokens, *others)


def deliver_kernel(rank, arrived, hot, output, input_grad, gains, head_gains):
    count, width = output.shape
    rows = arrived[...].reshape(count, arrived.shape[2])
    output[...] = dot_nn(hot[...], rows[:, :width]).astype(bf16)
    input_grad[...] = dot_nn(hot[...], rows[:, width : 2 * width]).astype(bf16)
    terms = rows[:, 2 * width : 2 * width + HEAD].astype(f32)
    odd = lax.broadcasted_iota(jnp.int32, terms.shape, 0) % 2
    gains[...] = jnp.concatenate(
        [
            jnp.sum(jnp.where(odd == 0, terms, 0.0), axis=0, keepdims=True),
            jnp.sum(jnp.where(odd == 1, terms, 0.0), axis=0, keepdims=True),
        ],
        axis=0,
    )
    terms = rows[:, 2 * width + HEAD :].astype(f32)
    sender = lax.broadcasted_iota(jnp.int32, terms.shape, 0) // (count // RANKS)
    head_gains[...] = jnp.sum(jnp.where(sender == rank[0], terms, 0.0), axis=0, keepdims=True)


def deliver(rank, rows, hot):
    count, lanes = rows.shape[0] * rows.shape[1], rows.shape[2]
    in_vmem = pl.BlockSpec(memory_space=pltpu.VMEM)
    shape = jax.ShapeDtypeStruct((count, lanes // 2 - HEAD), bf16)
    return pl.pallas_call(
        deliver_kernel,
        in_specs=[pl.BlockSpec(memory_space=pltpu.SMEM), in_vmem, in_vmem],
        out_shape=(
            shape,
            shape,
            jax.ShapeDtypeStruct((2, HEAD), f32),
            jax.ShapeDtypeStruct((1, HEAD), f32),
        ),
        compiler_params=pltpu.CompilerParams(vmem_limit_bytes=24 * MIB),
        name="deliver",
    )(rank.reshape(1), rows, hot)


def body(
    tokens,
    cotangent,
    pack_perm,
    lengths,
    routes,
    gates,
    attn_gain,
    w_query,
    w_key,
    w_value,
    query_gain,
    key_gain,
    w_out,
    moe_gain,
    w_gate,
    w_up,
    w_down,
):
    pair = lax.axis_index("pair")
    first = pair == 0
    lines = lax.axis_size("line")
    dp = 2 * lines
    te = lax.axis_size("tensor")
    me = lax.axis_index(DP)
    my_te = lax.axis_index("tensor")
    micro, block, width = tokens.shape
    ranks = block // dp
    own = micro * block
    part = own // te
    local = w_query.shape[1]
    heads = local // HEAD
    head_part = HEAD // dp
    quarters = dp // (micro * heads)
    expert_count = w_gate.shape[0]

    attn_local = stack_attention(w_query, w_key, w_value, w_out)
    moe_kept, moe_sent = stack_experts(pair, w_gate, w_up, w_down)

    blocks = pack_perm.reshape(micro, dp, block)
    root = blocks // block
    earlier = jnp.arange(block)[None, :] < jnp.arange(block)[:, None]
    rank = jnp.sum(
        ((root[:, :, :, None] == root[:, :, None, :]) & earlier).astype(jnp.int32), axis=3
    )
    from_me = (root == me)[:, :, None, :] & (
        rank[:, :, None, :] == jnp.arange(ranks, dtype=jnp.int32)[None, None, :, None]
    )
    given = jnp.sum(jnp.where(from_me, (blocks - me * block)[:, :, None, :], 0), axis=3)
    given = given + (jnp.arange(micro, dtype=jnp.int32) * block)[:, None, None]
    row_index = jnp.arange(own, dtype=jnp.int32)
    home_order = given.transpose(2, 1, 0).reshape(own)
    home_hot = (row_index[:, None] == home_order[None, :]).astype(bf16)
    slot = rank * dp + root
    slot_hot = slot[:, :, None, :] == jnp.arange(block, dtype=jnp.int32)[None, None, :, None]
    place_in = jnp.sum(
        jnp.where(slot_hot, jnp.arange(block, dtype=jnp.int32)[None, None, None, :], 0), axis=3
    )
    place_of = place_in + (jnp.arange(dp, dtype=jnp.int32) * block)[None, :, None]

    head_cut = heads * head_part
    head_gains = jnp.concatenate(
        [
            query_gain.reshape(1, head_cut),
            key_gain.reshape(1, head_cut),
            jnp.zeros((1, block - 2 * head_cut), bf16),
        ],
        axis=1,
    )
    gains = jnp.concatenate(
        [
            jnp.concatenate([attn_gain[None], head_gains], axis=1),
            jnp.concatenate([moe_gain[None], head_gains], axis=1),
        ],
        axis=0,
    )
    dealt = deal(
        jnp.stack([me, my_te]),
        blocks.transpose(1, 0, 2).reshape(part, block),
        tokens.reshape(own, width),
        cotangent.reshape(own, width),
        gains,
    )
    attn_local = in_order(first, attn_local, swap(attn_local), 1).reshape(4, 2 * block, local)
    attn_local = lax.optimization_barrier((attn_local, dealt))[0]
    attn_w = lax.all_gather(attn_local, "line", axis=0)
    dealt = exchange(dealt, DP).reshape(part, -1)
    part_tokens = dealt[:, :width]
    part_cotangent = dealt[:, width : 2 * width]
    gains = dealt[:, 3 * width :].reshape(dp, micro, 2 * block)
    attn_gain_f = turned(gains[:, 0, :block].reshape(1, width)).astype(f32)
    moe_gain_f = turned(gains[:, 1, :block].reshape(1, width)).astype(f32)

    def head_gain(cut):
        return cut.reshape(dp, heads, head_part).transpose(1, 0, 2).reshape(local).astype(f32)

    query_scale = head_gain(gains[:, 0, block : block + head_cut])
    key_scale = head_gain(gains[:, 0, block + head_cut : block + 2 * head_cut])
    own_tokens = spread(part_tokens, "tensor").reshape(own, width)

    pair_cotangent = in_order(first, part_cotangent, dealt[:, 2 * width : 3 * width])
    pair_cotangent = pair_cotangent.reshape(2 * part, width)
    pair_cotangent = lax.all_gather(pair_cotangent, "tensor", axis=0, tiled=True)
    pair_cotangent = pair_cotangent.reshape(te, 2, part, width).transpose(1, 0, 2, 3)
    pair_cotangent = pair_cotangent.reshape(2 * own, width)

    seq_ends = jnp.cumsum(lengths, axis=1)
    seq_starts = seq_ends - lengths

    def start_of(place, ends, starts):
        inside = (place[..., None] >= starts) & (place[..., None] < ends)
        return jnp.sum(jnp.where(inside, starts, 0), axis=-1)

    own_place = lax.dynamic_index_in_dim(place_of, me, axis=1, keepdims=False)
    own_start = start_of(own_place, seq_ends[:, None, :], seq_starts[:, None, :])
    position = (own_place - own_start).astype(f32)
    cosine, sine = rope_tables(position.reshape(own))
    pair_micro = me // (heads * quarters)
    quarter = me % quarters
    key_place = lax.dynamic_index_in_dim(place_of, pair_micro, axis=0, keepdims=False)
    query_place = lax.dynamic_slice_in_dim(
        key_place, quarter * (block // quarters), block // quarters, axis=1
    ).reshape(-1, 1)
    pair_ends = lax.dynamic_index_in_dim(seq_ends, pair_micro, axis=0)
    pair_starts = lax.dynamic_index_in_dim(seq_starts, pair_micro, axis=0)
    query_start = start_of(query_place, pair_ends[None], pair_starts[None])
    key_place = key_place.reshape(1, -1)

    hot = routes[..., None] == jnp.arange(expert_count, dtype=jnp.int32)
    dense = jnp.sum(jnp.where(hot, gates[..., None], 0.0), axis=2)
    own_slot_hot = lax.dynamic_index_in_dim(slot_hot, me, axis=1, keepdims=False)
    share = jnp.einsum(
        "msj,mje->mse", own_slot_hot.astype(f32), dense, precision=lax.Precision.HIGHEST
    )
    share = share.reshape(micro, ranks, dp, expert_count).transpose(1, 2, 0, 3)
    share = share.reshape(own, expert_count)
    scales = jnp.concatenate([query_scale, key_scale])[None]
    own_tokens, cosine, sine, scales, key_place, query_place, query_start = (
        lax.optimization_barrier(
            (own_tokens, cosine, sine, scales, key_place, query_place, query_start)
        )
    )
    normed_b, pre, value_b, squares = project(own_tokens, attn_gain_f, attn_w)
    moe_sent, share, _ = lax.optimization_barrier((moe_sent, share, squares))
    moe_got, share_got = swap(moe_sent), swap(share)
    sent, factors = pack(spread(squares, "tensor"), pre, value_b, cosine, sine, scales)
    moe_local = in_order(first, moe_kept, moe_got).reshape(2 * block, -1)
    share = in_order(first, share, share_got).reshape(2 * own, expert_count)
    share = lax.dynamic_slice_in_dim(share, pair * (expert_count // 2), expert_count // 2, axis=1)
    packed = exchange(sent, DP)
    moe_local = lax.optimization_barrier((moe_local, packed))[0]
    moe_w = lax.all_gather(moe_local, "line", axis=0, tiled=True)
    pair_mixed, log_total = attention(packed, key_place, query_place, query_start)
    mixed_b, attn_out = project_out(exchange(pair_mixed, DP), attn_w)

    def terms_of(value):
        return exchange(value.reshape(te, part, width), "tensor")

    hidden_one, moe_factor, moe_in = before_experts(
        terms_of(attn_out), part_tokens, moe_gain_f
    )

    moe_in = exchange(moe_in, PAIR_TENSOR)
    out_kept, out_sent, moe_grad_part, moe_grads = experts(
        my_te, moe_in, pair_cotangent, share, moe_w, lines
    )
    moe_grads = lax.psum_scatter(moe_grads, "line", scatter_dimension=0, tiled=False)
    moe_grad_terms = exchange(moe_grad_part, PAIR_TENSOR)
    delta_one, delta_attn, grad_moe_gain = after_experts(
        moe_grad_terms, hidden_one, moe_factor, moe_gain_f, part_cotangent
    )
    delta_attn = exchange(delta_attn, "tensor").reshape(own, width)
    def across(value, partner):
        return lax.ppermute(value, "tensor", [(k, partner(k)) for k in range(te)])

    out_sent = lax.optimization_barrier((out_sent, delta_attn))[0]
    out_got = across(out_sent, lambda k: 2 * (3 - k // 2) + k % 2)

    pair_delta = exchange(project_out_back(delta_attn, attn_w), DP)
    pair_grads = attention_back(
        packed, key_place, query_place, query_start, log_total, pair_delta
    )
    pair_grads, out_got, moe_grads = lax.optimization_barrier((pair_grads, out_got, moe_grads))
    out_kept, out_sent = halve(my_te // 2 % 2, out_kept, out_got)
    out_got = across(out_sent, lambda k: k ^ 2)
    got, out_got, moe_grads = lax.optimization_barrier(
        (exchange(pair_grads, DP), out_got, moe_grads)
    )
    out_terms = quarter_terms(my_te % 2, pair, out_kept, out_got)
    out_terms = (
        out_terms[0],
        swap(out_terms[1]),
        across(out_terms[2], lambda k: k ^ 1),
        lax.ppermute(
            out_terms[3], PAIR_TENSOR, [(k, (k + te) % (2 * te) ^ 1) for k in range(2 * te)]
        ),
    )
    weighted, delta_value, inner, gain_grads = unpack(got, pre, factors, cosine, sine, scales)
    inner, moe_grads = lax.optimization_barrier((spread(inner, "tensor"), moe_grads))
    low_lanes, high_lanes = moe_grads[:, :block], moe_grads[:, block:]
    grads_kept = jnp.where(first, low_lanes, high_lanes)
    grads_got = swap(jnp.where(first, high_lanes, low_lanes))
    delta_pre, attn_grad = project_back(inner, weighted, pre, factors, delta_value, attn_w)
    attn_grad, out_terms = lax.optimization_barrier((attn_grad, out_terms))
    attn_grad_terms = terms_of(attn_grad)
    attn_grads = attention_grads(
        normed_b, lax.optimization_barrier((delta_pre, attn_grad))[0], delta_attn, mixed_b
    )
    attn_grads = lax.psum_scatter(attn_grads, "line", scatter_dimension=0, tiled=False)
    low_rows, high_rows = attn_grads[:block], attn_grads[block:]
    attn_grads = jnp.where(first, low_rows, high_rows).astype(f32) + swap(
        jnp.where(first, high_rows, low_rows)
    ).astype(f32)

    def gain_cut(gradient):
        return gradient.reshape(heads, dp, head_part).transpose(1, 0, 2).reshape(dp, -1)

    head_gain_grads = jnp.concatenate([gain_cut(gain_grads[:, :local]), gain_cut(gain_grads[:, local:])], axis=1)
    head_gain_grads = jnp.pad(
        head_gain_grads[:, None], ((0, 0), (0, micro - 1), (0, HEAD - 2 * head_cut))
    ).reshape(part, HEAD)
    home = finish(
        micro,
        attn_grad_terms,
        part_tokens,
        attn_gain_f,
        delta_one,
        hidden_one,
        *out_terms,
        grad_moe_gain,
        head_gain_grads,
    )
    home, grads_got = lax.optimization_barrier((home, grads_got))
    home, attn_grads = lax.optimization_barrier(
        (exchange(home.reshape(te * dp, micro, -1), ("tensor",) + DP), attn_grads)
    )
    output, input_grad, gain_sum, head_gain_grads = deliver(
        my_te, home, home_hot
    )
    output = output.reshape(micro, block, width)
    input_grad = input_grad.reshape(micro, block, width)

    gate_grad, up_grad, down_grad = expert_gradients(pair, grads_kept, grads_got)
    return (
        output,
        input_grad,
        gain_sum[0],
        attn_grads[:, :local],
        attn_grads[:, local : 2 * local],
        attn_grads[:, 2 * local : 3 * local],
        head_gain_grads[0, :head_cut].reshape(heads, head_part),
        head_gain_grads[0, head_cut : 2 * head_cut].reshape(heads, head_part),
        attn_grads[:, 3 * local :].T,
        gain_sum[1],
        gate_grad,
        up_grad,
        down_grad,
    )


def solution(mesh):
    lines = mesh.shape["dp"] // 2
    devices = mesh.devices.reshape(2, lines, mesh.shape["tensor"])
    placed = (
        P(None, DP, None),
        P(None, DP, None),
        P(),
        P(),
        P(None, DP, None),
        P(None, DP, None),
        P(DP),
        P(DP, "tensor"),
        P(DP, "tensor"),
        P(DP, "tensor"),
        P("tensor", DP),
        P("tensor", DP),
        P("tensor", DP),
        P(DP),
        P(None, DP, "tensor"),
        P(None, DP, "tensor"),
        P(None, "tensor", DP),
    )
    return jax.shard_map(
        body,
        mesh=Mesh(devices, DP + ("tensor",)),
        in_specs=placed,
        out_specs=(
            P(None, DP, None),
            P(None, DP, None),
            P(DP),
            P(DP, "tensor"),
            P(DP, "tensor"),
            P(DP, "tensor"),
            P("tensor", DP),
            P("tensor", DP),
            P("tensor", DP),
            P(DP),
            P(None, DP, "tensor"),
            P(None, DP, "tensor"),
            P(None, "tensor", DP),
        ),
        check_vma=False,
    )
```

```python
import jax
import jax.numpy as jnp
from jax import lax
from jax.experimental import pallas as pl
from jax.experimental.pallas import tpu as pltpu
from jax.sharding import Mesh
from jax.sharding import PartitionSpec as P

HEAD = 128
MIB = 1024 * 1024
bf16 = jnp.bfloat16
f32 = jnp.float32

DP = ("pair", "line")
PAIR_TENSOR = ("pair", "tensor")

RANKS = 8

epsilon = 1e-05
rope_base = 10000.0


def rope_tables(position):
    half_dim = HEAD // 2
    frequency = rope_base ** (-(jnp.arange(half_dim, dtype=f32) * 2.0 / HEAD))
    angle = position[:, None] * frequency[None, :]
    cosine = jnp.concatenate([jnp.cos(angle), jnp.cos(angle)], axis=-1)
    sine = jnp.concatenate([jnp.sin(angle), jnp.sin(angle)], axis=-1)
    return (cosine, sine)


def norm_factor(values):
    return lax.rsqrt(jnp.mean(values * values, axis=-1, keepdims=True) + epsilon)


def norm_back(values, factor, gain, gradient):
    gained = gradient * gain
    inner_sum = jnp.sum(gained * values, axis=-1, keepdims=True)
    return factor * gained - values * (factor * factor * factor) * inner_sum / values.shape[-1]


def dot_nn(left_side, right_side):
    return jnp.dot(left_side, right_side, preferred_element_type=f32)


def dot_tn(left_side, right_side):
    return lax.dot_general(
        left_side, right_side, (((0,), (0,)), ((), ())), preferred_element_type=f32
    )


def dot_nt(left_side, right_side):
    return lax.dot_general(
        left_side, right_side, (((1,), (1,)), ((), ())), preferred_element_type=f32
    )


def exchange(value, axis):
    return lax.all_to_all(value, axis, split_axis=0, concat_axis=0, tiled=True)


def swap(value):
    return lax.ppermute(value, "pair", [(0, 1), (1, 0)])


def in_order(first, mine, other, axis=0):
    return jnp.stack([jnp.where(first, mine, other), jnp.where(first, other, mine)], axis=axis)


def turned(values):
    cut = values.reshape(values.shape[:-1] + (2, -1, HEAD))
    return jnp.swapaxes(cut, -3, -2).reshape(values.shape)


def spread(value, axis):
    count = lax.axis_size(axis)
    copies = jnp.broadcast_to(value[None], (count,) + value.shape)
    return exchange(copies, axis)


BLOCK = 512

IN_VMEM = pl.BlockSpec(memory_space=pltpu.VMEM)
IN_HBM = pl.BlockSpec(memory_space=pltpu.HBM)

KEYS = slice(0, 128)
VALUES = slice(128, 256)
QUERIES = slice(256, 288)
Q_BLOCKS = 4

MICRO = 2
HEADS = 2
QUARTERS = 4


def seen(sources, part):
    return slice(0, min(sources, (part + 1) * Q_BLOCKS) * 128)


def masked_scores(query, keys, key_place, query_place, query_start):
    scores = dot_nt(query, keys) * (HEAD ** (-0.5))
    visible = (key_place <= query_place) & (key_place >= query_start)
    return jnp.where(visible, scores, -1e30)


def attention_kernel(packed, key_place, query_place, query_start, mixed, log_total):
    sources = packed.shape[0]
    keys = packed[:, KEYS, :].reshape(sources * 128, HEAD)
    values = packed[:, VALUES, :].reshape(sources * 128, HEAD)
    for part in range(sources // Q_BLOCKS):
        blocks = slice(part * Q_BLOCKS, (part + 1) * Q_BLOCKS)
        rows = slice(part * Q_BLOCKS * 32, (part + 1) * Q_BLOCKS * 32)
        query = packed[blocks, QUERIES, :].reshape(Q_BLOCKS * 32, HEAD)
        past = seen(sources, part)
        scores = masked_scores(
            query, keys[past], key_place[:, past], query_place[rows, :], query_start[rows, :]
        )
        peak = jnp.max(scores, axis=-1, keepdims=True)
        weights = jnp.exp(scores - peak)
        total = jnp.sum(weights, axis=-1, keepdims=True)
        probs = (weights / total).astype(bf16)
        mixed[blocks, :, :] = (
            dot_nn(probs, values[past]).astype(bf16).reshape(Q_BLOCKS, 32, HEAD)
        )
        log_total[rows, :] = peak + jnp.log(total)


def attention_back_kernel(
    packed, key_place, query_place, query_start, log_total, delta_mixed, out, key_sum, value_sum
):
    sources = packed.shape[0]
    keys = packed[:, KEYS, :].reshape(sources * 128, HEAD)
    values = packed[:, VALUES, :].reshape(sources * 128, HEAD)
    scale = HEAD ** (-0.5)
    for part in reversed(range(sources // Q_BLOCKS)):
        blocks = slice(part * Q_BLOCKS, (part + 1) * Q_BLOCKS)
        rows = slice(part * Q_BLOCKS * 32, (part + 1) * Q_BLOCKS * 32)
        query = packed[blocks, QUERIES, :].reshape(Q_BLOCKS * 32, HEAD)
        delta = delta_mixed[blocks, :, :].reshape(Q_BLOCKS * 32, HEAD)
        past = seen(sources, part)
        scores = masked_scores(
            query, keys[past], key_place[:, past], query_place[rows, :], query_start[rows, :]
        )
        probs = jnp.exp(scores - log_total[rows, :])
        delta_probs = dot_nt(delta, values[past])
        inner = jnp.sum(probs * delta_probs, axis=-1, keepdims=True)
        delta_scores = (probs * (delta_probs - inner)).astype(bf16)
        out[blocks, QUERIES, :] = (
            (dot_nn(delta_scores, keys[past]) * scale).astype(bf16).reshape(Q_BLOCKS, 32, HEAD)
        )
        key_term = dot_tn(delta_scores, query)
        value_term = dot_tn(probs.astype(bf16), delta)
        if part == sources // Q_BLOCKS - 1:
            key_sum[...] = key_term
            value_sum[...] = value_term
        else:
            key_sum[past, :] += key_term
            value_sum[past, :] += value_term
    out[:, KEYS, :] = (key_sum[...] * scale).astype(bf16).reshape(sources, 128, HEAD)
    out[:, VALUES, :] = value_sum[...].astype(bf16).reshape(sources, 128, HEAD)


def attention(packed, key_place, query_place, query_start):
    sources = packed.shape[0]
    return pl.pallas_call(
        attention_kernel,
        out_shape=(
            jax.ShapeDtypeStruct((sources, 32, HEAD), bf16),
            jax.ShapeDtypeStruct((sources * 32, 1), f32),
        ),
        compiler_params=pltpu.CompilerParams(vmem_limit_bytes=40 * MIB),
        name="attention",
    )(packed, key_place, query_place, query_start)


def attention_back(packed, key_place, query_place, query_start, log_total, delta_mixed):
    sources = packed.shape[0]
    return pl.pallas_call(
        attention_back_kernel,
        out_shape=jax.ShapeDtypeStruct(packed.shape, bf16),
        scratch_shapes=[
            pltpu.VMEM((sources * 128, HEAD), f32),
            pltpu.VMEM((sources * 128, HEAD), f32),
        ],
        compiler_params=pltpu.CompilerParams(vmem_limit_bytes=40 * MIB),
        name="attention_back",
    )(packed, key_place, query_place, query_start, log_total, delta_mixed)


def order_hot(count, micro, forward):
    part = count // micro
    row = lax.broadcasted_iota(jnp.int32, (count, count), 0)
    column = lax.broadcasted_iota(jnp.int32, (count, count), 1)
    if not forward:
        row, column = column, row
    return jnp.where(column == micro * (row % part) + row // part, 1.0, 0.0).astype(bf16)


def reordered(values, micro, forward):
    return dot_nn(order_hot(values.shape[0], micro, forward), values).astype(bf16)


def half_signs(shape):
    return lax.broadcasted_iota(jnp.int32, shape, 1) < HEAD // 2


def row_sums(values):
    return jnp.sum(values.T, axis=0, keepdims=True)


def as_columns(row):
    return jnp.broadcast_to(row, (HEAD, row.shape[1])).T


def head_lanes(head):
    return slice(head * HEAD, (head + 1) * HEAD)


def pair_index(micro_index, head, quarter):
    return (micro_index * HEADS + head) * QUARTERS + quarter


def project_kernel(tokens, gain, stored, normed, pre, value, squares, weights, semaphore):
    copy = load(stored.at[:, 0:3], weights, semaphore)
    values = tokens[...].astype(f32)
    rows = (values * norm_factor(values) * gain[...]).astype(bf16)
    rows = reordered(rows, MICRO, True)
    normed[...] = rows
    local = value.shape[1]
    copy.wait()
    width = rows.shape[1]
    sums = []
    for k in range(2):
        values = dot_nn(rows, weights[:, k].reshape(width, local))
        pre[:, k * local : (k + 1) * local] = values
        sums.append(row_sums(values * values))
    value[...] = dot_nn(rows, weights[:, 2].reshape(width, local)).astype(bf16)
    squares[...] = jnp.concatenate(sums, axis=0)


def project(tokens, gain, weights):
    count, width = tokens.shape
    lines, _, rows, local = weights.shape
    return pl.pallas_call(
        project_kernel,
        in_specs=[IN_VMEM, IN_VMEM, IN_HBM],
        scratch_shapes=[pltpu.VMEM((lines, 3, rows, local), bf16), pltpu.SemaphoreType.DMA],
        out_specs=[IN_VMEM] * 4,
        out_shape=(
            jax.ShapeDtypeStruct((count, width), bf16),
            jax.ShapeDtypeStruct((count, 2 * local), f32),
            jax.ShapeDtypeStruct((count, local), bf16),
            jax.ShapeDtypeStruct((2, count), f32),
        ),
        compiler_params=pltpu.CompilerParams(vmem_limit_bytes=60 * MIB),
        name="project",
    )(tokens, gain, weights)


def pack_kernel(squares, pre, value, cosine, sine, scales, packed, factors):
    count, local = value.shape
    block = count // MICRO
    total = summed(squares)
    factor = lax.rsqrt(total / (local * squares.shape[0]) + epsilon)
    low = half_signs((count, HEAD))
    signed_sine = jnp.where(low, -sine[...], sine[...])
    columns = [as_columns(factor[k : k + 1]) for k in range(2)]
    factors[...] = jnp.concatenate(columns, axis=1)
    for head in range(HEADS):
        turned_heads = []
        for k in range(2):
            lanes = slice(k * local + head * HEAD, k * local + (head + 1) * HEAD)
            values = pre[:, lanes] * columns[k] * scales[:, lanes]
            rotated = values * cosine[...] + pltpu.roll(values, HEAD // 2, 1) * signed_sine
            turned_heads.append(rotated.astype(bf16))
        query, key = turned_heads
        for m in range(MICRO):
            rows = slice(m * block, (m + 1) * block)
            for quarter in range(QUARTERS):
                index = pair_index(m, head, quarter)
                start = m * block + quarter * block // QUARTERS
                packed[index, KEYS, :] = key[rows]
                packed[index, VALUES, :] = value[rows, head_lanes(head)]
                packed[index, QUERIES, :] = query[start : start + block // QUARTERS]


def pack(squares, pre, value, cosine, sine, scales):
    count, local = value.shape
    rows = (2 * QUARTERS + 1) * (count // MICRO // QUARTERS)
    return pl.pallas_call(
        pack_kernel,
        in_specs=[IN_VMEM] * 6,
        out_specs=[IN_VMEM] * 2,
        out_shape=(
            jax.ShapeDtypeStruct((MICRO * HEADS * QUARTERS, rows, HEAD), bf16),
            jax.ShapeDtypeStruct((count, 2 * HEAD), f32),
        ),
        compiler_params=pltpu.CompilerParams(vmem_limit_bytes=24 * MIB),
        name="pack",
    )(squares, pre, value, cosine, sine, scales)


def from_quarters(arrived, head):
    return jnp.concatenate(
        [
            arrived[pair_index(m, head, quarter)]
            for m in range(MICRO)
            for quarter in range(QUARTERS)
        ],
        axis=0,
    )


def project_out_kernel(arrived, stored, mixed, out, weights, semaphore):
    copy = load(stored.at[:, 3], weights, semaphore)
    rows = jnp.concatenate([from_quarters(arrived, head) for head in range(HEADS)], axis=1)
    rows = reordered(rows, MICRO, False)
    mixed[...] = rows
    copy.wait()
    out[...] = dot_nt(rows, weights[...].reshape(out.shape[1], rows.shape[1])).astype(bf16)


def project_out(arrived, weights):
    lines, _, rows, local = weights.shape
    count = arrived.shape[0] * arrived.shape[1] // HEADS
    return pl.pallas_call(
        project_out_kernel,
        in_specs=[IN_VMEM, IN_HBM],
        scratch_shapes=[pltpu.VMEM((lines, rows, local), bf16), pltpu.SemaphoreType.DMA],
        out_specs=[IN_VMEM] * 2,
        out_shape=(
            jax.ShapeDtypeStruct((count, local), bf16),
            jax.ShapeDtypeStruct((count, lines * rows), bf16),
        ),
        compiler_params=pltpu.CompilerParams(vmem_limit_bytes=60 * MIB),
        name="project_out",
    )(arrived, weights)


def project_out_back_kernel(delta, stored, out, weights, semaphore):
    load(stored.at[:, 3], weights, semaphore).wait()
    rows = dot_nn(delta[...], weights[...].reshape(delta.shape[1], -1)).astype(bf16)
    rows = reordered(rows, MICRO, True)
    step = out.shape[1]
    block = rows.shape[0] // MICRO
    for m in range(MICRO):
        for head in range(HEADS):
            for quarter in range(QUARTERS):
                start = m * block + quarter * step
                out[pair_index(m, head, quarter)] = rows[start : start + step, head_lanes(head)]


def project_out_back(delta, weights):
    count = delta.shape[0]
    lines, _, rows, local = weights.shape
    devices = MICRO * HEADS * QUARTERS
    return pl.pallas_call(
        project_out_back_kernel,
        in_specs=[IN_VMEM, IN_HBM],
        scratch_shapes=[
            pltpu.VMEM((lines, rows, local), bf16),
            pltpu.SemaphoreType.DMA,
        ],
        out_specs=IN_VMEM,
        out_shape=jax.ShapeDtypeStruct((devices, count * HEADS // devices, HEAD), bf16),
        compiler_params=pltpu.CompilerParams(vmem_limit_bytes=60 * MIB),
        name="project_out_back",
    )(delta, weights)


def unpack_kernel(
    arrived, pre, factors, cosine, sine, scales, weighted, delta_value, inner, gain_grads
):
    count, local = delta_value.shape
    low = half_signs((count, HEAD))
    signs = jnp.where(low, 1.0, -1.0)
    products = [None, None]
    for head in range(HEADS):
        sums = []
        for rows in (KEYS, VALUES):
            parts = []
            for m in range(MICRO):
                total = arrived[pair_index(m, head, 0), rows, :].astype(f32)
                for quarter in range(1, QUARTERS):
                    total = total + arrived[pair_index(m, head, quarter), rows, :].astype(f32)
                parts.append(total)
            sums.append(jnp.concatenate(parts, axis=0))
        delta_key, value = sums
        delta_value[:, head_lanes(head)] = value.astype(bf16)
        delta_query = jnp.concatenate(
            [
                arrived[pair_index(m, head, quarter), QUERIES, :]
                for m in range(MICRO)
                for quarter in range(QUARTERS)
            ],
            axis=0,
        ).astype(f32)
        for k, gradient in ((0, delta_query), (1, delta_key)):
            lanes = slice(k * local + head * HEAD, k * local + (head + 1) * HEAD)
            scaled = pltpu.roll(gradient * sine[...], HEAD // 2, 1) * signs
            normed_gradient = gradient * cosine[...] + scaled
            values = pre[:, lanes]
            gain_grads[:, lanes] = jnp.sum(
                normed_gradient * values * factors[:, head_lanes(k)], axis=0, keepdims=True
            )
            gained = normed_gradient * scales[:, lanes]
            weighted[:, lanes] = gained
            product = gained * values
            products[k] = product if head == 0 else products[k] + product
    inner[...] = jnp.concatenate([row_sums(product) for product in products], axis=0)


def unpack(arrived, pre, factors, cosine, sine, scales):
    count, lanes = pre.shape
    return pl.pallas_call(
        unpack_kernel,
        in_specs=[IN_VMEM] * 6,
        out_specs=[IN_VMEM] * 4,
        out_shape=(
            jax.ShapeDtypeStruct((count, lanes), f32),
            jax.ShapeDtypeStruct((count, lanes // 2), bf16),
            jax.ShapeDtypeStruct((2, count), f32),
            jax.ShapeDtypeStruct((1, lanes), f32),
        ),
        compiler_params=pltpu.CompilerParams(vmem_limit_bytes=24 * MIB),
        name="unpack",
    )(arrived, pre, factors, cosine, sine, scales)


def project_back_kernel(
    inner, weighted, pre, factors, value, stored, delta_pre, out, weights, semaphore
):
    local = value.shape[1]
    copy = load(stored.at[:, 0:3], weights, semaphore)
    total = summed(inner) / (local * inner.shape[0])
    for k in range(2):
        factor = factors[:, head_lanes(k)]
        column = factor * factor * factor * as_columns(total[k : k + 1])
        for head in range(HEADS):
            lanes = slice(k * local + head * HEAD, k * local + (head + 1) * HEAD)
            delta_pre[:, lanes] = (factor * weighted[:, lanes] - pre[:, lanes] * column).astype(
                bf16
            )
    delta_pre[:, 2 * local :] = value[...]
    rows = reordered(delta_pre[...], MICRO, False)
    copy.wait()
    lines, _, step, _ = weights.shape
    for line in range(lines):
        chunk = jnp.concatenate([weights[line, k] for k in range(3)], axis=1)
        out[:, line * step : (line + 1) * step] = dot_nt(rows, chunk).astype(bf16)


def project_back(inner, weighted, pre, factors, value, weights):
    count = value.shape[0]
    lines, _, rows, local = weights.shape
    return pl.pallas_call(
        project_back_kernel,
        in_specs=[IN_VMEM] * 5 + [IN_HBM],
        scratch_shapes=[
            pltpu.VMEM((lines, 3, rows, local), bf16),
            pltpu.SemaphoreType.DMA,
        ],
        out_specs=[IN_VMEM] * 2,
        out_shape=(
            jax.ShapeDtypeStruct((count, 3 * local), bf16),
            jax.ShapeDtypeStruct((count, lines * rows), bf16),
        ),
        compiler_params=pltpu.CompilerParams(vmem_limit_bytes=60 * MIB),
        name="project_back",
    )(inner, weighted, pre, factors, value, weights)


def load(source, target, semaphore):
    copy = pltpu.make_async_copy(source, target, semaphore)
    copy.start()
    return copy


def attention_grads_kernel(normed, delta_pre, delta_attn, mixed, out):
    lines = out.shape[0]
    pre_width = delta_pre.shape[1]
    for line in range(lines):
        lanes = slice(2 * line * HEAD, 2 * (line + 1) * HEAD)
        out[line, :, :pre_width] = dot_tn(normed[:, lanes], delta_pre[...]).astype(bf16)
        out[line, :, pre_width:] = dot_tn(delta_attn[:, lanes], mixed[...]).astype(bf16)


def attention_grads(normed, delta_pre, delta_attn, mixed):
    lines = normed.shape[1] // HEAD // 2
    return pl.pallas_call(
        attention_grads_kernel,
        out_shape=jax.ShapeDtypeStruct(
            (lines, 2 * HEAD, delta_pre.shape[1] + mixed.shape[1]), bf16
        ),
        compiler_params=pltpu.CompilerParams(vmem_limit_bytes=24 * MIB),
        name="attention_grads",
    )(normed, delta_pre, delta_attn, mixed)


def stack_attention_kernel(w_query, w_key, w_value, w_out, out):
    out[0] = w_query[...]
    out[1] = w_key[...]
    out[2] = w_value[...]
    out[3] = w_out[...].T


def stack_attention(w_query, w_key, w_value, w_out):
    return pl.pallas_call(
        stack_attention_kernel,
        out_shape=jax.ShapeDtypeStruct((4,) + w_query.shape, bf16),
        name="stack_attention",
    )(w_query, w_key, w_value, w_out)


def stack_experts_kernel(pair, w_gate, w_up, w_down, kept, sent):
    half = w_gate.shape[0] // 2
    each = BLOCK // HEAD
    for out, which in ((kept, pair[0]), (sent, 1 - pair[0])):
        for expert in range(half):
            for index, stored in enumerate((w_gate, w_up, w_down)):
                start = expert // each * 3 * BLOCK + index * BLOCK + expert % each * HEAD
                value = stored[which * half + expert]
                out[:, start : start + HEAD] = value.T if stored is w_down else value


def stack_experts(pair, w_gate, w_up, w_down):
    count, rows, hidden = w_gate.shape
    shape = jax.ShapeDtypeStruct((rows, 3 * count * hidden // 2), bf16)
    return pl.pallas_call(
        stack_experts_kernel,
        in_specs=[pl.BlockSpec(memory_space=pltpu.SMEM)]
        + [pl.BlockSpec(memory_space=pltpu.VMEM)] * 3,
        out_shape=(shape, shape),
        compiler_params=pltpu.CompilerParams(vmem_limit_bytes=24 * MIB),
        name="stack_experts",
    )(pair.reshape(1), w_gate, w_up, w_down)


def experts_kernel(my_rank, arrived, upstream, gates, weights, *refs):
    (
        out_kept,
        out_sent,
        delta_in,
        grads,
        held,
        hidden_all,
        deltas_all,
        grads_out,
        out_all,
        rows,
        in_sem,
        out_sem,
    ) = refs
    steps = held.shape[0]
    width = upstream.shape[1]
    lines = grads.shape[0]
    lane_part = width // lines
    part = out_kept.shape[2]
    loads = [
        pltpu.make_async_copy(
            weights.at[:, pl.ds(c * 3 * BLOCK, 3 * BLOCK)], held.at[c], in_sem.at[c]
        )
        for c in range(steps)
    ]
    for load in loads:
        load.start()
    for k in range(arrived.shape[0]):
        rows[k * part : (k + 1) * part, :] = from_blocks(arrived.at[k])
    stores = []
    for c in range(steps):
        loads[c].wait()
        gate_up = dot_nn(rows[...], held[c, :, 0 : 2 * BLOCK])
        gate_h, up_h = gate_up[:, :BLOCK], gate_up[:, BLOCK:]
        delta_hidden = dot_nn(upstream[...], held[c, :, 2 * BLOCK : 3 * BLOCK])
        share = jnp.concatenate(
            [
                jnp.broadcast_to(gates[:, e : e + 1], (gates.shape[0], HEAD))
                for e in range(c * BLOCK // HEAD, (c + 1) * BLOCK // HEAD)
            ],
            axis=1,
        )
        sigmoid_gate = 1.0 / (1.0 + jnp.exp(-gate_h))
        active = gate_h * sigmoid_gate
        hidden = (active * up_h * share).astype(bf16)
        delta_hidden = delta_hidden * share
        delta_gate = (
            delta_hidden * up_h * sigmoid_gate * (1.0 + gate_h * (1.0 - sigmoid_gate))
        ).astype(bf16)
        delta_up = (delta_hidden * active).astype(bf16)
        start = 2 * c * BLOCK
        hidden_all[:, c * BLOCK : (c + 1) * BLOCK] = hidden
        deltas_all[:, start : start + BLOCK] = delta_gate
        deltas_all[:, start + BLOCK : start + 2 * BLOCK] = delta_up
        deltas = deltas_all[:, start : start + 2 * BLOCK]
        slot = c % 2
        if c >= 2:
            stores[c - 2].wait()
        for n in range(lines):
            lanes = slice(n * lane_part, (n + 1) * lane_part)
            grads_out[slot, n, 0 : 2 * BLOCK, :] = dot_tn(deltas, rows[:, lanes]).astype(bf16)
            grads_out[slot, n, 2 * BLOCK :, :] = dot_tn(hidden, upstream[:, lanes]).astype(bf16)
        store = pltpu.make_async_copy(
            grads_out.at[slot], grads.at[:, pl.ds(c * 3 * BLOCK, 3 * BLOCK), :], out_sem.at[slot]
        )
        store.start()
        stores.append(store)
    for n in range(lines):
        lanes = slice(n * lane_part, (n + 1) * lane_part)
        gate_up = jnp.concatenate(
            [held[c, lanes, 0 : 2 * BLOCK] for c in range(steps)], axis=1
        )
        produced = dot_nt(deltas_all[...], gate_up).astype(bf16)
        for k in range(2 * RANKS):
            for b in range(lane_part // HEAD):
                delta_in[k, n * (lane_part // HEAD) + b] = produced[
                    k * part : (k + 1) * part, b * HEAD : (b + 1) * HEAD
                ]
        down = jnp.concatenate(
            [held[c, lanes, 2 * BLOCK : 3 * BLOCK] for c in range(steps)], axis=1
        )
        produced = dot_nt(hidden_all[...], down).astype(bf16)
        out_all[:, :, lanes] = produced.reshape(2 * RANKS, part, lane_part)
    high = my_rank[0] // (RANKS // 2)
    for p in range(2):
        for q in range(RANKS // 2):
            out_kept[q, p] = out_all[p * RANKS + high * (RANKS // 2) + q]
            out_sent[q, p] = out_all[p * RANKS + (1 - high) * (RANKS // 2) + q]
    for store in stores[-2:]:
        store.wait()


def experts(my_rank, arrived, upstream, gates, weights, lines):
    count, width = upstream.shape
    part = count // RANKS // 2
    steps = weights.shape[1] // (3 * BLOCK)
    in_vmem = pl.BlockSpec(memory_space=pltpu.VMEM)
    in_hbm = pl.BlockSpec(memory_space=pl.ANY)
    return pl.pallas_call(
        experts_kernel,
        in_specs=[pl.BlockSpec(memory_space=pltpu.SMEM), in_vmem, in_vmem, in_vmem, in_hbm],
        out_specs=[in_vmem, in_vmem, in_vmem, in_hbm],
        out_shape=(
            *[jax.ShapeDtypeStruct((RANKS // 2, 2, part, width), bf16)] * 2,
            jax.ShapeDtypeStruct(arrived.shape, bf16),
            jax.ShapeDtypeStruct((lines, weights.shape[1], width // lines), bf16),
        ),
        scratch_shapes=[
            pltpu.VMEM((steps, width, 3 * BLOCK), bf16),
            pltpu.VMEM((count, steps * BLOCK), bf16),
            pltpu.VMEM((count, 2 * steps * BLOCK), bf16),
            pltpu.VMEM((2, lines, 3 * BLOCK, width // lines), bf16),
            pltpu.VMEM((2 * RANKS, part, width), bf16),
            pltpu.VMEM((count, width), bf16),
            pltpu.SemaphoreType.DMA((steps,)),
            pltpu.SemaphoreType.DMA((2,)),
        ],
        compiler_params=pltpu.CompilerParams(vmem_limit_bytes=56 * MIB),
        name="experts",
    )(my_rank.reshape(1), arrived, upstream, gates, weights)


def expert_gradients_kernel(pair, kept, got, gate_grad, up_grad, down_grad):
    half = gate_grad.shape[0] // 2
    each = BLOCK // HEAD
    for stored, which in ((kept, pair[0]), (got, 1 - pair[0])):
        for expert in range(half):
            for index, out in enumerate((gate_grad, up_grad, down_grad)):
                start = expert // each * 3 * BLOCK + index * BLOCK + expert % each * HEAD
                value = stored[start : start + HEAD].astype(f32)
                out[which * half + expert] = value if out is down_grad else value.T


def expert_gradients(pair, kept, got):
    count = 2 * kept.shape[0] // 3 // HEAD
    in_vmem = pl.BlockSpec(memory_space=pltpu.VMEM)
    shape = jax.ShapeDtypeStruct((count, kept.shape[1], HEAD), f32)
    return pl.pallas_call(
        expert_gradients_kernel,
        in_specs=[pl.BlockSpec(memory_space=pltpu.SMEM), in_vmem, in_vmem],
        out_shape=(shape, shape, shape),
        compiler_params=pltpu.CompilerParams(vmem_limit_bytes=24 * MIB),
        name="expert_gradients",
    )(pair.reshape(1), kept, got)


def summed(terms):
    total = terms[0].astype(f32)
    for k in range(1, terms.shape[0]):
        total = total + terms[k].astype(f32)
    return total


def put_blocks(out, rows):
    for block in range(out.shape[0]):
        out[block] = rows[:, block * HEAD : (block + 1) * HEAD]


def from_blocks(blocks):
    return jnp.concatenate([blocks[k] for k in range(blocks.shape[0])], axis=1)


def lane_blocks(width, forward):
    lines = width // HEAD // 2
    moves = [(p * lines + n, n * 2 + p) for p in range(2) for n in range(lines)]
    return moves if forward else [(b, a) for a, b in moves]


def move_lanes(values, forward):
    moves = sorted((b, a) for a, b in lane_blocks(values.shape[-1], forward))
    return jnp.concatenate([values[:, a * HEAD : (a + 1) * HEAD] for _, a in moves], axis=1)


def deal_kernel(
    where, places, stored_tokens, stored_cotangent, gains, out, tokens, cotangent, semaphores
):
    copies = [
        load(stored_tokens, tokens, semaphores.at[0]),
        load(stored_cotangent, cotangent, semaphores.at[1]),
    ]
    count, width = tokens.shape
    rows, block = places.shape
    given = places[...] - where[0] * block
    mine = (given >= 0) & (given < block)
    before = lax.broadcasted_iota(jnp.int32, (block, block), 0) < lax.broadcasted_iota(
        jnp.int32, (block, block), 1
    )
    rank = dot_nn(
        jnp.where(mine, 1.0, 0.0).astype(bf16), jnp.where(before, 1.0, 0.0).astype(bf16)
    ).astype(jnp.int32)
    hit = mine & (rank == where[1])
    order = jnp.sum(jnp.where(hit, given, 0), axis=1, keepdims=True)
    micro = lax.broadcasted_iota(jnp.int32, (rows, 1), 0) % (count // block)
    hot = order + micro * block == lax.broadcasted_iota(jnp.int32, (rows, count), 1)
    hot = jnp.where(hot, 1.0, 0.0).astype(bf16)
    copies[0].wait()
    token_rows = move_lanes(dot_nn(hot, tokens[...]).astype(bf16), True)
    copies[1].wait()
    gradient = move_lanes(dot_nn(hot, cotangent[...]).astype(bf16), True)
    odd = lax.broadcasted_iota(jnp.int32, (rows, gains.shape[1]), 0) % 2 == 1
    values = gains[...].astype(f32)
    beside = jnp.where(odd, values[1:2], values[0:1]).astype(bf16)
    partner = jnp.concatenate([gradient[rows // 2 :], gradient[: rows // 2]], axis=0)
    sent = jnp.concatenate([token_rows, gradient, partner, beside], axis=1)
    for chunk in range(out.shape[0]):
        out[chunk] = sent[chunk * out.shape[1] : (chunk + 1) * out.shape[1]]


def deal(where, places, tokens, cotangent, gains):
    width = tokens.shape[1]
    return pl.pallas_call(
        deal_kernel,
        in_specs=[pl.BlockSpec(memory_space=pltpu.SMEM), IN_VMEM, IN_HBM, IN_HBM, IN_VMEM],
        scratch_shapes=[
            pltpu.VMEM(tokens.shape, bf16),
            pltpu.VMEM(cotangent.shape, bf16),
            pltpu.SemaphoreType.DMA((2,)),
        ],
        out_shape=jax.ShapeDtypeStruct(
            (places.shape[0] // MICRO, MICRO, 3 * width + gains.shape[1]), bf16
        ),
        compiler_params=pltpu.CompilerParams(vmem_limit_bytes=60 * MIB),
        name="deal",
    )(where, places, tokens, cotangent, gains)


def before_experts_kernel(terms, tokens, gain, hidden_one, factor, moe_in):
    hidden = tokens[...].astype(f32) + summed(terms)
    scale = norm_factor(hidden)
    hidden_one[...] = hidden
    factor[...] = scale
    rows = (hidden * scale * gain[...]).astype(bf16)
    for k in range(moe_in.shape[0]):
        put_blocks(moe_in.at[k], rows)


def before_experts(terms, tokens, gain):
    rows, width = tokens.shape
    return pl.pallas_call(
        before_experts_kernel,
        in_specs=[IN_VMEM] * 3,
        out_specs=[IN_VMEM] * 3,
        out_shape=(
            jax.ShapeDtypeStruct((rows, width), f32),
            jax.ShapeDtypeStruct((rows, 1), f32),
            jax.ShapeDtypeStruct((2 * RANKS, width // HEAD, rows, HEAD), bf16),
        ),
        compiler_params=pltpu.CompilerParams(vmem_limit_bytes=24 * MIB),
        name="before_experts",
    )(terms, tokens, gain)


def after_experts_kernel(
    terms, hidden_one, factor, gain, upstream, delta_one, delta_attn, gain_grad
):
    gradient = from_blocks(summed(terms))
    hidden = hidden_one[...]
    gain_grad[...] = jnp.sum(gradient * hidden * factor[...], axis=0, keepdims=True)
    delta = upstream[...].astype(f32) + norm_back(hidden, factor[...], gain[...], gradient)
    delta_one[...] = delta
    for k in range(delta_attn.shape[0]):
        delta_attn[k] = delta.astype(bf16)


def after_experts(terms, hidden_one, factor, gain, upstream):
    rows, width = upstream.shape
    return pl.pallas_call(
        after_experts_kernel,
        in_specs=[IN_VMEM] * 5,
        out_specs=[IN_VMEM] * 3,
        out_shape=(
            jax.ShapeDtypeStruct((rows, width), f32),
            jax.ShapeDtypeStruct((RANKS, rows, width), bf16),
            jax.ShapeDtypeStruct((1, width), f32),
        ),
        compiler_params=pltpu.CompilerParams(vmem_limit_bytes=24 * MIB),
        name="after_experts",
    )(terms, hidden_one, factor, gain, upstream)


def halve_kernel(bit, kept, got, mine, sent):
    half = mine.shape[0]
    for out, start in ((mine, bit[0] * half), (sent, (1 - bit[0]) * half)):
        for k in range(half):
            total = kept[start + k].astype(f32) + got[start + k].astype(f32)
            out[k] = total.astype(out.dtype)


def halve(bit, kept, got):
    shape = (kept.shape[0] // 2,) + kept.shape[1:]
    in_vmem = pl.BlockSpec(memory_space=pltpu.VMEM)
    return pl.pallas_call(
        halve_kernel,
        in_specs=[pl.BlockSpec(memory_space=pltpu.SMEM), in_vmem, in_vmem],
        out_specs=[IN_VMEM] * 2,
        out_shape=(jax.ShapeDtypeStruct(shape, f32), jax.ShapeDtypeStruct(shape, bf16)),
        compiler_params=pltpu.CompilerParams(vmem_limit_bytes=24 * MIB),
        name="halve",
    )(bit.reshape(1), kept, got)


def quarter_terms_kernel(bits, kept, got, mine, other, across_mine, across_other):
    for out, y, p in (
        (mine, bits[0], bits[1]),
        (other, bits[0], 1 - bits[1]),
        (across_mine, 1 - bits[0], bits[1]),
        (across_other, 1 - bits[0], 1 - bits[1]),
    ):
        out[...] = (kept[y, p].astype(f32) + got[y, p].astype(f32)).astype(out.dtype)


def quarter_terms(y, pair, kept, got):
    rows, width = kept.shape[2:]
    in_vmem = pl.BlockSpec(memory_space=pltpu.VMEM)
    return pl.pallas_call(
        quarter_terms_kernel,
        in_specs=[pl.BlockSpec(memory_space=pltpu.SMEM), in_vmem, in_vmem],
        out_specs=[IN_VMEM] * 4,
        out_shape=(
            jax.ShapeDtypeStruct((rows, width), f32),
            *[jax.ShapeDtypeStruct((rows, width), bf16)] * 3,
        ),
        compiler_params=pltpu.CompilerParams(vmem_limit_bytes=24 * MIB),
        name="quarter_terms",
    )(jnp.stack([y, pair]), kept, got)


def finish_kernel(
    terms,
    tokens,
    gain,
    delta_one,
    hidden_one,
    out_mine,
    out_second,
    out_third,
    out_fourth,
    moe_gain_grad,
    head_gain_grads,
    home,
):
    width = tokens.shape[1]
    values = tokens[...].astype(f32)
    gradient = summed(terms)
    factor = norm_factor(values)
    gain_grad = jnp.sum(gradient * values * factor, axis=0, keepdims=True)
    moe_out = out_mine[...]
    for term in (out_second, out_third, out_fourth):
        moe_out = moe_out + term[...].astype(f32)
    output = move_lanes((hidden_one[...] + moe_out).astype(bf16), False)
    input_grad = delta_one[...] + norm_back(values, factor, gain[...], gradient)
    input_grad = move_lanes(input_grad.astype(bf16), False)
    rows = []
    for moved, _ in sorted(lane_blocks(width, False), key=lambda move: move[1]):
        lanes = slice(moved * HEAD, (moved + 1) * HEAD)
        rows.append(gain_grad[:, lanes])
        rows.append(moe_gain_grad[:, lanes])
    gains = jnp.concatenate(rows, axis=0).astype(bf16)
    micro = home.shape[2]
    head_part = HEAD // home.shape[1]
    shape = (tokens.shape[0], head_gain_grads.shape[1])
    row, lane = (lax.broadcasted_iota(jnp.int32, shape, k) for k in range(2))
    kept = (row % micro == 0) & (lane % HEAD // head_part == row // micro)
    kept = jnp.where(kept, head_gain_grads[...], 0.0).astype(bf16)
    shape = (shape[1], HEAD)
    source, lane = (lax.broadcasted_iota(jnp.int32, shape, k) for k in range(2))
    chosen = lane == source // HEAD * head_part + source % head_part
    head_gains = dot_nn(kept, jnp.where(chosen, 1.0, 0.0).astype(bf16)).astype(bf16)
    sent = jnp.concatenate([output, input_grad, gains, head_gains], axis=1)
    for source in range(home.shape[1]):
        piece = sent[source * micro : (source + 1) * micro]
        for k in range(home.shape[0]):
            home[k, source] = piece


def finish(micro, terms, tokens, *others):
    rows, width = tokens.shape
    shape = (RANKS, rows // micro, micro, 2 * width + 2 * HEAD)
    return pl.pallas_call(
        finish_kernel,
        in_specs=[IN_VMEM] * 11,
        out_specs=IN_VMEM,
        out_shape=jax.ShapeDtypeStruct(shape, bf16),
        compiler_params=pltpu.CompilerParams(vmem_limit_bytes=24 * MIB),
        name="finish",
    )(terms, tokens, *others)


def deliver_kernel(rank, arrived, hot, output, input_grad, gains, head_gains):
    count, width = output.shape
    rows = arrived[...].reshape(count, arrived.shape[2])
    output[...] = dot_nn(hot[...], rows[:, :width]).astype(bf16)
    input_grad[...] = dot_nn(hot[...], rows[:, width : 2 * width]).astype(bf16)
    terms = rows[:, 2 * width : 2 * width + HEAD].astype(f32)
    odd = lax.broadcasted_iota(jnp.int32, terms.shape, 0) % 2
    gains[...] = jnp.concatenate(
        [
            jnp.sum(jnp.where(odd == 0, terms, 0.0), axis=0, keepdims=True),
            jnp.sum(jnp.where(odd == 1, terms, 0.0), axis=0, keepdims=True),
        ],
        axis=0,
    )
    terms = rows[:, 2 * width + HEAD :].astype(f32)
    sender = lax.broadcasted_iota(jnp.int32, terms.shape, 0) // (count // RANKS)
    head_gains[...] = jnp.sum(jnp.where(sender == rank[0], terms, 0.0), axis=0, keepdims=True)


def deliver(rank, rows, hot):
    count, lanes = rows.shape[0] * rows.shape[1], rows.shape[2]
    in_vmem = pl.BlockSpec(memory_space=pltpu.VMEM)
    shape = jax.ShapeDtypeStruct((count, lanes // 2 - HEAD), bf16)
    return pl.pallas_call(
        deliver_kernel,
        in_specs=[pl.BlockSpec(memory_space=pltpu.SMEM), in_vmem, in_vmem],
        out_shape=(
            shape,
            shape,
            jax.ShapeDtypeStruct((2, HEAD), f32),
            jax.ShapeDtypeStruct((1, HEAD), f32),
        ),
        compiler_params=pltpu.CompilerParams(vmem_limit_bytes=24 * MIB),
        name="deliver",
    )(rank.reshape(1), rows, hot)


def body(
    tokens,
    cotangent,
    pack_perm,
    lengths,
    routes,
    gates,
    attn_gain,
    w_query,
    w_key,
    w_value,
    query_gain,
    key_gain,
    w_out,
    moe_gain,
    w_gate,
    w_up,
    w_down,
):
    pair = lax.axis_index("pair")
    first = pair == 0
    lines = lax.axis_size("line")
    dp = 2 * lines
    te = lax.axis_size("tensor")
    me = lax.axis_index(DP)
    my_te = lax.axis_index("tensor")
    micro, block, width = tokens.shape
    ranks = block // dp
    own = micro * block
    part = own // te
    local = w_query.shape[1]
    heads = local // HEAD
    head_part = HEAD // dp
    quarters = dp // (micro * heads)
    expert_count = w_gate.shape[0]

    attn_local = stack_attention(w_query, w_key, w_value, w_out)
    moe_kept, moe_sent = stack_experts(pair, w_gate, w_up, w_down)

    blocks = pack_perm.reshape(micro, dp, block)
    root = blocks // block
    earlier = jnp.arange(block)[None, :] < jnp.arange(block)[:, None]
    rank = jnp.sum(
        ((root[:, :, :, None] == root[:, :, None, :]) & earlier).astype(jnp.int32), axis=3
    )
    from_me = (root == me)[:, :, None, :] & (
        rank[:, :, None, :] == jnp.arange(ranks, dtype=jnp.int32)[None, None, :, None]
    )
    given = jnp.sum(jnp.where(from_me, (blocks - me * block)[:, :, None, :], 0), axis=3)
    given = given + (jnp.arange(micro, dtype=jnp.int32) * block)[:, None, None]
    row_index = jnp.arange(own, dtype=jnp.int32)
    home_order = given.transpose(2, 1, 0).reshape(own)
    home_hot = (row_index[:, None] == home_order[None, :]).astype(bf16)
    slot = rank * dp + root
    slot_hot = slot[:, :, None, :] == jnp.arange(block, dtype=jnp.int32)[None, None, :, None]
    place_in = jnp.sum(
        jnp.where(slot_hot, jnp.arange(block, dtype=jnp.int32)[None, None, None, :], 0), axis=3
    )
    place_of = place_in + (jnp.arange(dp, dtype=jnp.int32) * block)[None, :, None]

    head_cut = heads * head_part
    head_gains = jnp.concatenate(
        [
            query_gain.reshape(1, head_cut),
            key_gain.reshape(1, head_cut),
            jnp.zeros((1, block - 2 * head_cut), bf16),
        ],
        axis=1,
    )
    gains = jnp.concatenate(
        [
            jnp.concatenate([attn_gain[None], head_gains], axis=1),
            jnp.concatenate([moe_gain[None], head_gains], axis=1),
        ],
        axis=0,
    )
    dealt = deal(
        jnp.stack([me, my_te]),
        blocks.transpose(1, 0, 2).reshape(part, block),
        tokens.reshape(own, width),
        cotangent.reshape(own, width),
        gains,
    )
    attn_local = in_order(first, attn_local, swap(attn_local), 1).reshape(4, 2 * block, local)
    attn_local = lax.optimization_barrier((attn_local, dealt))[0]
    attn_w = lax.all_gather(attn_local, "line", axis=0)
    dealt = exchange(dealt, DP).reshape(part, -1)
    part_tokens = dealt[:, :width]
    part_cotangent = dealt[:, width : 2 * width]
    gains = dealt[:, 3 * width :].reshape(dp, micro, 2 * block)
    attn_gain_f = turned(gains[:, 0, :block].reshape(1, width)).astype(f32)
    moe_gain_f = turned(gains[:, 1, :block].reshape(1, width)).astype(f32)

    def head_gain(cut):
        return cut.reshape(dp, heads, head_part).transpose(1, 0, 2).reshape(local).astype(f32)

    query_scale = head_gain(gains[:, 0, block : block + head_cut])
    key_scale = head_gain(gains[:, 0, block + head_cut : block + 2 * head_cut])
    own_tokens = spread(part_tokens, "tensor").reshape(own, width)

    pair_cotangent = in_order(first, part_cotangent, dealt[:, 2 * width : 3 * width])
    pair_cotangent = pair_cotangent.reshape(2 * part, width)
    pair_cotangent = lax.all_gather(pair_cotangent, "tensor", axis=0, tiled=True)
    pair_cotangent = pair_cotangent.reshape(te, 2, part, width).transpose(1, 0, 2, 3)
    pair_cotangent = pair_cotangent.reshape(2 * own, width)

    seq_ends = jnp.cumsum(lengths, axis=1)
    seq_starts = seq_ends - lengths

    def start_of(place, ends, starts):
        inside = (place[..., None] >= starts) & (place[..., None] < ends)
        return jnp.sum(jnp.where(inside, starts, 0), axis=-1)

    own_place = lax.dynamic_index_in_dim(place_of, me, axis=1, keepdims=False)
    own_start = start_of(own_place, seq_ends[:, None, :], seq_starts[:, None, :])
    position = (own_place - own_start).astype(f32)
    cosine, sine = rope_tables(position.reshape(own))
    pair_micro = me // (heads * quarters)
    quarter = me % quarters
    key_place = lax.dynamic_index_in_dim(place_of, pair_micro, axis=0, keepdims=False)
    query_place = lax.dynamic_slice_in_dim(
        key_place, quarter * (block // quarters), block // quarters, axis=1
    ).reshape(-1, 1)
    pair_ends = lax.dynamic_index_in_dim(seq_ends, pair_micro, axis=0)
    pair_starts = lax.dynamic_index_in_dim(seq_starts, pair_micro, axis=0)
    query_start = start_of(query_place, pair_ends[None], pair_starts[None])
    key_place = key_place.reshape(1, -1)

    hot = routes[..., None] == jnp.arange(expert_count, dtype=jnp.int32)
    dense = jnp.sum(jnp.where(hot, gates[..., None], 0.0), axis=2)
    own_slot_hot = lax.dynamic_index_in_dim(slot_hot, me, axis=1, keepdims=False)
    share = jnp.einsum(
        "msj,mje->mse", own_slot_hot.astype(f32), dense, precision=lax.Precision.HIGHEST
    )
    share = share.reshape(micro, ranks, dp, expert_count).transpose(1, 2, 0, 3)
    share = share.reshape(own, expert_count)
    scales = jnp.concatenate([query_scale, key_scale])[None]
    own_tokens, cosine, sine, scales, key_place, query_place, query_start = (
        lax.optimization_barrier(
            (own_tokens, cosine, sine, scales, key_place, query_place, query_start)
        )
    )
    normed_b, pre, value_b, squares = project(own_tokens, attn_gain_f, attn_w)
    moe_sent, share, _ = lax.optimization_barrier((moe_sent, share, squares))
    moe_got, share_got = swap(moe_sent), swap(share)
    sent, factors = pack(spread(squares, "tensor"), pre, value_b, cosine, sine, scales)
    moe_local = in_order(first, moe_kept, moe_got).reshape(2 * block, -1)
    share = in_order(first, share, share_got).reshape(2 * own, expert_count)
    share = lax.dynamic_slice_in_dim(share, pair * (expert_count // 2), expert_count // 2, axis=1)
    packed = exchange(sent, DP)
    moe_local = lax.optimization_barrier((moe_local, packed))[0]
    moe_w = lax.all_gather(moe_local, "line", axis=0, tiled=True)
    pair_mixed, log_total = attention(packed, key_place, query_place, query_start)
    mixed_b, attn_out = project_out(exchange(pair_mixed, DP), attn_w)

    def terms_of(value):
        return exchange(value.reshape(te, part, width), "tensor")

    hidden_one, moe_factor, moe_in = before_experts(
        terms_of(attn_out), part_tokens, moe_gain_f
    )

    moe_in = exchange(moe_in, PAIR_TENSOR)
    out_kept, out_sent, moe_grad_part, moe_grads = experts(
        my_te, moe_in, pair_cotangent, share, moe_w, lines
    )
    moe_grads = lax.psum_scatter(moe_grads, "line", scatter_dimension=0, tiled=False)
    moe_grad_terms = exchange(moe_grad_part, PAIR_TENSOR)
    delta_one, delta_attn, grad_moe_gain = after_experts(
        moe_grad_terms, hidden_one, moe_factor, moe_gain_f, part_cotangent
    )
    delta_attn = exchange(delta_attn, "tensor").reshape(own, width)
    def across(value, partner):
        return lax.ppermute(value, "tensor", [(k, partner(k)) for k in range(te)])

    out_sent = lax.optimization_barrier((out_sent, delta_attn))[0]
    out_got = across(out_sent, lambda k: 2 * (3 - k // 2) + k % 2)

    pair_delta = exchange(project_out_back(delta_attn, attn_w), DP)
    pair_grads = attention_back(
        packed, key_place, query_place, query_start, log_total, pair_delta
    )
    pair_grads, out_got, moe_grads = lax.optimization_barrier((pair_grads, out_got, moe_grads))
    out_kept, out_sent = halve(my_te // 2 % 2, out_kept, out_got)
    out_got = across(out_sent, lambda k: k ^ 2)
    got, out_got, moe_grads = lax.optimization_barrier(
        (exchange(pair_grads, DP), out_got, moe_grads)
    )
    out_terms = quarter_terms(my_te % 2, pair, out_kept, out_got)
    out_terms = (
        out_terms[0],
        swap(out_terms[1]),
        across(out_terms[2], lambda k: k ^ 1),
        lax.ppermute(
            out_terms[3], PAIR_TENSOR, [(k, (k + te) % (2 * te) ^ 1) for k in range(2 * te)]
        ),
    )
    weighted, delta_value, inner, gain_grads = unpack(got, pre, factors, cosine, sine, scales)
    inner, moe_grads = lax.optimization_barrier((spread(inner, "tensor"), moe_grads))
    low_lanes, high_lanes = moe_grads[:, :block], moe_grads[:, block:]
    grads_kept = jnp.where(first, low_lanes, high_lanes)
    grads_got = swap(jnp.where(first, high_lanes, low_lanes))
    delta_pre, attn_grad = project_back(inner, weighted, pre, factors, delta_value, attn_w)
    attn_grad, out_terms = lax.optimization_barrier((attn_grad, out_terms))
    attn_grad_terms = terms_of(attn_grad)
    attn_grads = attention_grads(
        normed_b, lax.optimization_barrier((delta_pre, attn_grad))[0], delta_attn, mixed_b
    )
    attn_grads = lax.psum_scatter(attn_grads, "line", scatter_dimension=0, tiled=False)
    low_rows, high_rows = attn_grads[:block], attn_grads[block:]
    attn_grads = jnp.where(first, low_rows, high_rows).astype(f32) + swap(
        jnp.where(first, high_rows, low_rows)
    ).astype(f32)

    home = finish(
        micro,
        attn_grad_terms,
        part_tokens,
        attn_gain_f,
        delta_one,
        hidden_one,
        *out_terms,
        grad_moe_gain,
        gain_grads,
    )
    home, grads_got = lax.optimization_barrier((home, grads_got))
    home, attn_grads = lax.optimization_barrier(
        (exchange(home.reshape(te * dp, micro, -1), ("tensor",) + DP), attn_grads)
    )
    output, input_grad, gain_sum, head_gain_grads = deliver(
        my_te, home, home_hot
    )
    output = output.reshape(micro, block, width)
    input_grad = input_grad.reshape(micro, block, width)

    gate_grad, up_grad, down_grad = expert_gradients(pair, grads_kept, grads_got)
    return (
        output,
        input_grad,
        gain_sum[0],
        attn_grads[:, :local],
        attn_grads[:, local : 2 * local],
        attn_grads[:, 2 * local : 3 * local],
        head_gain_grads[0, :head_cut].reshape(heads, head_part),
        head_gain_grads[0, head_cut : 2 * head_cut].reshape(heads, head_part),
        attn_grads[:, 3 * local :].T,
        gain_sum[1],
        gate_grad,
        up_grad,
        down_grad,
    )


def solution(mesh):
    lines = mesh.shape["dp"] // 2
    devices = mesh.devices.reshape(2, lines, mesh.shape["tensor"])
    placed = (
        P(None, DP, None),
        P(None, DP, None),
        P(),
        P(),
        P(None, DP, None),
        P(None, DP, None),
        P(DP),
        P(DP, "tensor"),
        P(DP, "tensor"),
        P(DP, "tensor"),
        P("tensor", DP),
        P("tensor", DP),
        P("tensor", DP),
        P(DP),
        P(None, DP, "tensor"),
        P(None, DP, "tensor"),
        P(None, "tensor", DP),
    )
    return jax.shard_map(
        body,
        mesh=Mesh(devices, DP + ("tensor",)),
        in_specs=placed,
        out_specs=(
            P(None, DP, None),
            P(None, DP, None),
            P(DP),
            P(DP, "tensor"),
            P(DP, "tensor"),
            P(DP, "tensor"),
            P("tensor", DP),
            P("tensor", DP),
            P("tensor", DP),
            P(DP),
            P(None, DP, "tensor"),
            P(None, DP, "tensor"),
            P(None, "tensor", DP),
        ),
        check_vma=False,
    )
```

```python
import jax
import jax.numpy as jnp
from jax import lax
from jax.experimental import pallas as pl
from jax.experimental.pallas import tpu as pltpu
from jax.sharding import Mesh
from jax.sharding import PartitionSpec as P

HEAD = 128
MIB = 1024 * 1024
bf16 = jnp.bfloat16
f32 = jnp.float32

DP = ("pair", "line")
PAIR_TENSOR = ("pair", "tensor")

RANKS = 8

epsilon = 1e-05
rope_base = 10000.0


def rope_tables(position):
    half_dim = HEAD // 2
    frequency = rope_base ** (-(jnp.arange(half_dim, dtype=f32) * 2.0 / HEAD))
    angle = position[:, None] * frequency[None, :]
    cosine = jnp.concatenate([jnp.cos(angle), jnp.cos(angle)], axis=-1)
    sine = jnp.concatenate([jnp.sin(angle), jnp.sin(angle)], axis=-1)
    return (cosine, sine)


def norm_factor(values):
    return lax.rsqrt(jnp.mean(values * values, axis=-1, keepdims=True) + epsilon)


def norm_back(values, factor, gain, gradient):
    gained = gradient * gain
    inner_sum = jnp.sum(gained * values, axis=-1, keepdims=True)
    return factor * gained - values * (factor * factor * factor) * inner_sum / values.shape[-1]


def dot_nn(left_side, right_side):
    return jnp.dot(left_side, right_side, preferred_element_type=f32)


def dot_tn(left_side, right_side):
    return lax.dot_general(
        left_side, right_side, (((0,), (0,)), ((), ())), preferred_element_type=f32
    )


def dot_nt(left_side, right_side):
    return lax.dot_general(
        left_side, right_side, (((1,), (1,)), ((), ())), preferred_element_type=f32
    )


def exchange(value, axis):
    return lax.all_to_all(value, axis, split_axis=0, concat_axis=0, tiled=True)


def swap(value):
    return lax.ppermute(value, "pair", [(0, 1), (1, 0)])


def in_order(first, mine, other, axis=0):
    return jnp.stack([jnp.where(first, mine, other), jnp.where(first, other, mine)], axis=axis)


def turned(values):
    cut = values.reshape(values.shape[:-1] + (2, -1, HEAD))
    return jnp.swapaxes(cut, -3, -2).reshape(values.shape)


def spread(value, axis):
    count = lax.axis_size(axis)
    copies = jnp.broadcast_to(value[None], (count,) + value.shape)
    return exchange(copies, axis)


BLOCK = 512

IN_VMEM = pl.BlockSpec(memory_space=pltpu.VMEM)
IN_HBM = pl.BlockSpec(memory_space=pltpu.HBM)

KEYS = slice(0, 128)
VALUES = slice(128, 256)
QUERIES = slice(256, 288)
Q_BLOCKS = 4

MICRO = 2
HEADS = 2
QUARTERS = 4


def seen(sources, part):
    return slice(0, min(sources, (part + 1) * Q_BLOCKS) * 128)


def masked_scores(query, keys, key_place, query_place, query_start):
    scores = dot_nt(query, keys) * (HEAD ** (-0.5))
    visible = (key_place <= query_place) & (key_place >= query_start)
    return jnp.where(visible, scores, -1e30)


def attention_kernel(packed, key_place, query_place, query_start, mixed, log_total):
    sources = packed.shape[0]
    keys = packed[:, KEYS, :].reshape(sources * 128, HEAD)
    values = packed[:, VALUES, :].reshape(sources * 128, HEAD)
    for part in range(sources // Q_BLOCKS):
        blocks = slice(part * Q_BLOCKS, (part + 1) * Q_BLOCKS)
        rows = slice(part * Q_BLOCKS * 32, (part + 1) * Q_BLOCKS * 32)
        query = packed[blocks, QUERIES, :].reshape(Q_BLOCKS * 32, HEAD)
        past = seen(sources, part)
        scores = masked_scores(
            query, keys[past], key_place[:, past], query_place[rows, :], query_start[rows, :]
        )
        peak = jnp.max(scores, axis=-1, keepdims=True)
        weights = jnp.exp(scores - peak)
        total = jnp.sum(weights, axis=-1, keepdims=True)
        probs = (weights / total).astype(bf16)
        mixed[blocks, :, :] = (
            dot_nn(probs, values[past]).astype(bf16).reshape(Q_BLOCKS, 32, HEAD)
        )
        log_total[rows, :] = peak + jnp.log(total)


def attention_back_kernel(
    packed, key_place, query_place, query_start, log_total, delta_mixed, out, key_sum, value_sum
):
    sources = packed.shape[0]
    keys = packed[:, KEYS, :].reshape(sources * 128, HEAD)
    values = packed[:, VALUES, :].reshape(sources * 128, HEAD)
    scale = HEAD ** (-0.5)
    for part in reversed(range(sources // Q_BLOCKS)):
        blocks = slice(part * Q_BLOCKS, (part + 1) * Q_BLOCKS)
        rows = slice(part * Q_BLOCKS * 32, (part + 1) * Q_BLOCKS * 32)
        query = packed[blocks, QUERIES, :].reshape(Q_BLOCKS * 32, HEAD)
        delta = delta_mixed[blocks, :, :].reshape(Q_BLOCKS * 32, HEAD)
        past = seen(sources, part)
        scores = masked_scores(
            query, keys[past], key_place[:, past], query_place[rows, :], query_start[rows, :]
        )
        probs = jnp.exp(scores - log_total[rows, :])
        delta_probs = dot_nt(delta, values[past])
        inner = jnp.sum(probs * delta_probs, axis=-1, keepdims=True)
        delta_scores = (probs * (delta_probs - inner)).astype(bf16)
        out[blocks, QUERIES, :] = (
            (dot_nn(delta_scores, keys[past]) * scale).astype(bf16).reshape(Q_BLOCKS, 32, HEAD)
        )
        key_term = dot_tn(delta_scores, query)
        value_term = dot_tn(probs.astype(bf16), delta)
        if part == sources // Q_BLOCKS - 1:
            key_sum[...] = key_term
            value_sum[...] = value_term
        else:
            key_sum[past, :] += key_term
            value_sum[past, :] += value_term
    out[:, KEYS, :] = (key_sum[...] * scale).astype(bf16).reshape(sources, 128, HEAD)
    out[:, VALUES, :] = value_sum[...].astype(bf16).reshape(sources, 128, HEAD)


def attention(packed, key_place, query_place, query_start):
    sources = packed.shape[0]
    return pl.pallas_call(
        attention_kernel,
        out_shape=(
            jax.ShapeDtypeStruct((sources, 32, HEAD), bf16),
            jax.ShapeDtypeStruct((sources * 32, 1), f32),
        ),
        compiler_params=pltpu.CompilerParams(vmem_limit_bytes=40 * MIB),
        name="attention",
    )(packed, key_place, query_place, query_start)


def attention_back(packed, key_place, query_place, query_start, log_total, delta_mixed):
    sources = packed.shape[0]
    return pl.pallas_call(
        attention_back_kernel,
        out_shape=jax.ShapeDtypeStruct(packed.shape, bf16),
        scratch_shapes=[
            pltpu.VMEM((sources * 128, HEAD), f32),
            pltpu.VMEM((sources * 128, HEAD), f32),
        ],
        compiler_params=pltpu.CompilerParams(vmem_limit_bytes=40 * MIB),
        name="attention_back",
    )(packed, key_place, query_place, query_start, log_total, delta_mixed)


def order_hot(count, micro, forward):
    part = count // micro
    row = lax.broadcasted_iota(jnp.int32, (count, count), 0)
    column = lax.broadcasted_iota(jnp.int32, (count, count), 1)
    if not forward:
        row, column = column, row
    return jnp.where(column == micro * (row % part) + row // part, 1.0, 0.0).astype(bf16)


def reordered(values, micro, forward):
    return dot_nn(order_hot(values.shape[0], micro, forward), values).astype(bf16)


def half_signs(shape):
    return lax.broadcasted_iota(jnp.int32, shape, 1) < HEAD // 2


def row_sums(values):
    return jnp.sum(values.T, axis=0, keepdims=True)


def as_columns(row):
    return jnp.broadcast_to(row, (HEAD, row.shape[1])).T


def head_lanes(head):
    return slice(head * HEAD, (head + 1) * HEAD)


def pair_index(micro_index, head, quarter):
    return (micro_index * HEADS + head) * QUARTERS + quarter


def project_kernel(tokens, gain, stored, normed, pre, value, squares, weights, semaphore):
    copies = load_lines(stored, slice(0, 3), weights, semaphore)
    values = tokens[...].astype(f32)
    rows = (values * norm_factor(values) * gain[...]).astype(bf16)
    rows = reordered(rows, MICRO, True)
    normed[...] = rows
    local = value.shape[1]
    for copy in copies:
        copy.wait()
    width = rows.shape[1]
    sums = []
    for k in range(2):
        values = dot_nn(rows, weights[:, k].reshape(width, local))
        pre[:, k * local : (k + 1) * local] = values
        sums.append(row_sums(values * values))
    value[...] = dot_nn(rows, weights[:, 2].reshape(width, local)).astype(bf16)
    squares[...] = jnp.concatenate(sums, axis=0)


def project(tokens, gain, weights):
    count, width = tokens.shape
    lines, _, rows, local = weights.shape
    return pl.pallas_call(
        project_kernel,
        in_specs=[IN_VMEM, IN_VMEM, IN_HBM],
        scratch_shapes=[pltpu.VMEM((lines, 3, rows, local), bf16), pltpu.SemaphoreType.DMA((lines,))],
        out_specs=[IN_VMEM] * 4,
        out_shape=(
            jax.ShapeDtypeStruct((count, width), bf16),
            jax.ShapeDtypeStruct((count, 2 * local), f32),
            jax.ShapeDtypeStruct((count, local), bf16),
            jax.ShapeDtypeStruct((2, count), f32),
        ),
        compiler_params=pltpu.CompilerParams(vmem_limit_bytes=60 * MIB),
        name="project",
    )(tokens, gain, weights)


def pack_kernel(squares, pre, value, cosine, sine, scales, packed, factors):
    count, local = value.shape
    block = count // MICRO
    total = summed(squares)
    factor = lax.rsqrt(total / (local * squares.shape[0]) + epsilon)
    low = half_signs((count, HEAD))
    signed_sine = jnp.where(low, -sine[...], sine[...])
    columns = [as_columns(factor[k : k + 1]) for k in range(2)]
    factors[...] = jnp.concatenate(columns, axis=1)
    for head in range(HEADS):
        turned_heads = []
        for k in range(2):
            lanes = slice(k * local + head * HEAD, k * local + (head + 1) * HEAD)
            values = pre[:, lanes] * columns[k] * scales[:, lanes]
            rotated = values * cosine[...] + pltpu.roll(values, HEAD // 2, 1) * signed_sine
            turned_heads.append(rotated.astype(bf16))
        query, key = turned_heads
        for m in range(MICRO):
            rows = slice(m * block, (m + 1) * block)
            for quarter in range(QUARTERS):
                index = pair_index(m, head, quarter)
                start = m * block + quarter * block // QUARTERS
                packed[index, KEYS, :] = key[rows]
                packed[index, VALUES, :] = value[rows, head_lanes(head)]
                packed[index, QUERIES, :] = query[start : start + block // QUARTERS]


def pack(squares, pre, value, cosine, sine, scales):
    count, local = value.shape
    rows = (2 * QUARTERS + 1) * (count // MICRO // QUARTERS)
    return pl.pallas_call(
        pack_kernel,
        in_specs=[IN_VMEM] * 6,
        out_specs=[IN_VMEM] * 2,
        out_shape=(
            jax.ShapeDtypeStruct((MICRO * HEADS * QUARTERS, rows, HEAD), bf16),
            jax.ShapeDtypeStruct((count, 2 * HEAD), f32),
        ),
        compiler_params=pltpu.CompilerParams(vmem_limit_bytes=24 * MIB),
        name="pack",
    )(squares, pre, value, cosine, sine, scales)


def from_quarters(arrived, head):
    return jnp.concatenate(
        [
            arrived[pair_index(m, head, quarter)]
            for m in range(MICRO)
            for quarter in range(QUARTERS)
        ],
        axis=0,
    )


def project_out_kernel(arrived, stored, mixed, out, weights, semaphore):
    copies = load_lines(stored, 3, weights, semaphore)
    rows = jnp.concatenate([from_quarters(arrived, head) for head in range(HEADS)], axis=1)
    rows = reordered(rows, MICRO, False)
    mixed[...] = rows
    for copy in copies:
        copy.wait()
    out[...] = dot_nt(rows, weights[...].reshape(out.shape[1], rows.shape[1])).astype(bf16)


def project_out(arrived, weights):
    lines, _, rows, local = weights.shape
    count = arrived.shape[0] * arrived.shape[1] // HEADS
    return pl.pallas_call(
        project_out_kernel,
        in_specs=[IN_VMEM, IN_HBM],
        scratch_shapes=[pltpu.VMEM((lines, rows, local), bf16), pltpu.SemaphoreType.DMA((lines,))],
        out_specs=[IN_VMEM] * 2,
        out_shape=(
            jax.ShapeDtypeStruct((count, local), bf16),
            jax.ShapeDtypeStruct((count, lines * rows), bf16),
        ),
        compiler_params=pltpu.CompilerParams(vmem_limit_bytes=60 * MIB),
        name="project_out",
    )(arrived, weights)


def project_out_back_kernel(delta, stored, out, weights, semaphore):
    for copy in load_lines(stored, 3, weights, semaphore):
        copy.wait()
    rows = dot_nn(delta[...], weights[...].reshape(delta.shape[1], -1)).astype(bf16)
    rows = reordered(rows, MICRO, True)
    step = out.shape[1]
    block = rows.shape[0] // MICRO
    for m in range(MICRO):
        for head in range(HEADS):
            for quarter in range(QUARTERS):
                start = m * block + quarter * step
                out[pair_index(m, head, quarter)] = rows[start : start + step, head_lanes(head)]


def project_out_back(delta, weights):
    count = delta.shape[0]
    lines, _, rows, local = weights.shape
    devices = MICRO * HEADS * QUARTERS
    return pl.pallas_call(
        project_out_back_kernel,
        in_specs=[IN_VMEM, IN_HBM],
        scratch_shapes=[
            pltpu.VMEM((lines, rows, local), bf16),
            pltpu.SemaphoreType.DMA((lines,)),
        ],
        out_specs=IN_VMEM,
        out_shape=jax.ShapeDtypeStruct((devices, count * HEADS // devices, HEAD), bf16),
        compiler_params=pltpu.CompilerParams(vmem_limit_bytes=60 * MIB),
        name="project_out_back",
    )(delta, weights)


def unpack_kernel(
    arrived, pre, factors, cosine, sine, scales, weighted, delta_value, inner, gain_grads
):
    count, local = delta_value.shape
    low = half_signs((count, HEAD))
    signs = jnp.where(low, 1.0, -1.0)
    products = [None, None]
    for head in range(HEADS):
        sums = []
        for rows in (KEYS, VALUES):
            parts = []
            for m in range(MICRO):
                total = arrived[pair_index(m, head, 0), rows, :].astype(f32)
                for quarter in range(1, QUARTERS):
                    total = total + arrived[pair_index(m, head, quarter), rows, :].astype(f32)
                parts.append(total)
            sums.append(jnp.concatenate(parts, axis=0))
        delta_key, value = sums
        delta_value[:, head_lanes(head)] = value.astype(bf16)
        delta_query = jnp.concatenate(
            [
                arrived[pair_index(m, head, quarter), QUERIES, :]
                for m in range(MICRO)
                for quarter in range(QUARTERS)
            ],
            axis=0,
        ).astype(f32)
        for k, gradient in ((0, delta_query), (1, delta_key)):
            lanes = slice(k * local + head * HEAD, k * local + (head + 1) * HEAD)
            scaled = pltpu.roll(gradient * sine[...], HEAD // 2, 1) * signs
            normed_gradient = gradient * cosine[...] + scaled
            values = pre[:, lanes]
            gain_grads[:, lanes] = jnp.sum(
                normed_gradient * values * factors[:, head_lanes(k)], axis=0, keepdims=True
            )
            gained = normed_gradient * scales[:, lanes]
            weighted[:, lanes] = gained
            product = gained * values
            products[k] = product if head == 0 else products[k] + product
    inner[...] = jnp.concatenate([row_sums(product) for product in products], axis=0)


def unpack(arrived, pre, factors, cosine, sine, scales):
    count, lanes = pre.shape
    return pl.pallas_call(
        unpack_kernel,
        in_specs=[IN_VMEM] * 6,
        out_specs=[IN_VMEM] * 4,
        out_shape=(
            jax.ShapeDtypeStruct((count, lanes), f32),
            jax.ShapeDtypeStruct((count, lanes // 2), bf16),
            jax.ShapeDtypeStruct((2, count), f32),
            jax.ShapeDtypeStruct((1, lanes), f32),
        ),
        compiler_params=pltpu.CompilerParams(vmem_limit_bytes=24 * MIB),
        name="unpack",
    )(arrived, pre, factors, cosine, sine, scales)


def project_back_kernel(
    inner, weighted, pre, factors, value, stored, delta_pre, out, weights, semaphore
):
    local = value.shape[1]
    copies = load_lines(stored, slice(0, 3), weights, semaphore)
    total = summed(inner) / (local * inner.shape[0])
    for k in range(2):
        factor = factors[:, head_lanes(k)]
        column = factor * factor * factor * as_columns(total[k : k + 1])
        for head in range(HEADS):
            lanes = slice(k * local + head * HEAD, k * local + (head + 1) * HEAD)
            delta_pre[:, lanes] = (factor * weighted[:, lanes] - pre[:, lanes] * column).astype(
                bf16
            )
    delta_pre[:, 2 * local :] = value[...]
    rows = reordered(delta_pre[...], MICRO, False)
    for copy in copies:
        copy.wait()
    lines, _, step, _ = weights.shape
    for line in range(lines):
        chunk = jnp.concatenate([weights[line, k] for k in range(3)], axis=1)
        out[:, line * step : (line + 1) * step] = dot_nt(rows, chunk).astype(bf16)


def project_back(inner, weighted, pre, factors, value, weights):
    count = value.shape[0]
    lines, _, rows, local = weights.shape
    return pl.pallas_call(
        project_back_kernel,
        in_specs=[IN_VMEM] * 5 + [IN_HBM],
        scratch_shapes=[
            pltpu.VMEM((lines, 3, rows, local), bf16),
            pltpu.SemaphoreType.DMA((lines,)),
        ],
        out_specs=[IN_VMEM] * 2,
        out_shape=(
            jax.ShapeDtypeStruct((count, 3 * local), bf16),
            jax.ShapeDtypeStruct((count, lines * rows), bf16),
        ),
        compiler_params=pltpu.CompilerParams(vmem_limit_bytes=60 * MIB),
        name="project_back",
    )(inner, weighted, pre, factors, value, weights)


def load(source, target, semaphore):
    copy = pltpu.make_async_copy(source, target, semaphore)
    copy.start()
    return copy


def load_lines(stored, matrices, target, semaphores):
    return [
        load(stored.at[line, matrices], target.at[line], semaphores.at[line])
        for line in range(target.shape[0])
    ]


def attention_grads_kernel(normed, delta_pre, delta_attn, mixed, out):
    lines = out.shape[0]
    pre_width = delta_pre.shape[1]
    for line in range(lines):
        lanes = slice(2 * line * HEAD, 2 * (line + 1) * HEAD)
        out[line, :, :pre_width] = dot_tn(normed[:, lanes], delta_pre[...]).astype(bf16)
        out[line, :, pre_width:] = dot_tn(delta_attn[:, lanes], mixed[...]).astype(bf16)


def attention_grads(normed, delta_pre, delta_attn, mixed):
    lines = normed.shape[1] // HEAD // 2
    return pl.pallas_call(
        attention_grads_kernel,
        out_shape=jax.ShapeDtypeStruct(
            (lines, 2 * HEAD, delta_pre.shape[1] + mixed.shape[1]), bf16
        ),
        compiler_params=pltpu.CompilerParams(vmem_limit_bytes=24 * MIB),
        name="attention_grads",
    )(normed, delta_pre, delta_attn, mixed)


def stack_attention_kernel(w_query, w_key, w_value, w_out, out):
    out[0] = w_query[...]
    out[1] = w_key[...]
    out[2] = w_value[...]
    out[3] = w_out[...].T


def stack_attention(w_query, w_key, w_value, w_out):
    return pl.pallas_call(
        stack_attention_kernel,
        out_shape=jax.ShapeDtypeStruct((4,) + w_query.shape, bf16),
        name="stack_attention",
    )(w_query, w_key, w_value, w_out)


def stack_experts_kernel(pair, w_gate, w_up, w_down, kept, sent):
    half = w_gate.shape[0] // 2
    each = BLOCK // HEAD
    for out, which in ((kept, pair[0]), (sent, 1 - pair[0])):
        for expert in range(half):
            for index, stored in enumerate((w_gate, w_up, w_down)):
                start = expert // each * 3 * BLOCK + index * BLOCK + expert % each * HEAD
                value = stored[which * half + expert]
                out[:, start : start + HEAD] = value.T if stored is w_down else value


def stack_experts(pair, w_gate, w_up, w_down):
    count, rows, hidden = w_gate.shape
    shape = jax.ShapeDtypeStruct((rows, 3 * count * hidden // 2), bf16)
    return pl.pallas_call(
        stack_experts_kernel,
        in_specs=[pl.BlockSpec(memory_space=pltpu.SMEM)]
        + [pl.BlockSpec(memory_space=pltpu.VMEM)] * 3,
        out_shape=(shape, shape),
        compiler_params=pltpu.CompilerParams(vmem_limit_bytes=24 * MIB),
        name="stack_experts",
    )(pair.reshape(1), w_gate, w_up, w_down)


def experts_kernel(my_rank, arrived, upstream, gates, weights, *refs):
    (
        out_kept,
        out_sent,
        delta_in,
        grads,
        held,
        hidden_all,
        deltas_all,
        grads_out,
        out_all,
        rows,
        in_sem,
        out_sem,
    ) = refs
    steps = held.shape[0]
    width = upstream.shape[1]
    lines = grads.shape[0]
    lane_part = width // lines
    part = out_kept.shape[2]
    loads = [
        pltpu.make_async_copy(
            weights.at[:, pl.ds(c * 3 * BLOCK, 3 * BLOCK)], held.at[c], in_sem.at[c]
        )
        for c in range(steps)
    ]
    for load in loads:
        load.start()
    for k in range(arrived.shape[0]):
        rows[k * part : (k + 1) * part, :] = from_blocks(arrived.at[k])
    stores = []
    for c in range(steps):
        loads[c].wait()
        gate_up = dot_nn(rows[...], held[c, :, 0 : 2 * BLOCK])
        gate_h, up_h = gate_up[:, :BLOCK], gate_up[:, BLOCK:]
        delta_hidden = dot_nn(upstream[...], held[c, :, 2 * BLOCK : 3 * BLOCK])
        share = jnp.concatenate(
            [
                jnp.broadcast_to(gates[:, e : e + 1], (gates.shape[0], HEAD))
                for e in range(c * BLOCK // HEAD, (c + 1) * BLOCK // HEAD)
            ],
            axis=1,
        )
        sigmoid_gate = 1.0 / (1.0 + jnp.exp(-gate_h))
        active = gate_h * sigmoid_gate
        hidden = (active * up_h * share).astype(bf16)
        delta_hidden = delta_hidden * share
        delta_gate = (
            delta_hidden * up_h * sigmoid_gate * (1.0 + gate_h * (1.0 - sigmoid_gate))
        ).astype(bf16)
        delta_up = (delta_hidden * active).astype(bf16)
        start = 2 * c * BLOCK
        hidden_all[:, c * BLOCK : (c + 1) * BLOCK] = hidden
        deltas_all[:, start : start + BLOCK] = delta_gate
        deltas_all[:, start + BLOCK : start + 2 * BLOCK] = delta_up
        deltas = deltas_all[:, start : start + 2 * BLOCK]
        slot = c % 2
        if c >= 2:
            stores[c - 2].wait()
        for n in range(lines):
            lanes = slice(n * lane_part, (n + 1) * lane_part)
            grads_out[slot, n, 0 : 2 * BLOCK, :] = dot_tn(deltas, rows[:, lanes]).astype(bf16)
            grads_out[slot, n, 2 * BLOCK :, :] = dot_tn(hidden, upstream[:, lanes]).astype(bf16)
        store = pltpu.make_async_copy(
            grads_out.at[slot], grads.at[:, pl.ds(c * 3 * BLOCK, 3 * BLOCK), :], out_sem.at[slot]
        )
        store.start()
        stores.append(store)
    for n in range(lines):
        lanes = slice(n * lane_part, (n + 1) * lane_part)
        gate_up = jnp.concatenate(
            [held[c, lanes, 0 : 2 * BLOCK] for c in range(steps)], axis=1
        )
        produced = dot_nt(deltas_all[...], gate_up).astype(bf16)
        for k in range(2 * RANKS):
            for b in range(lane_part // HEAD):
                delta_in[k, n * (lane_part // HEAD) + b] = produced[
                    k * part : (k + 1) * part, b * HEAD : (b + 1) * HEAD
                ]
        down = jnp.concatenate(
            [held[c, lanes, 2 * BLOCK : 3 * BLOCK] for c in range(steps)], axis=1
        )
        produced = dot_nt(hidden_all[...], down).astype(bf16)
        out_all[:, :, lanes] = produced.reshape(2 * RANKS, part, lane_part)
    high = my_rank[0] // (RANKS // 2)
    for p in range(2):
        for q in range(RANKS // 2):
            out_kept[q, p] = out_all[p * RANKS + high * (RANKS // 2) + q]
            out_sent[q, p] = out_all[p * RANKS + (1 - high) * (RANKS // 2) + q]
    for store in stores[-2:]:
        store.wait()


def experts(my_rank, arrived, upstream, gates, weights, lines):
    count, width = upstream.shape
    part = count // RANKS // 2
    steps = weights.shape[1] // (3 * BLOCK)
    in_vmem = pl.BlockSpec(memory_space=pltpu.VMEM)
    in_hbm = pl.BlockSpec(memory_space=pl.ANY)
    return pl.pallas_call(
        experts_kernel,
        in_specs=[pl.BlockSpec(memory_space=pltpu.SMEM), in_vmem, in_vmem, in_vmem, in_hbm],
        out_specs=[in_vmem, in_vmem, in_vmem, in_hbm],
        out_shape=(
            *[jax.ShapeDtypeStruct((RANKS // 2, 2, part, width), bf16)] * 2,
            jax.ShapeDtypeStruct(arrived.shape, bf16),
            jax.ShapeDtypeStruct((lines, weights.shape[1], width // lines), bf16),
        ),
        scratch_shapes=[
            pltpu.VMEM((steps, width, 3 * BLOCK), bf16),
            pltpu.VMEM((count, steps * BLOCK), bf16),
            pltpu.VMEM((count, 2 * steps * BLOCK), bf16),
            pltpu.VMEM((2, lines, 3 * BLOCK, width // lines), bf16),
            pltpu.VMEM((2 * RANKS, part, width), bf16),
            pltpu.VMEM((count, width), bf16),
            pltpu.SemaphoreType.DMA((steps,)),
            pltpu.SemaphoreType.DMA((2,)),
        ],
        compiler_params=pltpu.CompilerParams(vmem_limit_bytes=56 * MIB),
        name="experts",
    )(my_rank.reshape(1), arrived, upstream, gates, weights)


def expert_gradients_kernel(pair, kept, got, gate_grad, up_grad, down_grad):
    half = gate_grad.shape[0] // 2
    each = BLOCK // HEAD
    for stored, which in ((kept, pair[0]), (got, 1 - pair[0])):
        for expert in range(half):
            for index, out in enumerate((gate_grad, up_grad, down_grad)):
                start = expert // each * 3 * BLOCK + index * BLOCK + expert % each * HEAD
                value = stored[start : start + HEAD].astype(f32)
                out[which * half + expert] = value if out is down_grad else value.T


def expert_gradients(pair, kept, got):
    count = 2 * kept.shape[0] // 3 // HEAD
    in_vmem = pl.BlockSpec(memory_space=pltpu.VMEM)
    shape = jax.ShapeDtypeStruct((count, kept.shape[1], HEAD), f32)
    return pl.pallas_call(
        expert_gradients_kernel,
        in_specs=[pl.BlockSpec(memory_space=pltpu.SMEM), in_vmem, in_vmem],
        out_shape=(shape, shape, shape),
        compiler_params=pltpu.CompilerParams(vmem_limit_bytes=24 * MIB),
        name="expert_gradients",
    )(pair.reshape(1), kept, got)


def summed(terms):
    total = terms[0].astype(f32)
    for k in range(1, terms.shape[0]):
        total = total + terms[k].astype(f32)
    return total


def put_blocks(out, rows):
    for block in range(out.shape[0]):
        out[block] = rows[:, block * HEAD : (block + 1) * HEAD]


def from_blocks(blocks):
    return jnp.concatenate([blocks[k] for k in range(blocks.shape[0])], axis=1)


def lane_blocks(width, forward):
    lines = width // HEAD // 2
    moves = [(p * lines + n, n * 2 + p) for p in range(2) for n in range(lines)]
    return moves if forward else [(b, a) for a, b in moves]


def move_lanes(values, forward):
    moves = sorted((b, a) for a, b in lane_blocks(values.shape[-1], forward))
    return jnp.concatenate([values[:, a * HEAD : (a + 1) * HEAD] for _, a in moves], axis=1)


def deal_kernel(
    where, places, stored_tokens, stored_cotangent, gains, out, tokens, cotangent, semaphores
):
    copies = [
        load(stored_tokens, tokens, semaphores.at[0]),
        load(stored_cotangent, cotangent, semaphores.at[1]),
    ]
    count, width = tokens.shape
    rows, block = places.shape
    given = places[...] - where[0] * block
    mine = (given >= 0) & (given < block)
    before = lax.broadcasted_iota(jnp.int32, (block, block), 0) < lax.broadcasted_iota(
        jnp.int32, (block, block), 1
    )
    rank = dot_nn(
        jnp.where(mine, 1.0, 0.0).astype(bf16), jnp.where(before, 1.0, 0.0).astype(bf16)
    ).astype(jnp.int32)
    hit = mine & (rank == where[1])
    order = jnp.sum(jnp.where(hit, given, 0), axis=1, keepdims=True)
    micro = lax.broadcasted_iota(jnp.int32, (rows, 1), 0) % (count // block)
    hot = order + micro * block == lax.broadcasted_iota(jnp.int32, (rows, count), 1)
    hot = jnp.where(hot, 1.0, 0.0).astype(bf16)
    copies[0].wait()
    token_rows = move_lanes(dot_nn(hot, tokens[...]).astype(bf16), True)
    copies[1].wait()
    gradient = move_lanes(dot_nn(hot, cotangent[...]).astype(bf16), True)
    odd = lax.broadcasted_iota(jnp.int32, (rows, gains.shape[1]), 0) % 2 == 1
    values = gains[...].astype(f32)
    beside = jnp.where(odd, values[1:2], values[0:1]).astype(bf16)
    partner = jnp.concatenate([gradient[rows // 2 :], gradient[: rows // 2]], axis=0)
    sent = jnp.concatenate([token_rows, gradient, partner, beside], axis=1)
    for chunk in range(out.shape[0]):
        out[chunk] = sent[chunk * out.shape[1] : (chunk + 1) * out.shape[1]]


def deal(where, places, tokens, cotangent, gains):
    width = tokens.shape[1]
    return pl.pallas_call(
        deal_kernel,
        in_specs=[pl.BlockSpec(memory_space=pltpu.SMEM), IN_VMEM, IN_HBM, IN_HBM, IN_VMEM],
        scratch_shapes=[
            pltpu.VMEM(tokens.shape, bf16),
            pltpu.VMEM(cotangent.shape, bf16),
            pltpu.SemaphoreType.DMA((2,)),
        ],
        out_shape=jax.ShapeDtypeStruct(
            (places.shape[0] // MICRO, MICRO, 3 * width + gains.shape[1]), bf16
        ),
        compiler_params=pltpu.CompilerParams(vmem_limit_bytes=60 * MIB),
        name="deal",
    )(where, places, tokens, cotangent, gains)


def before_experts_kernel(terms, tokens, gain, hidden_one, factor, moe_in):
    hidden = tokens[...].astype(f32) + summed(terms)
    scale = norm_factor(hidden)
    hidden_one[...] = hidden
    factor[...] = scale
    rows = (hidden * scale * gain[...]).astype(bf16)
    for k in range(moe_in.shape[0]):
        put_blocks(moe_in.at[k], rows)


def before_experts(terms, tokens, gain):
    rows, width = tokens.shape
    return pl.pallas_call(
        before_experts_kernel,
        in_specs=[IN_VMEM] * 3,
        out_specs=[IN_VMEM] * 3,
        out_shape=(
            jax.ShapeDtypeStruct((rows, width), f32),
            jax.ShapeDtypeStruct((rows, 1), f32),
            jax.ShapeDtypeStruct((2 * RANKS, width // HEAD, rows, HEAD), bf16),
        ),
        compiler_params=pltpu.CompilerParams(vmem_limit_bytes=24 * MIB),
        name="before_experts",
    )(terms, tokens, gain)


def after_experts_kernel(
    terms, hidden_one, factor, gain, upstream, delta_one, delta_attn, gain_grad
):
    gradient = from_blocks(summed(terms))
    hidden = hidden_one[...]
    gain_grad[...] = jnp.sum(gradient * hidden * factor[...], axis=0, keepdims=True)
    delta = upstream[...].astype(f32) + norm_back(hidden, factor[...], gain[...], gradient)
    delta_one[...] = delta
    for k in range(delta_attn.shape[0]):
        delta_attn[k] = delta.astype(bf16)


def after_experts(terms, hidden_one, factor, gain, upstream):
    rows, width = upstream.shape
    return pl.pallas_call(
        after_experts_kernel,
        in_specs=[IN_VMEM] * 5,
        out_specs=[IN_VMEM] * 3,
        out_shape=(
            jax.ShapeDtypeStruct((rows, width), f32),
            jax.ShapeDtypeStruct((RANKS, rows, width), bf16),
            jax.ShapeDtypeStruct((1, width), f32),
        ),
        compiler_params=pltpu.CompilerParams(vmem_limit_bytes=24 * MIB),
        name="after_experts",
    )(terms, hidden_one, factor, gain, upstream)


def halve_kernel(bit, kept, got, mine, sent):
    half = mine.shape[0]
    for out, start in ((mine, bit[0] * half), (sent, (1 - bit[0]) * half)):
        for k in range(half):
            total = kept[start + k].astype(f32) + got[start + k].astype(f32)
            out[k] = total.astype(out.dtype)


def halve(bit, kept, got):
    shape = (kept.shape[0] // 2,) + kept.shape[1:]
    in_vmem = pl.BlockSpec(memory_space=pltpu.VMEM)
    return pl.pallas_call(
        halve_kernel,
        in_specs=[pl.BlockSpec(memory_space=pltpu.SMEM), in_vmem, in_vmem],
        out_specs=[IN_VMEM] * 2,
        out_shape=(jax.ShapeDtypeStruct(shape, f32), jax.ShapeDtypeStruct(shape, bf16)),
        compiler_params=pltpu.CompilerParams(vmem_limit_bytes=24 * MIB),
        name="halve",
    )(bit.reshape(1), kept, got)


def quarter_terms_kernel(bits, kept, got, mine, other, across_mine, across_other):
    for out, y, p in (
        (mine, bits[0], bits[1]),
        (other, bits[0], 1 - bits[1]),
        (across_mine, 1 - bits[0], bits[1]),
        (across_other, 1 - bits[0], 1 - bits[1]),
    ):
        out[...] = (kept[y, p].astype(f32) + got[y, p].astype(f32)).astype(out.dtype)


def quarter_terms(y, pair, kept, got):
    rows, width = kept.shape[2:]
    in_vmem = pl.BlockSpec(memory_space=pltpu.VMEM)
    return pl.pallas_call(
        quarter_terms_kernel,
        in_specs=[pl.BlockSpec(memory_space=pltpu.SMEM), in_vmem, in_vmem],
        out_specs=[IN_VMEM] * 4,
        out_shape=(
            jax.ShapeDtypeStruct((rows, width), f32),
            *[jax.ShapeDtypeStruct((rows, width), bf16)] * 3,
        ),
        compiler_params=pltpu.CompilerParams(vmem_limit_bytes=24 * MIB),
        name="quarter_terms",
    )(jnp.stack([y, pair]), kept, got)


def finish_kernel(
    terms,
    tokens,
    gain,
    delta_one,
    hidden_one,
    out_mine,
    out_second,
    out_third,
    out_fourth,
    moe_gain_grad,
    head_gain_grads,
    home,
):
    width = tokens.shape[1]
    values = tokens[...].astype(f32)
    gradient = summed(terms)
    factor = norm_factor(values)
    gain_grad = jnp.sum(gradient * values * factor, axis=0, keepdims=True)
    moe_out = out_mine[...]
    for term in (out_second, out_third, out_fourth):
        moe_out = moe_out + term[...].astype(f32)
    output = move_lanes((hidden_one[...] + moe_out).astype(bf16), False)
    input_grad = delta_one[...] + norm_back(values, factor, gain[...], gradient)
    input_grad = move_lanes(input_grad.astype(bf16), False)
    rows = []
    for moved, _ in sorted(lane_blocks(width, False), key=lambda move: move[1]):
        lanes = slice(moved * HEAD, (moved + 1) * HEAD)
        rows.append(gain_grad[:, lanes])
        rows.append(moe_gain_grad[:, lanes])
    gains = jnp.concatenate(rows, axis=0).astype(bf16)
    micro = home.shape[2]
    head_part = HEAD // home.shape[1]
    shape = (tokens.shape[0], head_gain_grads.shape[1])
    row, lane = (lax.broadcasted_iota(jnp.int32, shape, k) for k in range(2))
    kept = (row % micro == 0) & (lane % HEAD // head_part == row // micro)
    kept = jnp.where(kept, head_gain_grads[...], 0.0).astype(bf16)
    shape = (shape[1], HEAD)
    source, lane = (lax.broadcasted_iota(jnp.int32, shape, k) for k in range(2))
    chosen = lane == source // HEAD * head_part + source % head_part
    head_gains = dot_nn(kept, jnp.where(chosen, 1.0, 0.0).astype(bf16)).astype(bf16)
    sent = jnp.concatenate([output, input_grad, gains, head_gains], axis=1)
    for source in range(home.shape[1]):
        piece = sent[source * micro : (source + 1) * micro]
        for k in range(home.shape[0]):
            home[k, source] = piece


def finish(micro, terms, tokens, *others):
    rows, width = tokens.shape
    shape = (RANKS, rows // micro, micro, 2 * width + 2 * HEAD)
    return pl.pallas_call(
        finish_kernel,
        in_specs=[IN_VMEM] * 11,
        out_specs=IN_VMEM,
        out_shape=jax.ShapeDtypeStruct(shape, bf16),
        compiler_params=pltpu.CompilerParams(vmem_limit_bytes=24 * MIB),
        name="finish",
    )(terms, tokens, *others)


def deliver_kernel(rank, arrived, hot, output, input_grad, gains, head_gains):
    count, width = output.shape
    rows = arrived[...].reshape(count, arrived.shape[2])
    output[...] = dot_nn(hot[...], rows[:, :width]).astype(bf16)
    input_grad[...] = dot_nn(hot[...], rows[:, width : 2 * width]).astype(bf16)
    terms = rows[:, 2 * width : 2 * width + HEAD].astype(f32)
    odd = lax.broadcasted_iota(jnp.int32, terms.shape, 0) % 2
    gains[...] = jnp.concatenate(
        [
            jnp.sum(jnp.where(odd == 0, terms, 0.0), axis=0, keepdims=True),
            jnp.sum(jnp.where(odd == 1, terms, 0.0), axis=0, keepdims=True),
        ],
        axis=0,
    )
    terms = rows[:, 2 * width + HEAD :].astype(f32)
    sender = lax.broadcasted_iota(jnp.int32, terms.shape, 0) // (count // RANKS)
    head_gains[...] = jnp.sum(jnp.where(sender == rank[0], terms, 0.0), axis=0, keepdims=True)


def deliver(rank, rows, hot):
    count, lanes = rows.shape[0] * rows.shape[1], rows.shape[2]
    in_vmem = pl.BlockSpec(memory_space=pltpu.VMEM)
    shape = jax.ShapeDtypeStruct((count, lanes // 2 - HEAD), bf16)
    return pl.pallas_call(
        deliver_kernel,
        in_specs=[pl.BlockSpec(memory_space=pltpu.SMEM), in_vmem, in_vmem],
        out_shape=(
            shape,
            shape,
            jax.ShapeDtypeStruct((2, HEAD), f32),
            jax.ShapeDtypeStruct((1, HEAD), f32),
        ),
        compiler_params=pltpu.CompilerParams(vmem_limit_bytes=24 * MIB),
        name="deliver",
    )(rank.reshape(1), rows, hot)


def body(
    tokens,
    cotangent,
    pack_perm,
    lengths,
    routes,
    gates,
    attn_gain,
    w_query,
    w_key,
    w_value,
    query_gain,
    key_gain,
    w_out,
    moe_gain,
    w_gate,
    w_up,
    w_down,
):
    pair = lax.axis_index("pair")
    first = pair == 0
    lines = lax.axis_size("line")
    dp = 2 * lines
    te = lax.axis_size("tensor")
    me = lax.axis_index(DP)
    my_te = lax.axis_index("tensor")
    micro, block, width = tokens.shape
    ranks = block // dp
    own = micro * block
    part = own // te
    local = w_query.shape[1]
    heads = local // HEAD
    head_part = HEAD // dp
    quarters = dp // (micro * heads)
    expert_count = w_gate.shape[0]

    attn_local = stack_attention(w_query, w_key, w_value, w_out)
    moe_kept, moe_sent = stack_experts(pair, w_gate, w_up, w_down)

    blocks = pack_perm.reshape(micro, dp, block)
    root = blocks // block
    earlier = jnp.arange(block)[None, :] < jnp.arange(block)[:, None]
    rank = jnp.sum(
        ((root[:, :, :, None] == root[:, :, None, :]) & earlier).astype(jnp.int32), axis=3
    )
    from_me = (root == me)[:, :, None, :] & (
        rank[:, :, None, :] == jnp.arange(ranks, dtype=jnp.int32)[None, None, :, None]
    )
    given = jnp.sum(jnp.where(from_me, (blocks - me * block)[:, :, None, :], 0), axis=3)
    given = given + (jnp.arange(micro, dtype=jnp.int32) * block)[:, None, None]
    row_index = jnp.arange(own, dtype=jnp.int32)
    home_order = given.transpose(2, 1, 0).reshape(own)
    home_hot = (row_index[:, None] == home_order[None, :]).astype(bf16)
    slot = rank * dp + root
    slot_hot = slot[:, :, None, :] == jnp.arange(block, dtype=jnp.int32)[None, None, :, None]
    place_in = jnp.sum(
        jnp.where(slot_hot, jnp.arange(block, dtype=jnp.int32)[None, None, None, :], 0), axis=3
    )
    place_of = place_in + (jnp.arange(dp, dtype=jnp.int32) * block)[None, :, None]

    head_cut = heads * head_part
    head_gains = jnp.concatenate(
        [
            query_gain.reshape(1, head_cut),
            key_gain.reshape(1, head_cut),
            jnp.zeros((1, block - 2 * head_cut), bf16),
        ],
        axis=1,
    )
    gains = jnp.concatenate(
        [
            jnp.concatenate([attn_gain[None], head_gains], axis=1),
            jnp.concatenate([moe_gain[None], head_gains], axis=1),
        ],
        axis=0,
    )
    dealt = deal(
        jnp.stack([me, my_te]),
        blocks.transpose(1, 0, 2).reshape(part, block),
        tokens.reshape(own, width),
        cotangent.reshape(own, width),
        gains,
    )
    attn_local = in_order(first, attn_local, swap(attn_local), 1).reshape(4, 2 * block, local)
    attn_local = lax.optimization_barrier((attn_local, dealt))[0]
    attn_w = lax.all_gather(attn_local, "line", axis=0)
    dealt = exchange(dealt, DP).reshape(part, -1)
    part_tokens = dealt[:, :width]
    part_cotangent = dealt[:, width : 2 * width]
    gains = dealt[:, 3 * width :].reshape(dp, micro, 2 * block)
    attn_gain_f = turned(gains[:, 0, :block].reshape(1, width)).astype(f32)
    moe_gain_f = turned(gains[:, 1, :block].reshape(1, width)).astype(f32)

    def head_gain(cut):
        return cut.reshape(dp, heads, head_part).transpose(1, 0, 2).reshape(local).astype(f32)

    query_scale = head_gain(gains[:, 0, block : block + head_cut])
    key_scale = head_gain(gains[:, 0, block + head_cut : block + 2 * head_cut])
    own_tokens = spread(part_tokens, "tensor").reshape(own, width)

    pair_cotangent = in_order(first, part_cotangent, dealt[:, 2 * width : 3 * width])
    pair_cotangent = pair_cotangent.reshape(2 * part, width)
    pair_cotangent = lax.all_gather(pair_cotangent, "tensor", axis=0, tiled=True)
    pair_cotangent = pair_cotangent.reshape(te, 2, part, width).transpose(1, 0, 2, 3)
    pair_cotangent = pair_cotangent.reshape(2 * own, width)

    seq_ends = jnp.cumsum(lengths, axis=1)
    seq_starts = seq_ends - lengths

    def start_of(place, ends, starts):
        inside = (place[..., None] >= starts) & (place[..., None] < ends)
        return jnp.sum(jnp.where(inside, starts, 0), axis=-1)

    own_place = lax.dynamic_index_in_dim(place_of, me, axis=1, keepdims=False)
    own_start = start_of(own_place, seq_ends[:, None, :], seq_starts[:, None, :])
    position = (own_place - own_start).astype(f32)
    cosine, sine = rope_tables(position.reshape(own))
    pair_micro = me // (heads * quarters)
    quarter = me % quarters
    key_place = lax.dynamic_index_in_dim(place_of, pair_micro, axis=0, keepdims=False)
    query_place = lax.dynamic_slice_in_dim(
        key_place, quarter * (block // quarters), block // quarters, axis=1
    ).reshape(-1, 1)
    pair_ends = lax.dynamic_index_in_dim(seq_ends, pair_micro, axis=0)
    pair_starts = lax.dynamic_index_in_dim(seq_starts, pair_micro, axis=0)
    query_start = start_of(query_place, pair_ends[None], pair_starts[None])
    key_place = key_place.reshape(1, -1)

    hot = routes[..., None] == jnp.arange(expert_count, dtype=jnp.int32)
    dense = jnp.sum(jnp.where(hot, gates[..., None], 0.0), axis=2)
    own_slot_hot = lax.dynamic_index_in_dim(slot_hot, me, axis=1, keepdims=False)
    share = jnp.einsum(
        "msj,mje->mse", own_slot_hot.astype(f32), dense, precision=lax.Precision.HIGHEST
    )
    share = share.reshape(micro, ranks, dp, expert_count).transpose(1, 2, 0, 3)
    share = share.reshape(own, expert_count)
    scales = jnp.concatenate([query_scale, key_scale])[None]
    own_tokens, cosine, sine, scales, key_place, query_place, query_start = (
        lax.optimization_barrier(
            (own_tokens, cosine, sine, scales, key_place, query_place, query_start)
        )
    )
    normed_b, pre, value_b, squares = project(own_tokens, attn_gain_f, attn_w)
    moe_sent, share, _ = lax.optimization_barrier((moe_sent, share, squares))
    moe_got, share_got = swap(moe_sent), swap(share)
    sent, factors = pack(spread(squares, "tensor"), pre, value_b, cosine, sine, scales)
    moe_local = in_order(first, moe_kept, moe_got).reshape(2 * block, -1)
    share = in_order(first, share, share_got).reshape(2 * own, expert_count)
    share = lax.dynamic_slice_in_dim(share, pair * (expert_count // 2), expert_count // 2, axis=1)
    packed = exchange(sent, DP)
    moe_local = lax.optimization_barrier((moe_local, packed))[0]
    moe_w = lax.all_gather(moe_local, "line", axis=0, tiled=True)
    pair_mixed, log_total = attention(packed, key_place, query_place, query_start)
    mixed_b, attn_out = project_out(exchange(pair_mixed, DP), attn_w)

    def terms_of(value):
        return exchange(value.reshape(te, part, width), "tensor")

    hidden_one, moe_factor, moe_in = before_experts(
        terms_of(attn_out), part_tokens, moe_gain_f
    )

    moe_in = exchange(moe_in, PAIR_TENSOR)
    out_kept, out_sent, moe_grad_part, moe_grads = experts(
        my_te, moe_in, pair_cotangent, share, moe_w, lines
    )
    moe_grads = lax.psum_scatter(moe_grads, "line", scatter_dimension=0, tiled=False)
    moe_grad_terms = exchange(moe_grad_part, PAIR_TENSOR)
    delta_one, delta_attn, grad_moe_gain = after_experts(
        moe_grad_terms, hidden_one, moe_factor, moe_gain_f, part_cotangent
    )
    delta_attn = exchange(delta_attn, "tensor").reshape(own, width)
    def across(value, partner):
        return lax.ppermute(value, "tensor", [(k, partner(k)) for k in range(te)])

    out_sent = lax.optimization_barrier((out_sent, delta_attn))[0]
    out_got = across(out_sent, lambda k: 2 * (3 - k // 2) + k % 2)

    pair_delta = exchange(project_out_back(delta_attn, attn_w), DP)
    pair_grads = attention_back(
        packed, key_place, query_place, query_start, log_total, pair_delta
    )
    pair_grads, out_got, moe_grads = lax.optimization_barrier((pair_grads, out_got, moe_grads))
    out_kept, out_sent = halve(my_te // 2 % 2, out_kept, out_got)
    out_got = across(out_sent, lambda k: k ^ 2)
    got, out_got, moe_grads = lax.optimization_barrier(
        (exchange(pair_grads, DP), out_got, moe_grads)
    )
    out_terms = quarter_terms(my_te % 2, pair, out_kept, out_got)
    out_terms = (
        out_terms[0],
        swap(out_terms[1]),
        across(out_terms[2], lambda k: k ^ 1),
        lax.ppermute(
            out_terms[3], PAIR_TENSOR, [(k, (k + te) % (2 * te) ^ 1) for k in range(2 * te)]
        ),
    )
    weighted, delta_value, inner, gain_grads = unpack(got, pre, factors, cosine, sine, scales)
    inner, moe_grads = lax.optimization_barrier((spread(inner, "tensor"), moe_grads))
    low_lanes, high_lanes = moe_grads[:, :block], moe_grads[:, block:]
    grads_kept = jnp.where(first, low_lanes, high_lanes)
    grads_got = swap(jnp.where(first, high_lanes, low_lanes))
    delta_pre, attn_grad = project_back(inner, weighted, pre, factors, delta_value, attn_w)
    attn_grad, out_terms = lax.optimization_barrier((attn_grad, out_terms))
    attn_grad_terms = terms_of(attn_grad)
    attn_grads = attention_grads(
        normed_b, lax.optimization_barrier((delta_pre, attn_grad))[0], delta_attn, mixed_b
    )
    attn_grads = lax.psum_scatter(attn_grads, "line", scatter_dimension=0, tiled=False)
    low_rows, high_rows = attn_grads[:block], attn_grads[block:]
    attn_grads = jnp.where(first, low_rows, high_rows).astype(f32) + swap(
        jnp.where(first, high_rows, low_rows)
    ).astype(f32)

    home = finish(
        micro,
        attn_grad_terms,
        part_tokens,
        attn_gain_f,
        delta_one,
        hidden_one,
        *out_terms,
        grad_moe_gain,
        gain_grads,
    )
    home, grads_got = lax.optimization_barrier((home, grads_got))
    home, attn_grads = lax.optimization_barrier(
        (exchange(home.reshape(te * dp, micro, -1), ("tensor",) + DP), attn_grads)
    )
    output, input_grad, gain_sum, head_gain_grads = deliver(
        my_te, home, home_hot
    )
    output = output.reshape(micro, block, width)
    input_grad = input_grad.reshape(micro, block, width)

    gate_grad, up_grad, down_grad = expert_gradients(pair, grads_kept, grads_got)
    return (
        output,
        input_grad,
        gain_sum[0],
        attn_grads[:, :local],
        attn_grads[:, local : 2 * local],
        attn_grads[:, 2 * local : 3 * local],
        head_gain_grads[0, :head_cut].reshape(heads, head_part),
        head_gain_grads[0, head_cut : 2 * head_cut].reshape(heads, head_part),
        attn_grads[:, 3 * local :].T,
        gain_sum[1],
        gate_grad,
        up_grad,
        down_grad,
    )


def solution(mesh):
    lines = mesh.shape["dp"] // 2
    devices = mesh.devices.reshape(2, lines, mesh.shape["tensor"])
    placed = (
        P(None, DP, None),
        P(None, DP, None),
        P(),
        P(),
        P(None, DP, None),
        P(None, DP, None),
        P(DP),
        P(DP, "tensor"),
        P(DP, "tensor"),
        P(DP, "tensor"),
        P("tensor", DP),
        P("tensor", DP),
        P("tensor", DP),
        P(DP),
        P(None, DP, "tensor"),
        P(None, DP, "tensor"),
        P(None, "tensor", DP),
    )
    return jax.shard_map(
        body,
        mesh=Mesh(devices, DP + ("tensor",)),
        in_specs=placed,
        out_specs=(
            P(None, DP, None),
            P(None, DP, None),
            P(DP),
            P(DP, "tensor"),
            P(DP, "tensor"),
            P(DP, "tensor"),
            P("tensor", DP),
            P("tensor", DP),
            P("tensor", DP),
            P(DP),
            P(None, DP, "tensor"),
            P(None, DP, "tensor"),
            P(None, "tensor", DP),
        ),
        check_vma=False,
    )
```
